128 devices in a mesh: gx: 8 (over y, core), gy: 16 (over x, z).
Axes of the slice: x: 4, y: 4, z: 4, core: 2. Of those that a mesh axis runs over, the one named last changes fastest.
Arguments:
- velocity: float32 [3, 6, 2048, 4096], P(None, None, 'gx', 'gy'), may hold values from -6 to 6
- threshold: float32 [2048, 4096], P('gx', 'gy'), may hold values from 0.1 to 2
- dust_mass: float32 [7168, 16, 2, 1024], P(('gx', 'gy')), may hold values from 0 to 2
- settle_speed: float32 [16], replicated, may hold values from 0.02 to 1
- bin_share: float32 [16], replicated, may hold values from 0.02 to 0.3
- active_tiles: int32 [7168], replicated, may hold values from 0 to 8191, as said below
- tile_owner: int32 [7168], replicated, may hold values from 0 to 7167, as said below
Outputs:
- new_velocity: float32 [3, 6, 2048, 4096], P(None, None, 'gx', 'gy')
- dust_out: float32 [7168, 16, 2, 1024], P(('gx', 'gy'))
The draws below stay inside these ranges and needn't reach their ends.
Inputs may be any that keep to these rules, and one draw needn't show every extreme that they name: `active_tiles`: distinct tiles; the grid part of device (gx, gy) holds the tiles with tx // 8 == gx and ty // 8 == gy. `tile_owner`: One-to-one onto all 7168 slots, devices counted with gx slowest; one device holds at most 1 tile of any one device's grid part, and in every draw some device holds exactly 1 tile from some grid part.
All inputs are finite; a program needn't handle non-finite values.
Results may differ from the reference program's by a relative error of at most 0.0003.
Values sent between devices are 32-bit elements; how exact they have to be, the bound alone decides.
No kernel may reach another device: no remote copies, remote signals or barrier semaphores. Data moves between devices by JAX's collectives and lax.ppermute only.
A program may use at most 192 MiB of HBM per device.

```python
import math
import jax
import jax.numpy as jnp
from jax import lax

CX = 256
CY = 256
NZ = 6
TZ = 2
TILE = 32
BINS = 16
SLOTS = 56
NX = 2048
NY = 4096
NTX = 64
NTY = 128
OWNERS = 128
ACTIVE = 7168


def placement(key):
    tiles_x = CX // TILE
    tiles_y = CY // TILE
    tile_total = NTX * NTY
    home_cols = NTY // tiles_y
    tile_ids = jnp.arange(tile_total, dtype=jnp.int32)
    tile_x = tile_ids // NTY
    tile_y = tile_ids % NTY
    centre_key, across_key, jitter_key, owner_key, slot_key, order_key = jax.random.split(jax.random.fold_in(key, 101), 6)
    centre_x = jax.random.randint(centre_key, (), 0, NTX)
    centre_y = jax.random.randint(across_key, (), 0, NTY)
    offset_x = jnp.abs(tile_x - centre_x)
    offset_x = jnp.minimum(offset_x, NTX - offset_x)
    offset_y = jnp.abs(tile_y - centre_y)
    offset_y = jnp.minimum(offset_y, NTY - offset_y)
    scaled_x = offset_x * 64 // NTX
    scaled_y = offset_y * 64 // NTY
    jitter = jax.random.randint(jitter_key, (tile_total,), 0, 64)
    scores = (scaled_x * scaled_x + scaled_y * scaled_y + jitter) * tile_total + tile_ids
    chosen = jnp.argsort(scores)[:ACTIVE].astype(jnp.int32)
    home_dev = chosen // NTY // tiles_x * home_cols + chosen % NTY // tiles_y
    local_tile = chosen // NTY % tiles_x * tiles_y + chosen % NTY % tiles_y
    ordered = chosen[jnp.argsort(home_dev * (tiles_x * tiles_y) + local_tile)]
    position = jnp.arange(ACTIVE, dtype=jnp.int32)
    owner_relabel = jax.random.permutation(owner_key, OWNERS)
    slot_relabel = jax.vmap(lambda sub_key: jax.random.permutation(sub_key, SLOTS))(jax.random.split(slot_key, OWNERS))
    raw_owner = position % OWNERS
    raw_rank = position // OWNERS
    owned = owner_relabel[raw_owner] * SLOTS + slot_relabel[raw_owner, raw_rank]
    shuffle = jax.random.permutation(order_key, ACTIVE)
    return (ordered[shuffle].astype(jnp.int32), owned[shuffle].astype(jnp.int32))


def draw_active_tiles(key, part):
    shared = placement(key)
    return shared[0]


def draw_tile_owner(key, part):
    shared = placement(key)
    return shared[1]


def block_scale(stream_key, extent, shards, least, high):
    def one(axis_at, blocks):
        steps = jax.random.uniform(jax.random.fold_in(jax.random.fold_in(stream_key, 6), axis_at), (blocks,), jnp.float32, least / len(shards), high / len(shards))
        return jnp.repeat(jnp.exp(steps), extent[axis_at] // blocks).reshape((-1,) + (1,) * (len(extent) - axis_at - 1))

    level = one(*shards[0])
    for cut in shards[1:]:
        level = level * one(*cut)
    return level


def centred(own_key, shape, scale, reach, pieces=(), held_as=jnp.bfloat16):
    array = jax.random.normal(own_key, shape, jnp.float32) * scale
    if len(pieces) > 0:
        array = block_scale(own_key, shape, pieces, -0.22, 0.18) * array
    return jnp.clip(array, min=-reach, max=reach).astype(held_as)


def setup_inputs(seed: int = 0) -> dict:
    streams_of = jax.random.split(jax.random.key(seed), 8)
    velocity = centred(streams_of[0], (3, NZ, NX, NY), 1.0, 6.0, ((2, 8), (3, 16)), jnp.float32)
    threshold = jnp.clip(jnp.exp(math.log(2.0) - 2.9957323 * jax.random.uniform(streams_of[1], (NX, NY), jnp.float32) ** block_scale(streams_of[1], (NX, NY), ((0, 8), (1, 16)), -0.2, 0.2)), 0.1, 2.0)
    dust_mass = jnp.clip(2.0 * jax.random.uniform(streams_of[2], (ACTIVE, BINS, TZ, TILE * TILE), jnp.float32) ** block_scale(streams_of[2], (ACTIVE, BINS, TZ, TILE * TILE), ((0, 128),), -0.2, 0.2), 0.0, 2.0)
    settle_speed = jnp.clip(jnp.exp(jax.random.uniform(streams_of[3], (BINS,), jnp.float32, math.log(0.02), math.log(1.0))), 0.02, 1.0)
    bin_share = jnp.clip(jnp.exp(jax.random.uniform(streams_of[4], (BINS,), jnp.float32, math.log(0.02), math.log(0.3))), 0.02, 0.3)
    active_tiles = draw_active_tiles(jax.random.fold_in(streams_of[7], 71), 0)
    tile_owner = draw_tile_owner(jax.random.fold_in(streams_of[7], 71), 0)
    return {"velocity": velocity, "threshold": threshold, "dust_mass": dust_mass, "settle_speed": settle_speed, "bin_share": bin_share, "active_tiles": active_tiles, "tile_owner": tile_owner}


time_step = 0.1
viscosity = 0.2
dust_step = 0.1
diffusion = 0.1
roughness = 0.5
emit_rate = 0.5


def advance(padded):
    centre = padded[:, :, 1:-1, 1:-1]
    east_cell = padded[:, :, 2:, 1:-1]
    west_cell = padded[:, :, :-2, 1:-1]
    north_cell = padded[:, :, 1:-1, 2:]
    south_cell = padded[:, :, 1:-1, :-2]
    lower_cell = jnp.concatenate([-centre[:, :1], centre[:, :-1]], axis=1)
    upper_cell = jnp.concatenate([centre[:, 1:], centre[:, -1:]], axis=1)
    carried = 0.5 * (centre[0] * (east_cell - west_cell) + centre[1] * (north_cell - south_cell) + centre[2] * (upper_cell - lower_cell))
    spread = east_cell + west_cell + north_cell + south_cell + upper_cell + lower_cell - 6.0 * centre
    return centre + time_step * (viscosity * spread - carried)


def emission(new_velocity, threshold):
    stress = roughness * (new_velocity[0, 0] * new_velocity[0, 0] + new_velocity[1, 0] * new_velocity[1, 0])
    return emit_rate * stress * jnp.maximum(stress - threshold, 0.0)


def edge_strips(dust):
    tile_count, bin_count, layer_count, cell_count = dust.shape
    block_cube = dust.reshape(tile_count, bin_count, layer_count, TILE, TILE)
    return jnp.stack([block_cube[:, :, :, 0, :], block_cube[:, :, :, -1, :], block_cube[:, :, :, :, 0], block_cube[:, :, :, :, -1]], axis=1)


def upwind(speed, minus, centre, plus):
    return jnp.where(speed > 0, speed * (centre - minus), speed * (plus - centre))


def dust_update(dust, low_x, high_x, low_y, high_y, wind_tiles, uplift_tiles, settle_speed, bin_share):
    tile_count, bin_count, layer_count, cell_count = dust.shape
    block_cube = dust.reshape(tile_count, bin_count, layer_count, TILE, TILE)
    along_x = jnp.concatenate([low_x[:, :, :, None, :], block_cube, high_x[:, :, :, None, :]], axis=3)
    along_y = jnp.concatenate([low_y[:, :, :, :, None], block_cube, high_y[:, :, :, :, None]], axis=4)
    ground_zero = jnp.zeros_like(block_cube[:, :, :1])
    lower_cell = jnp.concatenate([ground_zero, block_cube[:, :, :-1]], axis=2)
    upper_cell = jnp.concatenate([block_cube[:, :, 1:], ground_zero], axis=2)
    west_cell = along_x[:, :, :, :-2]
    east_cell = along_x[:, :, :, 2:]
    south_cell = along_y[:, :, :, :, :-2]
    north_cell = along_y[:, :, :, :, 2:]
    shaped = wind_tiles.reshape(tile_count, 3, 1, layer_count, TILE, TILE)
    speed_east = shaped[:, 0]
    speed_north = shaped[:, 1]
    speed_up = shaped[:, 2] - settle_speed[None, :, None, None, None]
    carried = upwind(speed_east, west_cell, block_cube, east_cell) + upwind(speed_north, south_cell, block_cube, north_cell) + upwind(speed_up, lower_cell, block_cube, upper_cell)
    spread = west_cell + east_cell + south_cell + north_cell + lower_cell + upper_cell - 6.0 * block_cube
    source = uplift_tiles.reshape(tile_count, 1, TILE, TILE) * bin_share[None, :, None, None]
    lifted = jnp.concatenate([source[:, :, None], jnp.zeros_like(block_cube[:, :, 1:])], axis=2)
    return (block_cube + dust_step * (diffusion * spread - carried + lifted)).reshape(dust.shape)


def reference(velocity, threshold, dust_mass, settle_speed, bin_share, active_tiles, tile_owner):
    padded = jnp.pad(velocity, ((0, 0), (0, 0), (1, 1), (1, 1)), mode="wrap")
    new_velocity = advance(padded)
    uplift = emission(new_velocity, threshold)
    tiles_x = NX // TILE
    tiles_y = NY // TILE
    slot_total = OWNERS * SLOTS
    slot_of_tile = jnp.full((tiles_x * tiles_y,), -1, jnp.int32).at[active_tiles].set(tile_owner)
    tile_of_slot = jnp.zeros((slot_total,), jnp.int32).at[tile_owner].set(active_tiles)
    tile_x = tile_of_slot // tiles_y
    tile_y = tile_of_slot % tiles_y

    def neighbour(shift_x, shift_y):
        return slot_of_tile[((tile_x + shift_x) % tiles_x) * tiles_y + (tile_y + shift_y) % tiles_y]

    neighbour_slots = [neighbour(-1, 0), neighbour(1, 0), neighbour(0, -1), neighbour(0, 1)]
    facing = [1, 0, 3, 2]
    wind_all = new_velocity[:, :TZ].reshape(3, TZ, tiles_x, TILE, tiles_y, TILE).transpose(2, 4, 0, 1, 3, 5).reshape(tiles_x * tiles_y, 3, TZ, TILE * TILE)
    uplift_all = uplift.reshape(tiles_x, TILE, tiles_y, TILE).transpose(0, 2, 1, 3).reshape(tiles_x * tiles_y, TILE * TILE)
    wind_tiles = wind_all[tile_of_slot]
    uplift_tiles = uplift_all[tile_of_slot]
    dust = dust_mass
    for substep in range(2):
        edge_rows = edge_strips(dust)
        ghosts = []
        for slots_near, side in zip(neighbour_slots, facing):
            taken = edge_rows[jnp.maximum(slots_near, 0), side]
            ghosts.append(jnp.where((slots_near >= 0)[:, None, None, None], taken, 0.0))
        stacked = jnp.stack(ghosts, axis=1)

        def one_block(block_args):
            dust_block, rim_block, wind_block, uplift_block = block_args
            return dust_update(dust_block, rim_block[:, 0], rim_block[:, 1], rim_block[:, 2], rim_block[:, 3], wind_block, uplift_block, settle_speed, bin_share)

        dust = lax.map(one_block, (dust.reshape((OWNERS, SLOTS) + dust.shape[1:]), stacked.reshape((OWNERS, SLOTS) + stacked.shape[1:]), wind_tiles.reshape((OWNERS, SLOTS) + wind_tiles.shape[1:]), uplift_tiles.reshape((OWNERS, SLOTS) + uplift_tiles.shape[1:]))).reshape(dust_mass.shape)
    return new_velocity, dust
```

```python
import functools

import jax
import jax.numpy as jnp
from jax import lax
from jax.experimental import pallas as pl
from jax.experimental.pallas import tpu as pltpu
from jax.sharding import PartitionSpec as P

TZ = 2
TILE = 32
LANES = 128
ROWS = TILE * TILE // LANES
PLANES = 7
AXES = ("gx", "gy")

time_step = 0.1
viscosity = 0.2
dust_step = 0.1
diffusion = 0.1
roughness = 0.5
emit_rate = 0.5

WEST, SOUTH, NORTH, EAST = range(4)


def iotas(shape=(ROWS, LANES)):
    return lax.broadcasted_iota(jnp.int32, shape, 0), lax.broadcasted_iota(jnp.int32, shape, 1)


def lane_gather(x, index):
    return jnp.take_along_axis(x, index, axis=1)


def ring_pattern(depth):
    row, lane = iotas()
    group, within = lane // TILE, lane % TILE
    side = jnp.where(group == SOUTH, depth, TILE - 1 - depth)
    index = (within % 4) * TILE + side
    index = jnp.where(group == WEST, depth * TILE + within, index)
    index = jnp.where(group == EAST, (3 - depth) * TILE + within, index)
    source = jnp.where(group == WEST, 0, jnp.where(group == EAST, ROWS - 1, within // 4))
    return index, row == source


def ring_of(x, pattern):
    index, taken = pattern
    return jnp.sum(jnp.where(taken, lane_gather(x, index), 0.0), axis=0, keepdims=True)


def spread_rows(row):
    return jnp.broadcast_to(row, (ROWS, LANES))


def strips_kernel(home_ref, dust_ref, send_ref, rings, sems, *, block, bins):
    step = pl.program_id(0)
    slots = rings.shape[0]
    patterns = [ring_pattern(0), ring_pattern(1)]

    def one(j, carry):
        s = step * block + j
        for b in range(bins):
            for level in range(TZ):
                x = dust_ref[j, b, pl.ds(level, ROWS, stride=TZ), :]
                for depth in range(2):
                    at = depth * bins * TZ + b * TZ + level
                    rings[s, at : at + 1, :] = ring_of(x, patterns[depth])
        pltpu.make_async_copy(rings.at[s], send_ref.at[home_ref[s]], sems.at[s]).start()
        return carry

    lax.fori_loop(0, block, one, 0)

    @pl.when(step == pl.num_programs(0) - 1)
    def _():
        def wait(s, carry):
            pltpu.make_async_copy(rings.at[s], send_ref.at[home_ref[s]], sems.at[s]).wait()
            return carry

        lax.fori_loop(0, slots, wait, 0)


def dust_strips(home_of_slot, dust, owners):
    slots, bins = dust.shape[:2]
    block = 8 if slots % 8 == 0 else 4
    rows = 2 * bins * TZ
    return pl.pallas_call(
        functools.partial(strips_kernel, block=block, bins=bins),
        grid=(slots // block,),
        in_specs=[
            pl.BlockSpec(memory_space=pltpu.SMEM),
            pl.BlockSpec((block,) + dust.shape[1:], lambda i: (i, 0, 0, 0)),
        ],
        out_specs=pl.BlockSpec(memory_space=pl.ANY),
        out_shape=jax.ShapeDtypeStruct((owners, rows, LANES), jnp.float32),
        scratch_shapes=[
            pltpu.VMEM((slots, rows, LANES), jnp.float32),
            pltpu.SemaphoreType.DMA((slots,)),
        ],
        compiler_params=pltpu.CompilerParams(vmem_limit_bytes=32 << 20),
        cost_estimate=pl.CostEstimate(
            flops=20 * dust.size, bytes_accessed=dust.size * 4 + slots * rows * LANES * 4, transcendentals=0
        ),
        name="dust_strips",
    )(home_of_slot, dust)


def wind_kernel(
    owner_ref, vel_ref, xlo_ref, xhi_ref, ylo_ref, yhi_ref, thr_ref,
    new_ref, send_ref, ring_ref, padded, strip, tiles, load_sem, sems, *, levels
):
    fields, nx, ny = new_ref.shape
    load = pltpu.make_async_copy(vel_ref, padded.at[:, pl.ds(8, nx), :], load_sem)
    load.start()
    load.wait()
    padded[:, 7:8, :] = xlo_ref[...]
    padded[:, 8 + nx : 9 + nx, :] = xhi_ref[...]
    half = 16
    halves = ny // LANES
    tiles_y = ny // TILE
    pattern = ring_pattern(0)
    _, lane8 = iotas()
    group = lane8 // TILE

    def one_strip(ix, carry):
        for sub in range(TILE // half):
            base = pl.multiple_of(ix * TILE + sub * half, 8)
            lane = lax.broadcasted_iota(jnp.int32, (half, ny), 1)
            low = {}
            for z in range(levels):
                u, v, w = (padded[c * levels + z, pl.ds(base + 8, half), :] for c in range(3))
                for c in range(3):
                    f = c * levels + z
                    block = padded[f, pl.ds(base, half + 16), :]
                    centre = (u, v, w)[c]
                    west = pltpu.roll(block, 1, 0)[8 : 8 + half]
                    east = pltpu.roll(block, half + 15, 0)[8 : 8 + half]
                    south = jnp.where(lane == 0, ylo_ref[f, pl.ds(base, half), :], pltpu.roll(centre, 1, 1))
                    north = jnp.where(
                        lane == ny - 1, yhi_ref[f, pl.ds(base, half), :], pltpu.roll(centre, ny - 1, 1)
                    )
                    lower = -centre if z == 0 else padded[f - 1, pl.ds(base + 8, half), :]
                    upper = centre if z == levels - 1 else padded[f + 1, pl.ds(base + 8, half), :]
                    carried = 0.5 * (u * (east - west) + v * (north - south) + w * (upper - lower))
                    spread = east + west + north + south + upper + lower - 6.0 * centre
                    new = centre + time_step * (viscosity * spread - carried)
                    new_ref[f, pl.ds(base, half), :] = new
                    if z < TZ:
                        low[c * TZ + z] = new
            stress = roughness * (low[0] * low[0] + low[TZ] * low[TZ])
            low[PLANES - 1] = emit_rate * stress * jnp.maximum(
                stress - thr_ref[pl.ds(base, half), :], 0.0
            )
            for p in range(PLANES):
                for h in range(halves):
                    strip[p * halves + h, sub * half : (sub + 1) * half, :] = low[p][
                        :, h * LANES : (h + 1) * LANES
                    ]
        for p in range(PLANES):
            for h in range(halves):
                parts = [strip[p * halves + h, pl.ds(k, ROWS, stride=4), :] for k in range(4)]
                for t in range(4):
                    tile = ix * tiles_y + h * 4 + t
                    cells = pltpu.roll(parts[0], (-t * TILE) % LANES, 1) if t else parts[0]
                    for k in range(1, 4):
                        moved = pltpu.roll(parts[k], ((k - t) * TILE) % LANES, 1) if k != t else parts[k]
                        cells = jnp.where(group == k, moved, cells)
                    tiles[tile, p * ROWS : (p + 1) * ROWS, :] = cells
                    ring_ref[tile, p : p + 1, :] = ring_of(cells, pattern)

        def send(t, inner):
            tile = ix * tiles_y + t
            owner = owner_ref[tile]

            @pl.when(owner >= 0)
            def _():
                pltpu.make_async_copy(tiles.at[tile], send_ref.at[owner], sems.at[tile]).start()

            return inner

        lax.fori_loop(0, tiles_y, send, 0)
        return carry

    lax.fori_loop(0, nx // TILE, one_strip, 0)

    def wait(tile, carry):
        owner = owner_ref[tile]

        @pl.when(owner >= 0)
        def _():
            pltpu.make_async_copy(tiles.at[tile], send_ref.at[owner], sems.at[tile]).wait()

        return carry

    lax.fori_loop(0, tiles.shape[0], wait, 0)


def wind_step(owner_of_tile, velocity, xlo, xhi, ylo, yhi, threshold, owners):
    comps, levels, nx, ny = velocity.shape
    fields = comps * levels
    per_home = (nx // TILE) * (ny // TILE)
    smem = pl.BlockSpec(memory_space=pltpu.SMEM)
    hbm = pl.BlockSpec(memory_space=pl.ANY)
    vmem = pl.BlockSpec(memory_space=pltpu.VMEM)
    new, send, ring = pl.pallas_call(
        functools.partial(wind_kernel, levels=levels),
        in_specs=[smem, hbm, vmem, vmem, vmem, vmem, vmem],
        out_specs=[vmem, hbm, vmem],
        out_shape=[
            jax.ShapeDtypeStruct((fields, nx, ny), jnp.float32),
            jax.ShapeDtypeStruct((owners, PLANES * ROWS, LANES), jnp.float32),
            jax.ShapeDtypeStruct((per_home, 8, LANES), jnp.float32),
        ],
        scratch_shapes=[
            pltpu.VMEM((fields, nx + 16, ny), jnp.float32),
            pltpu.VMEM((PLANES * (ny // LANES), TILE, LANES), jnp.float32),
            pltpu.VMEM((per_home, PLANES * ROWS, LANES), jnp.float32),
            pltpu.SemaphoreType.DMA,
            pltpu.SemaphoreType.DMA((per_home,)),
        ],
        compiler_params=pltpu.CompilerParams(vmem_limit_bytes=40 << 20),
        cost_estimate=pl.CostEstimate(
            flops=40 * velocity.size, bytes_accessed=velocity.size * 10, transcendentals=0
        ),
        name="wind_step",
    )(
        owner_of_tile,
        velocity.reshape(fields, nx, ny),
        xlo.reshape(fields, 1, ny),
        xhi.reshape(fields, 1, ny),
        ylo.reshape(fields, nx, 1),
        yhi.reshape(fields, nx, 1),
        threshold,
    )
    return new.reshape(velocity.shape), send, ring


def pack_borders(outs, ring_at, tiles_x, tiles_y):
    rows = outs[0].shape[1]
    lane = lax.broadcasted_iota(jnp.int32, (rows, LANES), 1)
    borders = (
        (EAST, [((tiles_x - 1) * tiles_y + n) for n in range(tiles_y)]),
        (WEST, [n for n in range(tiles_y)]),
        (NORTH, [n * tiles_y + tiles_y - 1 for n in range(tiles_x)]),
        (SOUTH, [n * tiles_y for n in range(tiles_x)]),
    )
    for out, (side, tiles) in zip(outs, borders):
        for g in range(len(tiles) // 4):
            packed = None
            for q in range(4):
                strip = ring_at(tiles[4 * g + q])
                if q != side:
                    strip = pltpu.roll(strip, ((q - side) * TILE) % LANES, 1)
                packed = strip if packed is None else jnp.where(lane // TILE == q, strip, packed)
            out[g] = packed


def fill_halo(ext, borders, tiles_x, tiles_y):
    from_west, from_east, from_south, from_north = borders
    wide = tiles_y + 2
    for ref, side, places in (
        (from_west, EAST, [n + 1 for n in range(tiles_y)]),
        (from_east, WEST, [(tiles_x + 1) * wide + n + 1 for n in range(tiles_y)]),
        (from_south, NORTH, [(n + 1) * wide for n in range(tiles_x)]),
        (from_north, SOUTH, [(n + 1) * wide + tiles_y + 1 for n in range(tiles_x)]),
    ):
        for n, place in enumerate(places):
            strip = ref[n // 4]
            if n % 4 != side:
                strip = pltpu.roll(strip, ((side - n % 4) * TILE) % LANES, 1)
            ext[place] = strip


def seen_by(ext, place, wide):
    west, east = ext[place - wide], ext[place + wide]
    south, north = ext[place - 1], ext[place + 1]
    lane = lax.broadcasted_iota(jnp.int32, west.shape, 1)
    up = pltpu.roll(jnp.where(lane < 2 * TILE, north, west), TILE, 1)
    down = pltpu.roll(jnp.where(lane < 2 * TILE, east, south), LANES - TILE, 1)
    return jnp.where((lane // TILE) % 2 == 0, up, down)


def gather_rings_kernel(owner_ref, recv_ref, rings_ref, e_ref, w_ref, n_ref, s_ref, sems, *, tiles_x, tiles_y):
    per_home = tiles_x * tiles_y
    rows = e_ref.shape[1]

    def start(t, carry):
        owner = owner_ref[t]

        @pl.when(owner >= 0)
        def _():
            pltpu.make_async_copy(recv_ref.at[owner], rings_ref.at[t], sems.at[t]).start()

        @pl.when(owner < 0)
        def _():
            rings_ref[t] = jnp.zeros(rings_ref.shape[1:], jnp.float32)

        return carry

    lax.fori_loop(0, per_home, start, 0)

    def wait(t, carry):
        owner = owner_ref[t]

        @pl.when(owner >= 0)
        def _():
            pltpu.make_async_copy(recv_ref.at[owner], rings_ref.at[t], sems.at[t]).wait()

        return carry

    lax.fori_loop(0, per_home, wait, 0)
    pack_borders((e_ref, w_ref, n_ref, s_ref), lambda t: rings_ref[t, :rows, :], tiles_x, tiles_y)


def advance_rings_kernel(
    owner_ref, rings_ref, fw_ref, fe_ref, fs_ref, fn_ref, wind_ref, settle_ref, share_ref,
    seen_ref, later_ref, e_ref, w_ref, n_ref, s_ref, ext, *, tiles_x, tiles_y
):
    per_home = tiles_x * tiles_y
    rows = e_ref.shape[1]
    wide = tiles_y + 2
    fill_halo(ext, (fw_ref, fe_ref, fs_ref, fn_ref), tiles_x, tiles_y)

    def place_of(t):
        return (t // tiles_y + 1) * wide + t % tiles_y + 1

    def inner(t, carry):
        ext[place_of(t)] = rings_ref[t, :rows, :]
        return carry

    lax.fori_loop(0, per_home, inner, 0)

    row, lane = iotas()
    group, within = lane // TILE, lane % TILE
    even = row % 2 == 0
    on_x = (group == WEST) | (group == EAST)
    first, last = within == 0, within == TILE - 1
    high = jnp.where((group == EAST) | (group == NORTH), TILE - 1, 0)
    corner = jnp.where(
        on_x,
        jnp.where(first, SOUTH, NORTH) * TILE + high,
        jnp.where(first, WEST, EAST) * TILE + high,
    )

    def one(t, carry):
        place = place_of(t)
        seen = seen_by(ext, place, wide)
        seen_ref[t] = seen

        def level_rows(p):
            return jnp.where(even, spread_rows(wind_ref[t, p : p + 1, :]), spread_rows(wind_ref[t, p + 1 : p + 2, :]))

        u, v, w = (dust_step * level_rows(c * TZ) for c in range(3))
        uplift = dust_step * spread_rows(wind_ref[t, PLANES - 1 : PLANES, :])
        mix = dust_step * diffusion
        from_west = mix + jnp.maximum(u, 0.0)
        from_east = mix + jnp.maximum(-u, 0.0)
        from_south = mix + jnp.maximum(v, 0.0)
        from_north = mix + jnp.maximum(-v, 0.0)
        keep = 1.0 - 6.0 * mix - jnp.abs(u) - jnp.abs(v)
        active = owner_ref[t] >= 0
        for chunk in range(rows // ROWS):
            at = chunk * ROWS
            q = rings_ref[t, at : at + ROWS, :]
            deep = rings_ref[t, rows + at : rows + at + ROWS, :]
            out = seen[at : at + ROWS, :]
            beyond = lane_gather(out, corner)
            before = jnp.where(first, beyond, pltpu.roll(q, 1, 1))
            after = jnp.where(last, beyond, pltpu.roll(q, LANES - 1, 1))
            west = jnp.where(group == WEST, out, jnp.where(group == EAST, deep, before))
            east = jnp.where(group == WEST, deep, jnp.where(group == EAST, out, after))
            south = jnp.where(on_x, before, jnp.where(group == SOUTH, out, deep))
            north = jnp.where(on_x, after, jnp.where(group == SOUTH, deep, out))
            other = jnp.where(even, pltpu.roll(q, ROWS - 1, 0), pltpu.roll(q, 1, 0))
            rise = w - dust_step * settle_ref[at : at + ROWS, :]
            up = jnp.maximum(rise, 0.0)
            down = up - rise
            new = (
                (keep - up - down) * q
                + from_west * west
                + from_east * east
                + from_south * south
                + from_north * north
                + (mix + jnp.where(even, down, up)) * other
                + uplift * share_ref[at : at + ROWS, :]
            )
            later_ref[t, at : at + ROWS, :] = jnp.where(active, new, 0.0)
        return carry

    lax.fori_loop(0, per_home, one, 0)
    pack_borders((e_ref, w_ref, n_ref, s_ref), lambda t: later_ref[t], tiles_x, tiles_y)


def send_seen_kernel(
    owner_ref, later_ref, fw_ref, fe_ref, fs_ref, fn_ref, seen_ref, send_ref, ext, both, sems, *, tiles_x, tiles_y
):
    per_home = tiles_x * tiles_y
    rows = later_ref.shape[1]
    wide = tiles_y + 2
    fill_halo(ext, (fw_ref, fe_ref, fs_ref, fn_ref), tiles_x, tiles_y)

    def place_of(t):
        return (t // tiles_y + 1) * wide + t % tiles_y + 1

    def inner(t, carry):
        ext[place_of(t)] = later_ref[t]
        return carry

    lax.fori_loop(0, per_home, inner, 0)

    def one(t, carry):
        both[t, :rows, :] = seen_ref[t]
        both[t, rows:, :] = seen_by(ext, place_of(t), wide)
        owner = owner_ref[t]

        @pl.when(owner >= 0)
        def _():
            pltpu.make_async_copy(both.at[t], send_ref.at[owner], sems.at[t]).start()

        return carry

    lax.fori_loop(0, per_home, one, 0)

    def wait(t, carry):
        owner = owner_ref[t]

        @pl.when(owner >= 0)
        def _():
            pltpu.make_async_copy(both.at[t], send_ref.at[owner], sems.at[t]).wait()

        return carry

    lax.fori_loop(0, per_home, wait, 0)


def shifted(value, axis, steps):
    count = lax.axis_size(axis)
    return lax.ppermute(value, axis, [(source, (source + steps) % count) for source in range(count)])


def exchange_borders(borders):
    east, west, north, south = borders
    return shifted(east, "gx", 1), shifted(west, "gx", -1), shifted(north, "gy", 1), shifted(south, "gy", -1)


def relay_strips(owner_of_tile, received, wind_ring, settle_speed, bin_share, tiles_x, tiles_y):
    owners, both_rows, _ = received.shape
    rows = both_rows // 2
    per_home = tiles_x * tiles_y
    smem = pl.BlockSpec(memory_space=pltpu.SMEM)
    hbm = pl.BlockSpec(memory_space=pl.ANY)
    vmem = pl.BlockSpec(memory_space=pltpu.VMEM)
    f32 = lambda *shape: jax.ShapeDtypeStruct(shape, jnp.float32)
    packs = [f32(tiles_y // 4, rows, LANES)] * 2 + [f32(tiles_x // 4, rows, LANES)] * 2
    sizes = dict(tiles_x=tiles_x, tiles_y=tiles_y)
    params = pltpu.CompilerParams(vmem_limit_bytes=32 << 20)
    ext = pltpu.VMEM(((tiles_x + 2) * (tiles_y + 2), rows, LANES), jnp.float32)
    sems = pltpu.SemaphoreType.DMA((per_home,))
    cost = pl.CostEstimate(flops=1 << 22, bytes_accessed=per_home * both_rows * LANES * 12, transcendentals=0)
    rings, *borders = pl.pallas_call(
        functools.partial(gather_rings_kernel, **sizes),
        in_specs=[smem, hbm],
        out_specs=[vmem] * 5,
        out_shape=[f32(per_home, both_rows, LANES)] + packs,
        scratch_shapes=[sems],
        compiler_params=params,
        cost_estimate=cost,
        name="gather_rings",
    )(owner_of_tile, received)
    settle_rows = jnp.broadcast_to(jnp.repeat(settle_speed, TZ)[:, None], (rows, LANES))
    share_rows = jnp.broadcast_to(
        jnp.stack([bin_share, jnp.zeros_like(bin_share)], axis=1).reshape(-1, 1), (rows, LANES)
    )
    seen, later, *borders = pl.pallas_call(
        functools.partial(advance_rings_kernel, **sizes),
        in_specs=[smem] + [vmem] * 8,
        out_specs=[vmem] * 6,
        out_shape=[f32(per_home, rows, LANES)] * 2 + packs,
        scratch_shapes=[ext],
        compiler_params=params,
        cost_estimate=cost,
        name="advance_rings",
    )(owner_of_tile, rings, *exchange_borders(borders), wind_ring, settle_rows, share_rows)
    return pl.pallas_call(
        functools.partial(send_seen_kernel, **sizes),
        in_specs=[smem] + [vmem] * 6,
        out_specs=hbm,
        out_shape=f32(owners, both_rows, LANES),
        scratch_shapes=[ext, pltpu.VMEM((per_home, both_rows, LANES), jnp.float32), sems],
        compiler_params=params,
        cost_estimate=cost,
        name="send_seen",
    )(owner_of_tile, later, *exchange_borders(borders), seen)


def dust_kernel(
    home_ref, settle_ref, share_ref, dust_ref, wind_hbm, seen_hbm, out_ref, wind, seen, wind_sems, seen_sems,
    *, block, bins
):
    step = pl.program_id(0)
    slots = wind.shape[0]

    def wind_copy(s):
        return pltpu.make_async_copy(wind_hbm.at[home_ref[s]], wind.at[s], wind_sems.at[s])

    def seen_copy(s):
        return pltpu.make_async_copy(seen_hbm.at[home_ref[s]], seen.at[s], seen_sems.at[s])

    @pl.when(step == 0)
    def _():
        def start(s, carry):
            wind_copy(s).start()
            seen_copy(s).start()
            return carry

        lax.fori_loop(0, slots, start, 0)

    row, lane = iotas()
    within = lane % TILE
    first_y, last_y = within == 0, within == TILE - 1
    first_x = (row == 0) & (lane < TILE)
    last_x = (row == ROWS - 1) & (lane >= LANES - TILE)
    low_lanes, high_lanes = lane < TILE, lane >= LANES - TILE
    along = 4 * row + lane // TILE
    from_sides = jnp.where(first_y, SOUTH * TILE, NORTH * TILE) + along
    mix = dust_step * diffusion
    rows = bins * TZ

    def one(j, carry):
        s = step * block + j
        wind_copy(s).wait()
        seen_copy(s).wait()
        plane = [wind[s, p * ROWS : (p + 1) * ROWS, :] * dust_step for p in range(PLANES)]
        west_by, east_by, south_by, north_by, keep = [], [], [], [], []
        for level in range(TZ):
            u, v = plane[level], plane[TZ + level]
            west_by.append(mix + jnp.maximum(u, 0.0))
            east_by.append(mix + jnp.maximum(-u, 0.0))
            south_by.append(mix + jnp.maximum(v, 0.0))
            north_by.append(mix + jnp.maximum(-v, 0.0))
            keep.append(1.0 - 6.0 * mix - jnp.abs(u) - jnp.abs(v))
        for b in range(bins):
            q = [dust_ref[j, b, pl.ds(level, ROWS, stride=TZ), :] for level in range(TZ)]
            settle = settle_ref[b] * dust_step
            stay, mixed = [], []
            for level in range(TZ):
                rise = plane[2 * TZ + level] - settle
                up = jnp.maximum(rise, 0.0)
                down = up - rise
                stay.append(keep[level] - up - down)
                mixed.append(mix + (down if level == 0 else up))
            source = plane[PLANES - 1] * share_ref[b]
            for substep in range(2):
                new = []
                for level in range(TZ):
                    c = q[level]
                    at = substep * rows + b * TZ + level
                    edge = spread_rows(seen[s, at : at + 1, :])
                    side = lane_gather(edge, from_sides)
                    right = pltpu.roll(c, TILE, 1)
                    left = pltpu.roll(c, LANES - TILE, 1)
                    west = jnp.where(low_lanes, pltpu.roll(right, 1, 0), right)
                    west = jnp.where(first_x, edge, west)
                    east = jnp.where(high_lanes, pltpu.roll(left, ROWS - 1, 0), left)
                    east = jnp.where(last_x, edge, east)
                    south = jnp.where(first_y, side, pltpu.roll(c, 1, 1))
                    north = jnp.where(last_y, side, pltpu.roll(c, LANES - 1, 1))
                    value = (
                        stay[level] * c
                        + west_by[level] * west
                        + east_by[level] * east
                        + south_by[level] * south
                        + north_by[level] * north
                        + mixed[level] * q[1 - level]
                    )
                    if level == 0:
                        value = value + source
                    new.append(value)
                q = new
            for level in range(TZ):
                out_ref[j, b, pl.ds(level, ROWS, stride=TZ), :] = q[level]
        return carry

    lax.fori_loop(0, block, one, 0)


def dust_steps(home_of_slot, dust, wind_recv, seen_recv, settle_speed, bin_share):
    slots, bins = dust.shape[:2]
    block = 8 if slots % 8 == 0 else 4
    smem = pl.BlockSpec(memory_space=pltpu.SMEM)
    hbm = pl.BlockSpec(memory_space=pl.ANY)
    tile = pl.BlockSpec((block,) + dust.shape[1:], lambda i: (i, 0, 0, 0))
    return pl.pallas_call(
        functools.partial(dust_kernel, block=block, bins=bins),
        grid=(slots // block,),
        in_specs=[smem, smem, smem, tile, hbm, hbm],
        out_specs=tile,
        out_shape=jax.ShapeDtypeStruct(dust.shape, jnp.float32),
        scratch_shapes=[
            pltpu.VMEM((slots,) + wind_recv.shape[1:], jnp.float32),
            pltpu.VMEM((slots,) + seen_recv.shape[1:], jnp.float32),
            pltpu.SemaphoreType.DMA((slots,)),
            pltpu.SemaphoreType.DMA((slots,)),
        ],
        compiler_params=pltpu.CompilerParams(vmem_limit_bytes=32 << 20),
        cost_estimate=pl.CostEstimate(flops=60 * dust.size, bytes_accessed=dust.size * 12, transcendentals=0),
        name="dust_steps",
    )(home_of_slot, settle_speed, bin_share, dust, wind_recv, seen_recv)


def relay_rows(rows):
    return lax.all_to_all(rows, AXES, split_axis=0, concat_axis=0, tiled=True)


def per_device(velocity, threshold, dust_mass, settle_speed, bin_share, active_tiles, tile_owner):
    owners = lax.axis_size(AXES)
    grid_cols = lax.axis_size("gy")
    self_index = lax.axis_index(AXES)
    slots, bins = dust_mass.shape[:2]
    tiles_x = velocity.shape[2] // TILE
    tiles_y = velocity.shape[3] // TILE
    per_home = tiles_x * tiles_y
    tiles_across = tiles_y * grid_cols

    tile_x = active_tiles // tiles_across
    tile_y = active_tiles % tiles_across
    home_dev = tile_x // tiles_x * grid_cols + tile_y // tiles_y
    local_tile = tile_x % tiles_x * tiles_y + tile_y % tiles_y
    own_slot = tile_owner - self_index * slots
    mine = jnp.where(home_dev == self_index, local_tile, -1)
    slot_ids = jnp.arange(slots, dtype=jnp.int32)
    home_of_slot = jnp.sum(jnp.where(own_slot[None, :] == slot_ids[:, None], home_dev[None, :], 0), axis=1)
    tile_ids = jnp.arange(per_home, dtype=jnp.int32)
    owner_of_tile = jnp.max(
        jnp.where(mine[None, :] == tile_ids[:, None], (tile_owner // slots)[None, :], -1), axis=1
    )

    dust = dust_mass.reshape(slots, bins, TZ, ROWS, LANES).transpose(0, 1, 3, 2, 4)
    dust = dust.reshape(slots, bins, ROWS * TZ, LANES)

    xlo = shifted(velocity[:, :, -1, :], "gx", 1)
    xhi = shifted(velocity[:, :, 0, :], "gx", -1)
    ylo = shifted(velocity[:, :, :, -1], "gy", 1)
    yhi = shifted(velocity[:, :, :, 0], "gy", -1)

    strips = relay_rows(dust_strips(home_of_slot, dust, owners))
    new_velocity, wind_send, wind_ring = wind_step(
        owner_of_tile, velocity, xlo, xhi, ylo, yhi, threshold, owners
    )
    wind_recv = relay_rows(wind_send)
    seen_send = relay_strips(owner_of_tile, strips, wind_ring, settle_speed, bin_share, tiles_x, tiles_y)
    seen_recv = relay_rows(seen_send)
    out = dust_steps(home_of_slot, dust, wind_recv, seen_recv, settle_speed, bin_share)
    out = out.reshape(slots, bins, ROWS, TZ, LANES).transpose(0, 1, 3, 2, 4).reshape(dust_mass.shape)
    return new_velocity, out


def solution(mesh):
    in_specs = (
        P(None, None, "gx", "gy"),
        P("gx", "gy"),
        P(AXES, None, None, None),
        P(),
        P(),
        P(),
        P(),
    )
    out_specs = (P(None, None, "gx", "gy"), P(AXES, None, None, None))
    return jax.shard_map(
        per_device, mesh=mesh, in_specs=in_specs, out_specs=out_specs, check_vma=False
    )
```

```python
import functools

import jax
import jax.numpy as jnp
import ml_dtypes
import numpy as np
from jax import lax
from jax.experimental import pallas as pl
from jax.experimental.pallas import tpu as pltpu
from jax.sharding import PartitionSpec as P

TZ = 2
TILE = 32
LANES = 128
ROWS = TILE * TILE // LANES
PLANES = 7
AXES = ("gx", "gy")

time_step = 0.1
viscosity = 0.2
dust_step = 0.1
diffusion = 0.1
roughness = 0.5
emit_rate = 0.5

WEST, SOUTH, NORTH, EAST = range(4)


def iotas(shape=(ROWS, LANES)):
    return lax.broadcasted_iota(jnp.int32, shape, 0), lax.broadcasted_iota(jnp.int32, shape, 1)


def lane_gather(x, index):
    return jnp.take_along_axis(x, index, axis=1)


def ring_pattern(depth):
    row, lane = iotas()
    group, within = lane // TILE, lane % TILE
    side = jnp.where(group == SOUTH, depth, TILE - 1 - depth)
    index = (within % 4) * TILE + side
    index = jnp.where(group == WEST, depth * TILE + within, index)
    index = jnp.where(group == EAST, (3 - depth) * TILE + within, index)
    source = jnp.where(group == WEST, 0, jnp.where(group == EAST, ROWS - 1, within // 4))
    return index, row == source


def ring_of(x, pattern):
    index, taken = pattern
    return jnp.sum(jnp.where(taken, lane_gather(x, index), 0.0), axis=0, keepdims=True)


def spread_rows(row):
    return jnp.broadcast_to(row, (ROWS, LANES))


def halves_of(x):
    high = x.astype(jnp.bfloat16)
    return high, (x - high.astype(jnp.float32)).astype(jnp.bfloat16)


def moves(sources):
    lanes = np.arange(LANES)[:, None]
    once = (lanes == np.asarray(sources)[None, :]).astype(ml_dtypes.bfloat16)
    return np.concatenate([once, once], axis=0)


def ring_matrix():
    lane = np.arange(LANES)
    group, within = lane // TILE, lane % TILE
    blocks = []
    for r in range(ROWS):
        columns = []
        for depth in range(2):
            side = np.where(group == SOUTH, depth, TILE - 1 - depth)
            source = np.where(within // 4 == r, (within % 4) * TILE + side, -1)
            source = np.where(group == WEST, depth * TILE + within if r == 0 else -1, source)
            source = np.where(group == EAST, (3 - depth) * TILE + within if r == ROWS - 1 else -1, source)
            columns.append(source)
        blocks.append(moves(np.concatenate(columns)))
    return np.concatenate(blocks, axis=0)


def shift_matrix():
    lane = np.arange(LANES)
    return moves(np.concatenate([(lane + d) % LANES for d in (-1, 1, -TILE, TILE)]))


def side_matrix():
    lane = np.arange(LANES)
    columns = []
    for r in range(ROWS):
        along = 4 * r + lane // TILE
        source = np.where(lane % TILE == 0, SOUTH * TILE + along, -1)
        columns.append(np.where(lane % TILE == TILE - 1, NORTH * TILE + along, source))
    return moves(np.concatenate(columns))


def strips_kernel(home_ref, dust_ref, matrix_ref, send_ref, rings, sems, *, block, bins):
    step = pl.program_id(0)
    slots = rings.shape[0]
    each = TZ * bins

    parts = []
    for r in range(ROWS):
        x = jnp.concatenate(
            [
                dust_ref[j, pl.ds(r * TZ + level, bins, stride=ROWS * TZ), :]
                for j in range(block)
                for level in range(TZ)
            ],
            axis=0,
        )
        parts += halves_of(x)
    found = jnp.dot(
        jnp.concatenate(parts, axis=1), matrix_ref[...], preferred_element_type=jnp.float32
    )
    for j in range(block):
        for depth in range(2):
            rings[step * block + j, depth * each : (depth + 1) * each, :] = found[
                j * each : (j + 1) * each, depth * LANES : (depth + 1) * LANES
            ]

    def send(j, carry):
        s = step * block + j
        pltpu.make_async_copy(rings.at[s], send_ref.at[home_ref[s]], sems.at[s]).start()
        return carry

    lax.fori_loop(0, block, send, 0)

    @pl.when(step == pl.num_programs(0) - 1)
    def _():
        def wait(s, carry):
            pltpu.make_async_copy(rings.at[s], send_ref.at[home_ref[s]], sems.at[s]).wait()
            return carry

        lax.fori_loop(0, slots, wait, 0)


def dust_strips(home_of_slot, dust, bins, owners):
    slots, cells = dust.shape[:2]
    block = 8 if slots % 8 == 0 else 4
    rows = 2 * bins * TZ
    matrix = jnp.asarray(ring_matrix())
    return pl.pallas_call(
        functools.partial(strips_kernel, block=block, bins=bins),
        grid=(slots // block,),
        in_specs=[
            pl.BlockSpec(memory_space=pltpu.SMEM),
            pl.BlockSpec((block, cells, LANES), lambda i: (i, 0, 0)),
            pl.BlockSpec(matrix.shape, lambda i: (0, 0)),
        ],
        out_specs=pl.BlockSpec(memory_space=pl.ANY),
        out_shape=jax.ShapeDtypeStruct((owners, rows, LANES), jnp.float32),
        scratch_shapes=[
            pltpu.VMEM((slots, rows, LANES), jnp.float32),
            pltpu.SemaphoreType.DMA((slots,)),
        ],
        compiler_params=pltpu.CompilerParams(vmem_limit_bytes=32 << 20),
        cost_estimate=pl.CostEstimate(
            flops=20 * dust.size, bytes_accessed=dust.size * 4 + slots * rows * LANES * 4, transcendentals=0
        ),
        name="dust_strips",
    )(home_of_slot, dust, matrix)


def wind_kernel(
    owner_ref, vel_ref, xlo_ref, xhi_ref, ylo_ref, yhi_ref, thr_ref,
    new_ref, send_ref, ring_ref, padded, strip, tiles, load_sem, sems, *, levels
):
    fields, nx, ny = new_ref.shape
    load = pltpu.make_async_copy(vel_ref, padded.at[:, pl.ds(8, nx), :], load_sem)
    load.start()
    load.wait()
    padded[:, 7:8, :] = xlo_ref[...]
    padded[:, 8 + nx : 9 + nx, :] = xhi_ref[...]
    half = 16
    halves = ny // LANES
    tiles_y = ny // TILE
    pattern = ring_pattern(0)
    _, lane8 = iotas()
    group = lane8 // TILE

    def one_strip(ix, carry):
        for sub in range(TILE // half):
            base = pl.multiple_of(ix * TILE + sub * half, 8)
            lane = lax.broadcasted_iota(jnp.int32, (half, ny), 1)
            low = {}
            for z in range(levels):
                u, v, w = (padded[c * levels + z, pl.ds(base + 8, half), :] for c in range(3))
                for c in range(3):
                    f = c * levels + z
                    block = padded[f, pl.ds(base, half + 16), :]
                    centre = (u, v, w)[c]
                    west = pltpu.roll(block, 1, 0)[8 : 8 + half]
                    east = pltpu.roll(block, half + 15, 0)[8 : 8 + half]
                    south = jnp.where(lane == 0, ylo_ref[f, pl.ds(base, half), :], pltpu.roll(centre, 1, 1))
                    north = jnp.where(
                        lane == ny - 1, yhi_ref[f, pl.ds(base, half), :], pltpu.roll(centre, ny - 1, 1)
                    )
                    lower = -centre if z == 0 else padded[f - 1, pl.ds(base + 8, half), :]
                    upper = centre if z == levels - 1 else padded[f + 1, pl.ds(base + 8, half), :]
                    carried = 0.5 * (u * (east - west) + v * (north - south) + w * (upper - lower))
                    spread = east + west + north + south + upper + lower - 6.0 * centre
                    new = centre + time_step * (viscosity * spread - carried)
                    new_ref[f, pl.ds(base, half), :] = new
                    if z < TZ:
                        low[c * TZ + z] = new
            stress = roughness * (low[0] * low[0] + low[TZ] * low[TZ])
            low[PLANES - 1] = emit_rate * stress * jnp.maximum(
                stress - thr_ref[pl.ds(base, half), :], 0.0
            )
            for p in range(PLANES):
                for h in range(halves):
                    strip[p * halves + h, sub * half : (sub + 1) * half, :] = low[p][
                        :, h * LANES : (h + 1) * LANES
                    ]
        for p in range(PLANES):
            for h in range(halves):
                parts = [strip[p * halves + h, pl.ds(k, ROWS, stride=4), :] for k in range(4)]
                for t in range(4):
                    tile = ix * tiles_y + h * 4 + t
                    cells = pltpu.roll(parts[0], (-t * TILE) % LANES, 1) if t else parts[0]
                    for k in range(1, 4):
                        moved = pltpu.roll(parts[k], ((k - t) * TILE) % LANES, 1) if k != t else parts[k]
                        cells = jnp.where(group == k, moved, cells)
                    tiles[tile, p * ROWS : (p + 1) * ROWS, :] = cells
                    ring_ref[tile, p : p + 1, :] = ring_of(cells, pattern)

        def send(t, inner):
            tile = ix * tiles_y + t
            owner = owner_ref[tile]

            @pl.when(owner >= 0)
            def _():
                pltpu.make_async_copy(tiles.at[tile], send_ref.at[owner], sems.at[tile]).start()

            return inner

        lax.fori_loop(0, tiles_y, send, 0)
        return carry

    lax.fori_loop(0, nx // TILE, one_strip, 0)

    def wait(tile, carry):
        owner = owner_ref[tile]

        @pl.when(owner >= 0)
        def _():
            pltpu.make_async_copy(tiles.at[tile], send_ref.at[owner], sems.at[tile]).wait()

        return carry

    lax.fori_loop(0, tiles.shape[0], wait, 0)


def wind_step(owner_of_tile, velocity, xlo, xhi, ylo, yhi, threshold, owners):
    comps, levels, nx, ny = velocity.shape
    fields = comps * levels
    per_home = (nx // TILE) * (ny // TILE)
    smem = pl.BlockSpec(memory_space=pltpu.SMEM)
    hbm = pl.BlockSpec(memory_space=pl.ANY)
    vmem = pl.BlockSpec(memory_space=pltpu.VMEM)
    new, send, ring = pl.pallas_call(
        functools.partial(wind_kernel, levels=levels),
        in_specs=[smem, hbm, vmem, vmem, vmem, vmem, vmem],
        out_specs=[vmem, hbm, vmem],
        out_shape=[
            jax.ShapeDtypeStruct((fields, nx, ny), jnp.float32),
            jax.ShapeDtypeStruct((owners, PLANES * ROWS, LANES), jnp.float32),
            jax.ShapeDtypeStruct((per_home, 8, LANES), jnp.float32),
        ],
        scratch_shapes=[
            pltpu.VMEM((fields, nx + 16, ny), jnp.float32),
            pltpu.VMEM((PLANES * (ny // LANES), TILE, LANES), jnp.float32),
            pltpu.VMEM((per_home, PLANES * ROWS, LANES), jnp.float32),
            pltpu.SemaphoreType.DMA,
            pltpu.SemaphoreType.DMA((per_home,)),
        ],
        compiler_params=pltpu.CompilerParams(vmem_limit_bytes=40 << 20),
        cost_estimate=pl.CostEstimate(
            flops=40 * velocity.size, bytes_accessed=velocity.size * 10, transcendentals=0
        ),
        name="wind_step",
    )(
        owner_of_tile,
        velocity.reshape(fields, nx, ny),
        xlo.reshape(fields, 1, ny),
        xhi.reshape(fields, 1, ny),
        ylo.reshape(fields, nx, 1),
        yhi.reshape(fields, nx, 1),
        threshold,
    )
    return new.reshape(velocity.shape), send, ring


def pack_borders(outs, ring_at, tiles_x, tiles_y):
    rows = outs[0].shape[1]
    lane = lax.broadcasted_iota(jnp.int32, (rows, LANES), 1)
    borders = (
        (EAST, [((tiles_x - 1) * tiles_y + n) for n in range(tiles_y)]),
        (WEST, [n for n in range(tiles_y)]),
        (NORTH, [n * tiles_y + tiles_y - 1 for n in range(tiles_x)]),
        (SOUTH, [n * tiles_y for n in range(tiles_x)]),
    )
    for out, (side, tiles) in zip(outs, borders):
        for g in range(len(tiles) // 4):
            packed = None
            for q in range(4):
                strip = ring_at(tiles[4 * g + q])
                if q != side:
                    strip = pltpu.roll(strip, ((q - side) * TILE) % LANES, 1)
                packed = strip if packed is None else jnp.where(lane // TILE == q, strip, packed)
            out[g] = packed


def fill_halo(ext, borders, tiles_x, tiles_y):
    from_west, from_east, from_south, from_north = borders
    wide = tiles_y + 2
    for ref, side, places in (
        (from_west, EAST, [n + 1 for n in range(tiles_y)]),
        (from_east, WEST, [(tiles_x + 1) * wide + n + 1 for n in range(tiles_y)]),
        (from_south, NORTH, [(n + 1) * wide for n in range(tiles_x)]),
        (from_north, SOUTH, [(n + 1) * wide + tiles_y + 1 for n in range(tiles_x)]),
    ):
        for n, place in enumerate(places):
            strip = ref[n // 4]
            if n % 4 != side:
                strip = pltpu.roll(strip, ((side - n % 4) * TILE) % LANES, 1)
            ext[place] = strip


def seen_by(ext, place, wide):
    west, east = ext[place - wide], ext[place + wide]
    south, north = ext[place - 1], ext[place + 1]
    lane = lax.broadcasted_iota(jnp.int32, west.shape, 1)
    up = pltpu.roll(jnp.where(lane < 2 * TILE, north, west), TILE, 1)
    down = pltpu.roll(jnp.where(lane < 2 * TILE, east, south), LANES - TILE, 1)
    return jnp.where((lane // TILE) % 2 == 0, up, down)


def gather_rings_kernel(owner_ref, recv_ref, rings_ref, e_ref, w_ref, n_ref, s_ref, *, tiles_x, tiles_y):
    rows = e_ref.shape[1]

    def one(t, carry):
        owner = owner_ref[t]
        rings = recv_ref[jnp.maximum(owner, 0)]
        rings_ref[t] = jnp.where(owner >= 0, rings, 0.0)
        return carry

    lax.fori_loop(0, tiles_x * tiles_y, one, 0)
    pack_borders((e_ref, w_ref, n_ref, s_ref), lambda t: rings_ref[t, :rows, :], tiles_x, tiles_y)


def advance_rings_kernel(
    owner_ref, rings_ref, fw_ref, fe_ref, fs_ref, fn_ref, wind_ref, settle_ref, share_ref,
    seen_ref, later_ref, e_ref, w_ref, n_ref, s_ref, ext, *, tiles_x, tiles_y
):
    per_home = tiles_x * tiles_y
    rows = e_ref.shape[1]
    wide = tiles_y + 2
    fill_halo(ext, (fw_ref, fe_ref, fs_ref, fn_ref), tiles_x, tiles_y)

    def place_of(t):
        return (t // tiles_y + 1) * wide + t % tiles_y + 1

    def inner(t, carry):
        ext[place_of(t)] = rings_ref[t, :rows, :]
        return carry

    lax.fori_loop(0, per_home, inner, 0)

    _, lane = iotas()
    group, within = lane // TILE, lane % TILE
    on_x = (group == WEST) | (group == EAST)
    first, last = within == 0, within == TILE - 1
    high = jnp.where((group == EAST) | (group == NORTH), TILE - 1, 0)
    corner = jnp.where(
        on_x,
        jnp.where(first, SOUTH, NORTH) * TILE + high,
        jnp.where(first, WEST, EAST) * TILE + high,
    )

    def one(t, carry):
        place = place_of(t)
        seen = seen_by(ext, place, wide)
        seen_ref[t] = seen

        uplift = dust_step * spread_rows(wind_ref[t, PLANES - 1 : PLANES, :])
        mix = dust_step * diffusion
        active = owner_ref[t] >= 0
        bins = rows // TZ
        for chunk in range(rows // ROWS):
            at = chunk * ROWS
            level, bin_at = at // bins, at % bins
            if bin_at == 0:
                u, v, w = (
                    dust_step * spread_rows(wind_ref[t, c * TZ + level : c * TZ + level + 1, :]) for c in range(3)
                )
                from_west = mix + jnp.maximum(u, 0.0)
                from_east = mix + jnp.maximum(-u, 0.0)
                from_south = mix + jnp.maximum(v, 0.0)
                from_north = mix + jnp.maximum(-v, 0.0)
                keep = 1.0 - 6.0 * mix - jnp.abs(u) - jnp.abs(v)
            q = rings_ref[t, at : at + ROWS, :]
            deep = rings_ref[t, rows + at : rows + at + ROWS, :]
            out = seen[at : at + ROWS, :]
            beyond = lane_gather(out, corner)
            before = jnp.where(first, beyond, pltpu.roll(q, 1, 1))
            after = jnp.where(last, beyond, pltpu.roll(q, LANES - 1, 1))
            west = jnp.where(group == WEST, out, jnp.where(group == EAST, deep, before))
            east = jnp.where(group == WEST, deep, jnp.where(group == EAST, out, after))
            south = jnp.where(on_x, before, jnp.where(group == SOUTH, out, deep))
            north = jnp.where(on_x, after, jnp.where(group == SOUTH, deep, out))
            other_at = (1 - level) * bins + bin_at
            other = rings_ref[t, other_at : other_at + ROWS, :]
            rise = w - dust_step * settle_ref[bin_at : bin_at + ROWS, :]
            up = jnp.maximum(rise, 0.0)
            down = up - rise
            new = (
                (keep - up - down) * q
                + from_west * west
                + from_east * east
                + from_south * south
                + from_north * north
                + (mix + (down if level == 0 else up)) * other
            )
            if level == 0:
                new = new + uplift * share_ref[bin_at : bin_at + ROWS, :]
            later_ref[t, at : at + ROWS, :] = jnp.where(active, new, 0.0)
        return carry

    lax.fori_loop(0, per_home, one, 0)
    pack_borders((e_ref, w_ref, n_ref, s_ref), lambda t: later_ref[t], tiles_x, tiles_y)


def send_seen_kernel(
    owner_ref, later_ref, fw_ref, fe_ref, fs_ref, fn_ref, seen_ref, send_ref, ext, both, sems, *, tiles_x, tiles_y
):
    per_home = tiles_x * tiles_y
    rows = later_ref.shape[1]
    wide = tiles_y + 2
    fill_halo(ext, (fw_ref, fe_ref, fs_ref, fn_ref), tiles_x, tiles_y)

    def place_of(t):
        return (t // tiles_y + 1) * wide + t % tiles_y + 1

    def inner(t, carry):
        ext[place_of(t)] = later_ref[t]
        return carry

    lax.fori_loop(0, per_home, inner, 0)

    def one(t, carry):
        both[t, :rows, :] = seen_ref[t]
        both[t, rows:, :] = seen_by(ext, place_of(t), wide)
        owner = owner_ref[t]

        @pl.when(owner >= 0)
        def _():
            pltpu.make_async_copy(both.at[t], send_ref.at[owner], sems.at[t]).start()

        return carry

    lax.fori_loop(0, per_home, one, 0)

    def wait(t, carry):
        owner = owner_ref[t]

        @pl.when(owner >= 0)
        def _():
            pltpu.make_async_copy(both.at[t], send_ref.at[owner], sems.at[t]).wait()

        return carry

    lax.fori_loop(0, per_home, wait, 0)


def shifted(value, axis, steps):
    count = lax.axis_size(axis)
    return lax.ppermute(value, axis, [(source, (source + steps) % count) for source in range(count)])


def exchange_borders(borders):
    east, west, north, south = borders
    return shifted(east, "gx", 1), shifted(west, "gx", -1), shifted(north, "gy", 1), shifted(south, "gy", -1)


def f32(*shape):
    return jax.ShapeDtypeStruct(shape, jnp.float32)


def ring_call(kernel, tiles_x, tiles_y, rows, outs, scratch, name, hbm_out=False):
    smem = pl.BlockSpec(memory_space=pltpu.SMEM)
    vmem = pl.BlockSpec(memory_space=pltpu.VMEM)
    size = tiles_x * tiles_y * rows * LANES

    def call(owner_of_tile, *inputs):
        return pl.pallas_call(
            functools.partial(kernel, tiles_x=tiles_x, tiles_y=tiles_y),
            in_specs=[smem] + [vmem] * len(inputs),
            out_specs=pl.BlockSpec(memory_space=pl.ANY) if hbm_out else [vmem] * len(outs),
            out_shape=outs[0] if hbm_out else outs,
            scratch_shapes=scratch,
            compiler_params=pltpu.CompilerParams(vmem_limit_bytes=32 << 20),
            cost_estimate=pl.CostEstimate(flops=16 * size, bytes_accessed=16 * size, transcendentals=0),
            name=name,
        )(owner_of_tile, *inputs)

    return call


def border_shapes(tiles_x, tiles_y, rows):
    return [f32(tiles_y // 4, rows, LANES)] * 2 + [f32(tiles_x // 4, rows, LANES)] * 2


def gather_rings(owner_of_tile, received, tiles_x, tiles_y):
    both_rows = received.shape[1]
    rows = both_rows // 2
    outs = [f32(tiles_x * tiles_y, both_rows, LANES)] + border_shapes(tiles_x, tiles_y, rows)
    return ring_call(gather_rings_kernel, tiles_x, tiles_y, rows, outs, [], "gather_rings")(owner_of_tile, received)


def relay_rings(owner_of_tile, rings, borders, wind_ring, settle_speed, bin_share, tiles_x, tiles_y, owners):
    per_home, both_rows, _ = rings.shape
    rows = both_rows // 2
    ext = pltpu.VMEM(((tiles_x + 2) * (tiles_y + 2), rows, LANES), jnp.float32)
    settle_rows = jnp.broadcast_to(settle_speed[:, None], settle_speed.shape + (LANES,))
    share_rows = jnp.broadcast_to(bin_share[:, None], bin_share.shape + (LANES,))
    outs = [f32(per_home, rows, LANES)] * 2 + border_shapes(tiles_x, tiles_y, rows)
    advance = ring_call(advance_rings_kernel, tiles_x, tiles_y, rows, outs, [ext], "advance_rings")
    seen, later, *borders = advance(owner_of_tile, rings, *borders, wind_ring, settle_rows, share_rows)
    outs = [f32(owners, both_rows, LANES)]
    scratch = [ext, pltpu.VMEM((per_home, both_rows, LANES), jnp.float32), pltpu.SemaphoreType.DMA((per_home,))]
    send = ring_call(send_seen_kernel, tiles_x, tiles_y, rows, outs, scratch, "send_seen", hbm_out=True)
    return send(owner_of_tile, later, *exchange_borders(borders), seen)


def dust_kernel(home_ref, share_ref, settle_ref, dust_ref, shift_ref, wind_ref, *refs, block, bins, outer):
    if outer:
        side_ref, seen_ref, out_ref, coef, sides, edges, *work = refs
    else:
        out_ref, coef, *work = refs
    lanes = len(work) // 2
    step = pl.program_id(0)
    each = TZ * bins
    if outer:
        for j in range(block):
            edges[j] = seen_ref[home_ref[step * block + j]]
        spread = jnp.dot(
            jnp.concatenate(halves_of(edges[...].reshape(block * 2 * each, LANES)), axis=1),
            side_ref[...],
            preferred_element_type=jnp.float32,
        )
        for r in range(ROWS):
            sides[r] = spread[:, r * LANES : (r + 1) * LANES]

    _, lane = iotas()
    within = lane % TILE
    first_y, last_y = within == 0, within == TILE - 1
    low_lanes, high_lanes = lane < TILE, lane >= LANES - TILE
    mix = dust_step * diffusion
    chunks = bins // ROWS
    settle = [dust_step * settle_ref[h * ROWS : (h + 1) * ROWS, :] for h in range(chunks)]
    share = [share_ref[h * ROWS : (h + 1) * ROWS, :] for h in range(chunks)]

    def prepare(k, j):
        held = work[2 * k]
        home = home_ref[step * block + j]
        plane = [wind_ref[home, p * ROWS : (p + 1) * ROWS, :] * dust_step for p in range(PLANES)]
        for level in range(TZ):
            u, v = plane[level], plane[TZ + level]
            south_by = mix + jnp.maximum(v, 0.0)
            north_by = mix + jnp.maximum(-v, 0.0)
            coef[k, 0, level] = mix + jnp.maximum(u, 0.0)
            coef[k, 1, level] = mix + jnp.maximum(-u, 0.0)
            coef[k, 4, level] = 1.0 - 6.0 * mix - jnp.abs(u) - jnp.abs(v)
            coef[k, 5, level] = plane[2 * TZ + level]
            if outer:
                coef[k, 2, level] = south_by
                coef[k, 3, level] = north_by
                coef[k, 7, level] = jnp.where(first_y, south_by, jnp.where(last_y, north_by, 0.0))
            else:
                coef[k, 2, level] = jnp.where(first_y, 0.0, south_by)
                coef[k, 3, level] = jnp.where(last_y, 0.0, north_by)
        coef[k, 6, 0] = plane[PLANES - 1]
        for r in range(ROWS):
            for level in range(TZ):
                at = (r * TZ + level) * bins
                cells = dust_ref[j, pl.ds(r * TZ + level, bins, stride=ROWS * TZ), :]
                if not outer:
                    held[at : at + bins, :] = cells
                    continue
                for h in range(chunks):
                    edge_at = level * bins + h * ROWS
                    q = cells[h * ROWS : (h + 1) * ROWS]
                    q = q + spread_rows(coef[k, 7, level, r : r + 1, :]) * sides[r, pl.ds(j * 2 * each + edge_at, ROWS), :]
                    if r == 0 or r == ROWS - 1:
                        edge = edges[j, edge_at : edge_at + ROWS, :]
                        here = low_lanes if r == 0 else high_lanes
                        by = spread_rows(coef[k, 0 if r == 0 else 1, level, r : r + 1, :])
                        q = q + jnp.where(here, by * edge, 0.0)
                    held[at + h * ROWS : at + (h + 1) * ROWS, :] = q

    def shift(k):
        held, shifts = work[2 * k], work[2 * k + 1]
        shifts[...] = jnp.dot(
            jnp.concatenate(halves_of(held[...]), axis=1), shift_ref[...], preferred_element_type=jnp.float32
        )

    def update(k, j):
        held, shifts = work[2 * k], work[2 * k + 1]
        nothing = jnp.zeros((ROWS, LANES), jnp.float32)
        for r in range(ROWS):
            for h in range(chunks):
                cells = [held[(r * TZ + level) * bins + h * ROWS :][:ROWS] for level in range(TZ)]
                for level in range(TZ):
                    at = (r * TZ + level) * bins + h * ROWS
                    edge_at = each + level * bins + h * ROWS

                    def moved(which, rows_up=0):
                        first = at + rows_up * TZ * bins
                        return shifts[first : first + ROWS, which * LANES : (which + 1) * LANES]

                    def by(which):
                        return spread_rows(coef[k, which, level, r : r + 1, :])

                    edge = edges[j, edge_at : edge_at + ROWS, :] if outer else nothing
                    before = edge if r == 0 else moved(2, -1)
                    after = edge if r == ROWS - 1 else moved(3, 1)
                    south, north = moved(0), moved(1)
                    if outer:
                        side = sides[r, pl.ds(j * 2 * each + edge_at, ROWS), :]
                        south = jnp.where(first_y, side, south)
                        north = jnp.where(last_y, side, north)
                    west = jnp.where(low_lanes, before, moved(2))
                    east = jnp.where(high_lanes, after, moved(3))
                    rise = by(5) - settle[h]
                    up = jnp.maximum(rise, 0.0)
                    mixed = mix + (up - rise if level == 0 else up)
                    value = (
                        (by(4) - jnp.abs(rise)) * cells[level]
                        + by(0) * west
                        + by(1) * east
                        + by(2) * south
                        + by(3) * north
                        + mixed * cells[1 - level]
                    )
                    if level == 0:
                        value = value + spread_rows(coef[k, 6, 0, r : r + 1, :]) * share[h]
                    first = h * ROWS * ROWS * TZ + r * TZ + level
                    out_ref[j, pl.ds(first, ROWS, stride=ROWS * TZ), :] = value

    def some(i, carry):
        for k in range(lanes):
            prepare(k, i * lanes + k)
        for k in range(lanes):
            shift(k)
        for k in range(lanes):
            update(k, i * lanes + k)
        return carry

    lax.fori_loop(0, block // lanes, some, 0)


def dust_substep(home_of_slot, dust, wind_recv, settle_speed, bin_share, seen_recv=None):
    slots, cells = dust.shape[:2]
    bins = settle_speed.shape[0]
    block = 8 if slots % 8 == 0 else 4
    lanes = 2
    outer = seen_recv is not None
    smem = pl.BlockSpec(memory_space=pltpu.SMEM)
    vmem = pl.BlockSpec(memory_space=pltpu.VMEM)
    tile = pl.BlockSpec((block, cells, LANES), lambda i: (i, 0, 0))
    settle = jnp.broadcast_to(settle_speed[:, None], (bins, LANES))
    share = jnp.broadcast_to(bin_share[:, None], (bins, LANES))
    inputs = [home_of_slot, share, settle, dust, jnp.asarray(shift_matrix()), wind_recv]
    scratch = [pltpu.VMEM((lanes, PLANES + 1, TZ, ROWS, LANES), jnp.float32)]
    if outer:
        inputs += [jnp.asarray(side_matrix()), seen_recv]
        scratch += [
            pltpu.VMEM((ROWS, block * seen_recv.shape[1], LANES), jnp.float32),
            pltpu.VMEM((block,) + seen_recv.shape[1:], jnp.float32),
        ]
    scratch += [pltpu.VMEM((cells, LANES), jnp.float32), pltpu.VMEM((cells, 4 * LANES), jnp.float32)] * lanes
    return pl.pallas_call(
        functools.partial(dust_kernel, block=block, bins=bins, outer=outer),
        grid=(slots // block,),
        in_specs=[smem, vmem, vmem, tile] + [vmem] * (len(inputs) - 4),
        out_specs=tile,
        out_shape=jax.ShapeDtypeStruct(dust.shape, jnp.float32),
        scratch_shapes=scratch,
        compiler_params=pltpu.CompilerParams(vmem_limit_bytes=32 << 20),
        cost_estimate=pl.CostEstimate(flops=60 * dust.size, bytes_accessed=dust.size * 12, transcendentals=0),
        name="dust_outer" if outer else "dust_inner",
    )(*inputs)


def relay_rows(rows):
    return lax.all_to_all(rows, AXES, split_axis=0, concat_axis=0, tiled=True)


def per_device(velocity, threshold, dust_mass, settle_speed, bin_share, active_tiles, tile_owner):
    owners = lax.axis_size(AXES)
    grid_cols = lax.axis_size("gy")
    self_index = lax.axis_index(AXES)
    slots, bins = dust_mass.shape[:2]
    tiles_x = velocity.shape[2] // TILE
    tiles_y = velocity.shape[3] // TILE
    per_home = tiles_x * tiles_y
    tiles_across = tiles_y * grid_cols

    tile_x = active_tiles // tiles_across
    tile_y = active_tiles % tiles_across
    home_dev = tile_x // tiles_x * grid_cols + tile_y // tiles_y
    local_tile = tile_x % tiles_x * tiles_y + tile_y % tiles_y
    own_slot = tile_owner - self_index * slots
    mine = jnp.where(home_dev == self_index, local_tile, -1)
    slot_ids = jnp.arange(slots, dtype=jnp.int32)
    home_of_slot = jnp.sum(jnp.where(own_slot[None, :] == slot_ids[:, None], home_dev[None, :], 0), axis=1)
    tile_ids = jnp.arange(per_home, dtype=jnp.int32)
    owner_of_tile = jnp.max(
        jnp.where(mine[None, :] == tile_ids[:, None], (tile_owner // slots)[None, :], -1), axis=1
    )

    dust = dust_mass.reshape(slots, bins, TZ, ROWS, LANES).transpose(0, 1, 3, 2, 4)
    dust = dust.reshape(slots, bins * ROWS * TZ, LANES)

    xlo = shifted(velocity[:, :, -1, :], "gx", 1)
    xhi = shifted(velocity[:, :, 0, :], "gx", -1)
    ylo = shifted(velocity[:, :, :, -1], "gy", 1)
    yhi = shifted(velocity[:, :, :, 0], "gy", -1)

    strips_send = dust_strips(home_of_slot, dust, bins, owners)
    strips_send, xlo, xhi, ylo, yhi = lax.optimization_barrier((strips_send, xlo, xhi, ylo, yhi))
    strips = relay_rows(strips_send)
    new_velocity, wind_send, wind_ring = wind_step(
        owner_of_tile, velocity, xlo, xhi, ylo, yhi, threshold, owners
    )
    rings, *borders = gather_rings(owner_of_tile, strips, tiles_x, tiles_y)
    borders = exchange_borders(borders)
    wind_send, *borders = lax.optimization_barrier((wind_send, *borders))
    wind_recv = relay_rows(wind_send)
    seen_send = relay_rings(
        owner_of_tile, rings, borders, wind_ring, settle_speed, bin_share, tiles_x, tiles_y, owners
    )
    seen_recv = relay_rows(seen_send)
    inner = dust_substep(home_of_slot, dust, wind_recv, settle_speed, bin_share)
    out = dust_substep(home_of_slot, inner, wind_recv, settle_speed, bin_share, seen_recv)
    out = out.reshape(slots, bins, ROWS, TZ, LANES).transpose(0, 1, 3, 2, 4).reshape(dust_mass.shape)
    return new_velocity, out


def solution(mesh):
    in_specs = (
        P(None, None, "gx", "gy"),
        P("gx", "gy"),
        P(AXES, None, None, None),
        P(),
        P(),
        P(),
        P(),
    )
    out_specs = (P(None, None, "gx", "gy"), P(AXES, None, None, None))
    return jax.shard_map(
        per_device, mesh=mesh, in_specs=in_specs, out_specs=out_specs, check_vma=False
    )
```

```python
import functools

import jax
import jax.numpy as jnp
import ml_dtypes
import numpy as np
from jax import lax
from jax.experimental import pallas as pl
from jax.experimental.pallas import tpu as pltpu
from jax.sharding import PartitionSpec as P

TZ = 2
TILE = 32
LANES = 128
ROWS = TILE * TILE // LANES
PLANES = 7
AXES = ("gx", "gy")

time_step = 0.1
viscosity = 0.2
dust_step = 0.1
diffusion = 0.1
roughness = 0.5
emit_rate = 0.5

WEST, SOUTH, NORTH, EAST = range(4)


def iotas(shape=(ROWS, LANES)):
    return lax.broadcasted_iota(jnp.int32, shape, 0), lax.broadcasted_iota(jnp.int32, shape, 1)


def lane_gather(x, index):
    return jnp.take_along_axis(x, index, axis=1)


def ring_pattern(depth):
    row, lane = iotas()
    group, within = lane // TILE, lane % TILE
    side = jnp.where(group == SOUTH, depth, TILE - 1 - depth)
    index = (within % 4) * TILE + side
    index = jnp.where(group == WEST, depth * TILE + within, index)
    index = jnp.where(group == EAST, (3 - depth) * TILE + within, index)
    source = jnp.where(group == WEST, 0, jnp.where(group == EAST, ROWS - 1, within // 4))
    return index, row == source


def ring_of(x, pattern):
    index, taken = pattern
    return jnp.sum(jnp.where(taken, lane_gather(x, index), 0.0), axis=0, keepdims=True)


def spread_rows(row):
    return jnp.broadcast_to(row, (ROWS, LANES))


def f32(*shape):
    return jax.ShapeDtypeStruct(shape, jnp.float32)


def in_hbm(x):
    return pltpu.with_memory_space_constraint(x, pltpu.HBM)


def halves_of(x):
    high = x.astype(jnp.bfloat16)
    return high, (x - high.astype(jnp.float32)).astype(jnp.bfloat16)


def moves(sources):
    lanes = np.arange(LANES)[:, None]
    once = (lanes == np.asarray(sources)[None, :]).astype(ml_dtypes.bfloat16)
    return np.concatenate([once, once], axis=0)


def ring_matrix():
    lane = np.arange(LANES)
    group, within = lane // TILE, lane % TILE
    blocks = []
    for r in range(ROWS):
        columns = []
        for depth in range(2):
            side = np.where(group == SOUTH, depth, TILE - 1 - depth)
            source = np.where(within // 4 == r, (within % 4) * TILE + side, -1)
            source = np.where(group == WEST, depth * TILE + within if r == 0 else -1, source)
            source = np.where(group == EAST, (3 - depth) * TILE + within if r == ROWS - 1 else -1, source)
            columns.append(source)
        blocks.append(moves(np.concatenate(columns)))
    return np.concatenate(blocks, axis=0)


def shift_matrix():
    lane = np.arange(LANES)
    return moves(np.concatenate([(lane + d) % LANES for d in (-1, 1, -TILE, TILE)]))


def side_matrix():
    lane = np.arange(LANES)
    columns = []
    for r in range(ROWS):
        along = 4 * r + lane // TILE
        source = np.where(lane % TILE == 0, SOUTH * TILE + along, -1)
        columns.append(np.where(lane % TILE == TILE - 1, NORTH * TILE + along, source))
    return moves(np.concatenate(columns))


def strips_kernel(home_ref, dust_ref, matrix_ref, send_ref, rings, sems, *, block, bins):
    step = pl.program_id(0)
    slots = rings.shape[0]
    each = TZ * bins

    parts = []
    for r in range(ROWS):
        x = jnp.concatenate(
            [
                dust_ref[j, pl.ds(r * TZ + level, bins, stride=ROWS * TZ), :]
                for j in range(block)
                for level in range(TZ)
            ],
            axis=0,
        )
        parts += halves_of(x)
    found = jnp.dot(
        jnp.concatenate(parts, axis=1), matrix_ref[...], preferred_element_type=jnp.float32
    )
    for j in range(block):
        for depth in range(2):
            rings[step * block + j, depth * each : (depth + 1) * each, :] = found[
                j * each : (j + 1) * each, depth * LANES : (depth + 1) * LANES
            ]

    def send(j, carry):
        s = step * block + j
        pltpu.make_async_copy(rings.at[s], send_ref.at[home_ref[s]], sems.at[s]).start()
        return carry

    lax.fori_loop(0, block, send, 0)

    @pl.when(step == pl.num_programs(0) - 1)
    def _():
        def wait(s, carry):
            pltpu.make_async_copy(rings.at[s], send_ref.at[home_ref[s]], sems.at[s]).wait()
            return carry

        lax.fori_loop(0, slots, wait, 0)


def dust_strips(home_of_slot, dust, bins, owners):
    slots, cells = dust.shape[:2]
    block = 8 if slots % 8 == 0 else 4
    rows = 2 * bins * TZ
    matrix = jnp.asarray(ring_matrix())
    return pl.pallas_call(
        functools.partial(strips_kernel, block=block, bins=bins),
        grid=(slots // block,),
        in_specs=[
            pl.BlockSpec(memory_space=pltpu.SMEM),
            pl.BlockSpec((block, cells, LANES), lambda i: (i, 0, 0)),
            pl.BlockSpec(matrix.shape, lambda i: (0, 0)),
        ],
        out_specs=pl.BlockSpec(memory_space=pltpu.HBM),
        out_shape=pltpu.HBM((owners, rows, LANES), jnp.float32),
        scratch_shapes=[
            pltpu.VMEM((slots, rows, LANES), jnp.float32),
            pltpu.SemaphoreType.DMA((slots,)),
        ],
        compiler_params=pltpu.CompilerParams(vmem_limit_bytes=32 << 20),
        cost_estimate=pl.CostEstimate(
            flops=20 * dust.size, bytes_accessed=dust.size * 4 + slots * rows * LANES * 4, transcendentals=0
        ),
        name="dust_strips",
    )(home_of_slot, in_hbm(dust), matrix)


def wind_kernel(
    owner_ref, vel_ref, xlo_ref, xhi_ref, ylo_ref, yhi_ref, thr_ref,
    new_ref, send_ref, ring_ref, padded, strip, tiles, load_sem, sems, *, levels
):
    fields, nx, ny = new_ref.shape
    load = pltpu.make_async_copy(vel_ref, padded.at[:, pl.ds(8, nx), :], load_sem)
    load.start()
    load.wait()
    padded[:, 7:8, :] = xlo_ref[...]
    padded[:, 8 + nx : 9 + nx, :] = xhi_ref[...]
    half = 16
    halves = ny // LANES
    tiles_y = ny // TILE
    pattern = ring_pattern(0)
    _, lane8 = iotas()
    group = lane8 // TILE

    def one_strip(ix, carry):
        for sub in range(TILE // half):
            base = pl.multiple_of(ix * TILE + sub * half, 8)
            lane = lax.broadcasted_iota(jnp.int32, (half, ny), 1)
            low = {}
            for z in range(levels):
                u, v, w = (padded[c * levels + z, pl.ds(base + 8, half), :] for c in range(3))
                for c in range(3):
                    f = c * levels + z
                    block = padded[f, pl.ds(base, half + 16), :]
                    centre = (u, v, w)[c]
                    west = pltpu.roll(block, 1, 0)[8 : 8 + half]
                    east = pltpu.roll(block, half + 15, 0)[8 : 8 + half]
                    south = jnp.where(lane == 0, ylo_ref[f, pl.ds(base, half), :], pltpu.roll(centre, 1, 1))
                    north = jnp.where(
                        lane == ny - 1, yhi_ref[f, pl.ds(base, half), :], pltpu.roll(centre, ny - 1, 1)
                    )
                    lower = -centre if z == 0 else padded[f - 1, pl.ds(base + 8, half), :]
                    upper = centre if z == levels - 1 else padded[f + 1, pl.ds(base + 8, half), :]
                    carried = 0.5 * (u * (east - west) + v * (north - south) + w * (upper - lower))
                    spread = east + west + north + south + upper + lower - 6.0 * centre
                    new = centre + time_step * (viscosity * spread - carried)
                    new_ref[f, pl.ds(base, half), :] = new
                    if z < TZ:
                        low[c * TZ + z] = new
            stress = roughness * (low[0] * low[0] + low[TZ] * low[TZ])
            low[PLANES - 1] = emit_rate * stress * jnp.maximum(
                stress - thr_ref[pl.ds(base, half), :], 0.0
            )
            for p in range(PLANES):
                for h in range(halves):
                    strip[p * halves + h, sub * half : (sub + 1) * half, :] = low[p][
                        :, h * LANES : (h + 1) * LANES
                    ]
        for p in range(PLANES):
            for h in range(halves):
                parts = [strip[p * halves + h, pl.ds(k, ROWS, stride=4), :] for k in range(4)]
                for t in range(4):
                    tile = ix * tiles_y + h * 4 + t
                    cells = pltpu.roll(parts[0], (-t * TILE) % LANES, 1) if t else parts[0]
                    for k in range(1, 4):
                        moved = pltpu.roll(parts[k], ((k - t) * TILE) % LANES, 1) if k != t else parts[k]
                        cells = jnp.where(group == k, moved, cells)
                    tiles[tile, p * ROWS : (p + 1) * ROWS, :] = cells
                    ring_ref[tile, p : p + 1, :] = ring_of(cells, pattern)

        def send(t, inner):
            tile = ix * tiles_y + t
            owner = owner_ref[tile]

            @pl.when(owner >= 0)
            def _():
                pltpu.make_async_copy(tiles.at[tile], send_ref.at[owner], sems.at[tile]).start()

            return inner

        lax.fori_loop(0, tiles_y, send, 0)
        return carry

    lax.fori_loop(0, nx // TILE, one_strip, 0)

    def wait(tile, carry):
        owner = owner_ref[tile]

        @pl.when(owner >= 0)
        def _():
            pltpu.make_async_copy(tiles.at[tile], send_ref.at[owner], sems.at[tile]).wait()

        return carry

    lax.fori_loop(0, tiles.shape[0], wait, 0)


def wind_step(owner_of_tile, velocity, xlo, xhi, ylo, yhi, threshold, owners):
    comps, levels, nx, ny = velocity.shape
    fields = comps * levels
    per_home = (nx // TILE) * (ny // TILE)
    smem = pl.BlockSpec(memory_space=pltpu.SMEM)
    hbm = pl.BlockSpec(memory_space=pltpu.HBM)
    vmem = pl.BlockSpec(memory_space=pltpu.VMEM)
    new, send, ring = pl.pallas_call(
        functools.partial(wind_kernel, levels=levels),
        in_specs=[smem, hbm, vmem, vmem, vmem, vmem, vmem],
        out_specs=[vmem, hbm, vmem],
        out_shape=[
            f32(fields, nx, ny),
            pltpu.HBM((owners, PLANES * ROWS, LANES), jnp.float32),
            f32(per_home, 8, LANES),
        ],
        scratch_shapes=[
            pltpu.VMEM((fields, nx + 16, ny), jnp.float32),
            pltpu.VMEM((PLANES * (ny // LANES), TILE, LANES), jnp.float32),
            pltpu.VMEM((per_home, PLANES * ROWS, LANES), jnp.float32),
            pltpu.SemaphoreType.DMA,
            pltpu.SemaphoreType.DMA((per_home,)),
        ],
        compiler_params=pltpu.CompilerParams(vmem_limit_bytes=40 << 20),
        cost_estimate=pl.CostEstimate(
            flops=40 * velocity.size, bytes_accessed=velocity.size * 10, transcendentals=0
        ),
        name="wind_step",
    )(
        owner_of_tile,
        in_hbm(velocity.reshape(fields, nx, ny)),
        xlo.reshape(fields, 1, ny),
        xhi.reshape(fields, 1, ny),
        ylo.reshape(fields, nx, 1),
        yhi.reshape(fields, nx, 1),
        threshold,
    )
    return new.reshape(velocity.shape), send, ring


def pack_borders(outs, ring_at, tiles_x, tiles_y):
    rows = outs[0].shape[1]
    lane = lax.broadcasted_iota(jnp.int32, (rows, LANES), 1)
    borders = (
        (EAST, [((tiles_x - 1) * tiles_y + n) for n in range(tiles_y)]),
        (WEST, [n for n in range(tiles_y)]),
        (NORTH, [n * tiles_y + tiles_y - 1 for n in range(tiles_x)]),
        (SOUTH, [n * tiles_y for n in range(tiles_x)]),
    )
    for out, (side, tiles) in zip(outs, borders):
        for g in range(len(tiles) // 4):
            packed = None
            for q in range(4):
                strip = ring_at(tiles[4 * g + q])
                if q != side:
                    strip = pltpu.roll(strip, ((q - side) * TILE) % LANES, 1)
                packed = strip if packed is None else jnp.where(lane // TILE == q, strip, packed)
            out[g] = packed


def fill_halo(ext, borders, tiles_x, tiles_y):
    from_west, from_east, from_south, from_north = borders
    wide = tiles_y + 2
    for ref, side, places in (
        (from_west, EAST, [n + 1 for n in range(tiles_y)]),
        (from_east, WEST, [(tiles_x + 1) * wide + n + 1 for n in range(tiles_y)]),
        (from_south, NORTH, [(n + 1) * wide for n in range(tiles_x)]),
        (from_north, SOUTH, [(n + 1) * wide + tiles_y + 1 for n in range(tiles_x)]),
    ):
        for n, place in enumerate(places):
            strip = ref[n // 4]
            if n % 4 != side:
                strip = pltpu.roll(strip, ((side - n % 4) * TILE) % LANES, 1)
            ext[place] = strip


def seen_by(ext, place, wide):
    west, east = ext[place - wide], ext[place + wide]
    south, north = ext[place - 1], ext[place + 1]
    lane = lax.broadcasted_iota(jnp.int32, west.shape, 1)
    up = pltpu.roll(jnp.where(lane < 2 * TILE, north, west), TILE, 1)
    down = pltpu.roll(jnp.where(lane < 2 * TILE, east, south), LANES - TILE, 1)
    return jnp.where((lane // TILE) % 2 == 0, up, down)


def gather_rings_kernel(owner_ref, recv_ref, rings_ref, e_ref, w_ref, n_ref, s_ref, *, tiles_x, tiles_y):
    rows = e_ref.shape[1]

    def one(t, carry):
        owner = owner_ref[t]
        rings = recv_ref[jnp.maximum(owner, 0)]
        rings_ref[t] = jnp.where(owner >= 0, rings, 0.0)
        return carry

    lax.fori_loop(0, tiles_x * tiles_y, one, 0)
    pack_borders((e_ref, w_ref, n_ref, s_ref), lambda t: rings_ref[t, :rows, :], tiles_x, tiles_y)


def advance_rings_kernel(
    owner_ref, rings_ref, fw_ref, fe_ref, fs_ref, fn_ref, wind_ref, settle_ref, share_ref,
    seen_ref, later_ref, e_ref, w_ref, n_ref, s_ref, ext, *, tiles_x, tiles_y
):
    per_home = tiles_x * tiles_y
    rows = e_ref.shape[1]
    wide = tiles_y + 2
    fill_halo(ext, (fw_ref, fe_ref, fs_ref, fn_ref), tiles_x, tiles_y)

    def place_of(t):
        return (t // tiles_y + 1) * wide + t % tiles_y + 1

    def inner(t, carry):
        ext[place_of(t)] = rings_ref[t, :rows, :]
        return carry

    lax.fori_loop(0, per_home, inner, 0)

    _, lane = iotas()
    group, within = lane // TILE, lane % TILE
    on_x = (group == WEST) | (group == EAST)
    first, last = within == 0, within == TILE - 1
    high = jnp.where((group == EAST) | (group == NORTH), TILE - 1, 0)
    corner = jnp.where(
        on_x,
        jnp.where(first, SOUTH, NORTH) * TILE + high,
        jnp.where(first, WEST, EAST) * TILE + high,
    )

    def one(t, carry):
        place = place_of(t)
        seen = seen_by(ext, place, wide)
        seen_ref[t] = seen

        uplift = dust_step * spread_rows(wind_ref[t, PLANES - 1 : PLANES, :])
        mix = dust_step * diffusion
        active = owner_ref[t] >= 0
        bins = rows // TZ
        for chunk in range(rows // ROWS):
            at = chunk * ROWS
            level, bin_at = at // bins, at % bins
            if bin_at == 0:
                u, v, w = (
                    dust_step * spread_rows(wind_ref[t, c * TZ + level : c * TZ + level + 1, :]) for c in range(3)
                )
                from_west = mix + jnp.maximum(u, 0.0)
                from_east = mix + jnp.maximum(-u, 0.0)
                from_south = mix + jnp.maximum(v, 0.0)
                from_north = mix + jnp.maximum(-v, 0.0)
                keep = 1.0 - 6.0 * mix - jnp.abs(u) - jnp.abs(v)
            q = rings_ref[t, at : at + ROWS, :]
            deep = rings_ref[t, rows + at : rows + at + ROWS, :]
            out = seen[at : at + ROWS, :]
            beyond = lane_gather(out, corner)
            before = jnp.where(first, beyond, pltpu.roll(q, 1, 1))
            after = jnp.where(last, beyond, pltpu.roll(q, LANES - 1, 1))
            west = jnp.where(group == WEST, out, jnp.where(group == EAST, deep, before))
            east = jnp.where(group == WEST, deep, jnp.where(group == EAST, out, after))
            south = jnp.where(on_x, before, jnp.where(group == SOUTH, out, deep))
            north = jnp.where(on_x, after, jnp.where(group == SOUTH, deep, out))
            other_at = (1 - level) * bins + bin_at
            other = rings_ref[t, other_at : other_at + ROWS, :]
            rise = w - dust_step * settle_ref[bin_at : bin_at + ROWS, :]
            up = jnp.maximum(rise, 0.0)
            down = up - rise
            new = (
                (keep - up - down) * q
                + from_west * west
                + from_east * east
                + from_south * south
                + from_north * north
                + (mix + (down if level == 0 else up)) * other
            )
            if level == 0:
                new = new + uplift * share_ref[bin_at : bin_at + ROWS, :]
            later_ref[t, at : at + ROWS, :] = jnp.where(active, new, 0.0)
        return carry

    lax.fori_loop(0, per_home, one, 0)
    pack_borders((e_ref, w_ref, n_ref, s_ref), lambda t: later_ref[t], tiles_x, tiles_y)


def send_seen_kernel(
    owner_ref, later_ref, fw_ref, fe_ref, fs_ref, fn_ref, seen_ref, send_ref, ext, both, sems, *, tiles_x, tiles_y
):
    per_home = tiles_x * tiles_y
    rows = later_ref.shape[1]
    wide = tiles_y + 2
    fill_halo(ext, (fw_ref, fe_ref, fs_ref, fn_ref), tiles_x, tiles_y)

    def place_of(t):
        return (t // tiles_y + 1) * wide + t % tiles_y + 1

    def inner(t, carry):
        ext[place_of(t)] = later_ref[t]
        return carry

    lax.fori_loop(0, per_home, inner, 0)

    def one(t, carry):
        both[t, :rows, :] = seen_ref[t]
        both[t, rows:, :] = seen_by(ext, place_of(t), wide)
        owner = owner_ref[t]

        @pl.when(owner >= 0)
        def _():
            pltpu.make_async_copy(both.at[t], send_ref.at[owner], sems.at[t]).start()

        return carry

    lax.fori_loop(0, per_home, one, 0)

    def wait(t, carry):
        owner = owner_ref[t]

        @pl.when(owner >= 0)
        def _():
            pltpu.make_async_copy(both.at[t], send_ref.at[owner], sems.at[t]).wait()

        return carry

    lax.fori_loop(0, per_home, wait, 0)


def shifted(value, axis, steps):
    count = lax.axis_size(axis)
    return lax.ppermute(value, axis, [(source, (source + steps) % count) for source in range(count)])


def exchange_borders(borders):
    east, west, north, south = borders
    return shifted(east, "gx", 1), shifted(west, "gx", -1), shifted(north, "gy", 1), shifted(south, "gy", -1)


def ring_call(kernel, tiles_x, tiles_y, rows, outs, scratch, name, hbm_out=False):
    smem = pl.BlockSpec(memory_space=pltpu.SMEM)
    vmem = pl.BlockSpec(memory_space=pltpu.VMEM)
    size = tiles_x * tiles_y * rows * LANES

    def call(owner_of_tile, *inputs):
        return pl.pallas_call(
            functools.partial(kernel, tiles_x=tiles_x, tiles_y=tiles_y),
            in_specs=[smem] + [vmem] * len(inputs),
            out_specs=pl.BlockSpec(memory_space=pltpu.HBM) if hbm_out else [vmem] * len(outs),
            out_shape=outs[0] if hbm_out else outs,
            scratch_shapes=scratch,
            compiler_params=pltpu.CompilerParams(vmem_limit_bytes=32 << 20),
            cost_estimate=pl.CostEstimate(flops=16 * size, bytes_accessed=16 * size, transcendentals=0),
            name=name,
        )(owner_of_tile, *inputs)

    return call


def border_shapes(tiles_x, tiles_y, rows):
    return [f32(tiles_y // 4, rows, LANES)] * 2 + [f32(tiles_x // 4, rows, LANES)] * 2


def gather_rings(owner_of_tile, received, tiles_x, tiles_y):
    both_rows = received.shape[1]
    rows = both_rows // 2
    outs = [f32(tiles_x * tiles_y, both_rows, LANES)] + border_shapes(tiles_x, tiles_y, rows)
    return ring_call(gather_rings_kernel, tiles_x, tiles_y, rows, outs, [], "gather_rings")(owner_of_tile, received)


def relay_rings(owner_of_tile, rings, borders, wind_ring, settle_speed, bin_share, tiles_x, tiles_y, owners):
    per_home, both_rows, _ = rings.shape
    rows = both_rows // 2
    ext = pltpu.VMEM(((tiles_x + 2) * (tiles_y + 2), rows, LANES), jnp.float32)
    settle_rows = jnp.broadcast_to(settle_speed[:, None], settle_speed.shape + (LANES,))
    share_rows = jnp.broadcast_to(bin_share[:, None], bin_share.shape + (LANES,))
    outs = [f32(per_home, rows, LANES)] * 2 + border_shapes(tiles_x, tiles_y, rows)
    advance = ring_call(advance_rings_kernel, tiles_x, tiles_y, rows, outs, [ext], "advance_rings")
    seen, later, *borders = advance(owner_of_tile, rings, *borders, wind_ring, settle_rows, share_rows)
    outs = [pltpu.HBM((owners, both_rows, LANES), jnp.float32)]
    scratch = [ext, pltpu.VMEM((per_home, both_rows, LANES), jnp.float32), pltpu.SemaphoreType.DMA((per_home,))]
    send = ring_call(send_seen_kernel, tiles_x, tiles_y, rows, outs, scratch, "send_seen", hbm_out=True)
    return send(owner_of_tile, later, *exchange_borders(borders), seen)


def dust_kernel(home_ref, share_ref, settle_ref, dust_ref, shift_ref, wind_ref, *refs, block, bins, outer):
    if outer:
        side_ref, seen_ref, out_ref, coef, sides, edges, *work = refs
    else:
        out_ref, kept_ref, coef, *work = refs
    lanes = len(work) // 2
    step = pl.program_id(0)
    each = TZ * bins
    if outer:
        for j in range(block):
            edges[j] = seen_ref[home_ref[step * block + j]]
        spread = jnp.dot(
            jnp.concatenate(halves_of(edges[...].reshape(block * 2 * each, LANES)), axis=1),
            side_ref[...],
            preferred_element_type=jnp.float32,
        )
        for r in range(ROWS):
            sides[r] = spread[:, r * LANES : (r + 1) * LANES]

    _, lane = iotas()
    within = lane % TILE
    first_y, last_y = within == 0, within == TILE - 1
    low_lanes, high_lanes = lane < TILE, lane >= LANES - TILE
    mix = dust_step * diffusion
    chunks = bins // ROWS
    settle = [dust_step * settle_ref[h * ROWS : (h + 1) * ROWS, :] for h in range(chunks)]
    share = [share_ref[h * ROWS : (h + 1) * ROWS, :] for h in range(chunks)]

    def prepare(k, j):
        held = work[2 * k]
        home = home_ref[step * block + j]
        if not outer:
            kept_ref[j] = wind_ref[home]
        wind_at = j if outer else home
        plane = [wind_ref[wind_at, p * ROWS : (p + 1) * ROWS, :] * dust_step for p in range(PLANES)]
        for level in range(TZ):
            u, v = plane[level], plane[TZ + level]
            south_by = mix + jnp.maximum(v, 0.0)
            north_by = mix + jnp.maximum(-v, 0.0)
            coef[k, 0, level] = mix + jnp.maximum(u, 0.0)
            coef[k, 1, level] = mix + jnp.maximum(-u, 0.0)
            coef[k, 4, level] = 1.0 - 6.0 * mix - jnp.abs(u) - jnp.abs(v)
            coef[k, 5, level] = plane[2 * TZ + level]
            if outer:
                coef[k, 2, level] = south_by
                coef[k, 3, level] = north_by
                coef[k, 7, level] = jnp.where(first_y, south_by, jnp.where(last_y, north_by, 0.0))
            else:
                coef[k, 2, level] = jnp.where(first_y, 0.0, south_by)
                coef[k, 3, level] = jnp.where(last_y, 0.0, north_by)
        coef[k, 6, 0] = plane[PLANES - 1]
        for r in range(ROWS):
            for level in range(TZ):
                at = (r * TZ + level) * bins
                cells = dust_ref[j, pl.ds(r * TZ + level, bins, stride=ROWS * TZ), :]
                if not outer:
                    held[at : at + bins, :] = cells
                    continue
                for h in range(chunks):
                    edge_at = level * bins + h * ROWS
                    q = cells[h * ROWS : (h + 1) * ROWS]
                    q = q + spread_rows(coef[k, 7, level, r : r + 1, :]) * sides[r, pl.ds(j * 2 * each + edge_at, ROWS), :]
                    if r == 0 or r == ROWS - 1:
                        edge = edges[j, edge_at : edge_at + ROWS, :]
                        here = low_lanes if r == 0 else high_lanes
                        by = spread_rows(coef[k, 0 if r == 0 else 1, level, r : r + 1, :])
                        q = q + jnp.where(here, by * edge, 0.0)
                    held[at + h * ROWS : at + (h + 1) * ROWS, :] = q

    def shift(k):
        held, shifts = work[2 * k], work[2 * k + 1]
        shifts[...] = jnp.dot(
            jnp.concatenate(halves_of(held[...]), axis=1), shift_ref[...], preferred_element_type=jnp.float32
        )

    def update(k, j):
        held, shifts = work[2 * k], work[2 * k + 1]
        nothing = jnp.zeros((ROWS, LANES), jnp.float32)
        for r in range(ROWS):
            for h in range(chunks):
                cells = [held[(r * TZ + level) * bins + h * ROWS :][:ROWS] for level in range(TZ)]
                for level in range(TZ):
                    at = (r * TZ + level) * bins + h * ROWS
                    edge_at = each + level * bins + h * ROWS

                    def moved(which, rows_up=0):
                        first = at + rows_up * TZ * bins
                        return shifts[first : first + ROWS, which * LANES : (which + 1) * LANES]

                    def by(which):
                        return spread_rows(coef[k, which, level, r : r + 1, :])

                    edge = edges[j, edge_at : edge_at + ROWS, :] if outer else nothing
                    before = edge if r == 0 else moved(2, -1)
                    after = edge if r == ROWS - 1 else moved(3, 1)
                    south, north = moved(0), moved(1)
                    if outer:
                        side = sides[r, pl.ds(j * 2 * each + edge_at, ROWS), :]
                        south = jnp.where(first_y, side, south)
                        north = jnp.where(last_y, side, north)
                    west = jnp.where(low_lanes, before, moved(2))
                    east = jnp.where(high_lanes, after, moved(3))
                    rise = by(5) - settle[h]
                    up = jnp.maximum(rise, 0.0)
                    mixed = mix + (up - rise if level == 0 else up)
                    value = (
                        (by(4) - jnp.abs(rise)) * cells[level]
                        + by(0) * west
                        + by(1) * east
                        + by(2) * south
                        + by(3) * north
                        + mixed * cells[1 - level]
                    )
                    if level == 0:
                        value = value + spread_rows(coef[k, 6, 0, r : r + 1, :]) * share[h]
                    first = h * ROWS * ROWS * TZ + r * TZ + level
                    out_ref[j, pl.ds(first, ROWS, stride=ROWS * TZ), :] = value

    def some(i, carry):
        for k in range(lanes):
            prepare(k, i * lanes + k)
        for k in range(lanes):
            shift(k)
        for k in range(lanes):
            update(k, i * lanes + k)
        return carry

    lax.fori_loop(0, block // lanes, some, 0)


def dust_substep(home_of_slot, dust, wind, settle_speed, bin_share, seen_recv=None):
    slots, cells = dust.shape[:2]
    bins = settle_speed.shape[0]
    block = 8 if slots % 8 == 0 else 4
    lanes = 2
    outer = seen_recv is not None
    smem = pl.BlockSpec(memory_space=pltpu.SMEM)
    vmem = pl.BlockSpec(memory_space=pltpu.VMEM)
    tile = pl.BlockSpec((block, cells, LANES), lambda i: (i, 0, 0))
    settle = jnp.broadcast_to(settle_speed[:, None], (bins, LANES))
    share = jnp.broadcast_to(bin_share[:, None], (bins, LANES))
    wind_rows = pl.BlockSpec((block,) + wind.shape[1:], lambda i: (i, 0, 0))
    inputs = [home_of_slot, share, settle, in_hbm(dust), jnp.asarray(shift_matrix()), in_hbm(wind) if outer else wind]
    scratch = [pltpu.VMEM((lanes, PLANES + 1, TZ, ROWS, LANES), jnp.float32)]
    if outer:
        inputs += [jnp.asarray(side_matrix()), seen_recv]
        scratch += [
            pltpu.VMEM((ROWS, block * seen_recv.shape[1], LANES), jnp.float32),
            pltpu.VMEM((block,) + seen_recv.shape[1:], jnp.float32),
        ]
    out_shape = f32(*dust.shape)
    if not outer:
        out_shape = [pltpu.HBM(dust.shape, jnp.float32), pltpu.HBM((slots,) + wind.shape[1:], jnp.float32)]
    scratch += [pltpu.VMEM((cells, LANES), jnp.float32), pltpu.VMEM((cells, 4 * LANES), jnp.float32)] * lanes
    return pl.pallas_call(
        functools.partial(dust_kernel, block=block, bins=bins, outer=outer),
        grid=(slots // block,),
        in_specs=[smem, vmem, vmem, tile, vmem, wind_rows if outer else vmem] + [vmem] * (len(inputs) - 6),
        out_specs=tile if outer else [tile, wind_rows],
        out_shape=out_shape,
        scratch_shapes=scratch,
        compiler_params=pltpu.CompilerParams(vmem_limit_bytes=32 << 20),
        cost_estimate=pl.CostEstimate(flops=60 * dust.size, bytes_accessed=dust.size * 12, transcendentals=0),
        name="dust_outer" if outer else "dust_inner",
    )(*inputs)


def relay_rows(rows):
    return lax.all_to_all(rows, AXES, split_axis=0, concat_axis=0, tiled=True)


def per_device(velocity, threshold, dust_mass, settle_speed, bin_share, active_tiles, tile_owner):
    owners = lax.axis_size(AXES)
    grid_cols = lax.axis_size("gy")
    self_index = lax.axis_index(AXES)
    slots, bins = dust_mass.shape[:2]
    tiles_x = velocity.shape[2] // TILE
    tiles_y = velocity.shape[3] // TILE
    per_home = tiles_x * tiles_y
    tiles_across = tiles_y * grid_cols

    tile_x = active_tiles // tiles_across
    tile_y = active_tiles % tiles_across
    home_dev = tile_x // tiles_x * grid_cols + tile_y // tiles_y
    local_tile = tile_x % tiles_x * tiles_y + tile_y % tiles_y
    own_slot = tile_owner - self_index * slots
    mine = jnp.where(home_dev == self_index, local_tile, -1)
    slot_ids = jnp.arange(slots, dtype=jnp.int32)
    home_of_slot = jnp.sum(jnp.where(own_slot[None, :] == slot_ids[:, None], home_dev[None, :], 0), axis=1)
    tile_ids = jnp.arange(per_home, dtype=jnp.int32)
    owner_of_tile = jnp.max(
        jnp.where(mine[None, :] == tile_ids[:, None], (tile_owner // slots)[None, :], -1), axis=1
    )

    dust = dust_mass.reshape(slots, bins, TZ, ROWS, LANES).transpose(0, 1, 3, 2, 4)
    dust = dust.reshape(slots, bins * ROWS * TZ, LANES)

    xlo = shifted(velocity[:, :, -1, :], "gx", 1)
    xhi = shifted(velocity[:, :, 0, :], "gx", -1)
    ylo = shifted(velocity[:, :, :, -1], "gy", 1)
    yhi = shifted(velocity[:, :, :, 0], "gy", -1)

    strips_send = dust_strips(home_of_slot, dust, bins, owners)
    strips_send, xlo, xhi, ylo, yhi = lax.optimization_barrier((strips_send, xlo, xhi, ylo, yhi))
    strips = relay_rows(strips_send)
    new_velocity, wind_send, wind_ring = wind_step(
        owner_of_tile, velocity, xlo, xhi, ylo, yhi, threshold, owners
    )
    strips, wind_send, wind_ring = lax.optimization_barrier((strips, wind_send, wind_ring))
    rings, *borders = gather_rings(owner_of_tile, strips, tiles_x, tiles_y)
    borders = exchange_borders(borders)
    wind_send, *borders = lax.optimization_barrier((wind_send, *borders))
    wind_recv = relay_rows(wind_send)
    seen_send = relay_rings(
        owner_of_tile, rings, borders, wind_ring, settle_speed, bin_share, tiles_x, tiles_y, owners
    )
    seen_recv = relay_rows(seen_send)
    inner, wind_held = dust_substep(home_of_slot, dust, wind_recv, settle_speed, bin_share)
    out = dust_substep(home_of_slot, inner, wind_held, settle_speed, bin_share, seen_recv)
    out = out.reshape(slots, bins, ROWS, TZ, LANES).transpose(0, 1, 3, 2, 4).reshape(dust_mass.shape)
    return new_velocity, out


def solution(mesh):
    in_specs = (
        P(None, None, "gx", "gy"),
        P("gx", "gy"),
        P(AXES, None, None, None),
        P(),
        P(),
        P(),
        P(),
    )
    out_specs = (P(None, None, "gx", "gy"), P(AXES, None, None, None))
    return jax.shard_map(
        per_device, mesh=mesh, in_specs=in_specs, out_specs=out_specs, check_vma=False
    )
```

```python
import functools

import jax
import jax.numpy as jnp
import ml_dtypes
import numpy as np
from jax import lax
from jax.experimental import pallas as pl
from jax.experimental.pallas import tpu as pltpu
from jax.sharding import PartitionSpec as P

TZ = 2
TILE = 32
LANES = 128
ROWS = TILE * TILE // LANES
PLANES = 7
AXES = ("gx", "gy")

time_step = 0.1
viscosity = 0.2
dust_step = 0.1
diffusion = 0.1
roughness = 0.5
emit_rate = 0.5

WEST, SOUTH, NORTH, EAST = range(4)


def iotas(shape=(ROWS, LANES)):
    return lax.broadcasted_iota(jnp.int32, shape, 0), lax.broadcasted_iota(jnp.int32, shape, 1)


def lane_gather(x, index):
    return jnp.take_along_axis(x, index, axis=1)


def ring_pattern(depth):
    row, lane = iotas()
    group, within = lane // TILE, lane % TILE
    side = jnp.where(group == SOUTH, depth, TILE - 1 - depth)
    index = (within % 4) * TILE + side
    index = jnp.where(group == WEST, depth * TILE + within, index)
    index = jnp.where(group == EAST, (3 - depth) * TILE + within, index)
    source = jnp.where(group == WEST, 0, jnp.where(group == EAST, ROWS - 1, within // 4))
    return index, row == source


def ring_of(x, pattern):
    index, taken = pattern
    return jnp.sum(jnp.where(taken, lane_gather(x, index), 0.0), axis=0, keepdims=True)


def spread_rows(row):
    return jnp.broadcast_to(row, (ROWS, LANES))


def f32(*shape):
    return jax.ShapeDtypeStruct(shape, jnp.float32)


def in_hbm(x):
    return pltpu.with_memory_space_constraint(x, pltpu.HBM)


def halves_of(x):
    high = x.astype(jnp.bfloat16)
    return high, (x - high.astype(jnp.float32)).astype(jnp.bfloat16)


def moves(sources):
    lanes = np.arange(LANES)[:, None]
    once = (lanes == np.asarray(sources)[None, :]).astype(ml_dtypes.bfloat16)
    return np.concatenate([once, once], axis=0)


def ring_matrix():
    lane = np.arange(LANES)
    group, within = lane // TILE, lane % TILE
    blocks = []
    for r in range(ROWS):
        columns = []
        for depth in range(2):
            side = np.where(group == SOUTH, depth, TILE - 1 - depth)
            source = np.where(within // 4 == r, (within % 4) * TILE + side, -1)
            source = np.where(group == WEST, depth * TILE + within if r == 0 else -1, source)
            source = np.where(group == EAST, (3 - depth) * TILE + within if r == ROWS - 1 else -1, source)
            columns.append(source)
        blocks.append(moves(np.concatenate(columns)))
    return np.concatenate(blocks, axis=0)


def shift_matrix():
    lane = np.arange(LANES)
    return moves(np.concatenate([(lane + d) % LANES for d in (-1, 1, -TILE, TILE)]))


def side_matrix():
    lane = np.arange(LANES)
    columns = []
    for r in range(ROWS):
        along = 4 * r + lane // TILE
        source = np.where(lane % TILE == 0, SOUTH * TILE + along, -1)
        columns.append(np.where(lane % TILE == TILE - 1, NORTH * TILE + along, source))
    return moves(np.concatenate(columns))


def strips_kernel(home_ref, dust_hbm, matrix_ref, send_ref, dust, rings, load_sems, sems, *, block, bins):
    slots = rings.shape[0]
    each = TZ * bins

    def load(i):
        some = pl.ds(i * block, block)
        return pltpu.make_async_copy(dust_hbm.at[some], dust.at[some], load_sems.at[i])

    def send(s):
        return pltpu.make_async_copy(rings.at[s], send_ref.at[home_ref[s]], sems.at[s])

    for i in range(slots // block):
        load(i).start()

    def one(i, carry):
        load(i).wait()
        parts = []
        for r in range(ROWS):
            x = jnp.concatenate(
                [
                    dust[i * block + j, pl.ds(r * TZ + level, bins, stride=ROWS * TZ), :]
                    for j in range(block)
                    for level in range(TZ)
                ],
                axis=0,
            )
            parts += halves_of(x)
        found = jnp.dot(
            jnp.concatenate(parts, axis=1), matrix_ref[...], preferred_element_type=jnp.float32
        )
        for j in range(block):
            for depth in range(2):
                rings[i * block + j, depth * each : (depth + 1) * each, :] = found[
                    j * each : (j + 1) * each, depth * LANES : (depth + 1) * LANES
                ]
            send(i * block + j).start()
        return carry

    lax.fori_loop(0, slots // block, one, 0)

    def wait(s, carry):
        send(s).wait()
        return carry

    lax.fori_loop(0, slots, wait, 0)


def dust_strips(home_of_slot, dust, bins, owners):
    slots, cells = dust.shape[:2]
    block = 8 if slots % 8 == 0 else 4
    rows = 2 * bins * TZ
    matrix = jnp.asarray(ring_matrix())
    hbm = pl.BlockSpec(memory_space=pltpu.HBM)
    return pl.pallas_call(
        functools.partial(strips_kernel, block=block, bins=bins),
        in_specs=[pl.BlockSpec(memory_space=pltpu.SMEM), hbm, pl.BlockSpec(memory_space=pltpu.VMEM)],
        out_specs=hbm,
        out_shape=pltpu.HBM((owners, rows, LANES), jnp.float32),
        scratch_shapes=[
            pltpu.VMEM(dust.shape, jnp.float32),
            pltpu.VMEM((slots, rows, LANES), jnp.float32),
            pltpu.SemaphoreType.DMA((slots // block,)),
            pltpu.SemaphoreType.DMA((slots,)),
        ],
        compiler_params=pltpu.CompilerParams(vmem_limit_bytes=32 << 20),
        cost_estimate=pl.CostEstimate(
            flops=20 * dust.size, bytes_accessed=dust.size * 4 + slots * rows * LANES * 4, transcendentals=0
        ),
        name="dust_strips",
    )(home_of_slot, in_hbm(dust), matrix)


def faces_kernel(vel_ref, x_last_ref, x_first_ref, y_last_ref, y_first_ref, first, last, low, high, x_sems, y_sems):
    fields, nx, ny = vel_ref.shape
    x_copies = [
        pltpu.make_async_copy(vel_ref.at[:, pl.ds(0, ROWS), :], first, x_sems.at[0]),
        pltpu.make_async_copy(vel_ref.at[:, pl.ds(nx - ROWS, ROWS), :], last, x_sems.at[1]),
    ]
    y_copies = [
        (
            pltpu.make_async_copy(vel_ref.at[f, :, pl.ds(0, LANES)], low.at[f], y_sems.at[0, f]),
            pltpu.make_async_copy(vel_ref.at[f, :, pl.ds(ny - LANES, LANES)], high.at[f], y_sems.at[1, f]),
        )
        for f in range(fields)
    ]
    for pair in y_copies:
        for copy in pair:
            copy.start()
    for copy in x_copies:
        copy.start()
    lane = lax.broadcasted_iota(jnp.int32, (nx, LANES), 1)
    for f, (low_copy, high_copy) in enumerate(y_copies):
        low_copy.wait()
        high_copy.wait()
        from_low = pltpu.roll(low[f], f, 1) if f else low[f]
        from_high = pltpu.roll(high[f], f + 1, 1)
        if f == 0:
            y_first_ref[...], y_last_ref[...] = from_low, from_high
        else:
            y_first_ref[...] = jnp.where(lane == f, from_low, y_first_ref[...])
            y_last_ref[...] = jnp.where(lane == f, from_high, y_last_ref[...])
    for copy in x_copies:
        copy.wait()
    for f in range(fields):
        x_first_ref[f : f + 1, :] = first[f, 0:1, :]
        x_last_ref[f : f + 1, :] = last[f, ROWS - 1 : ROWS, :]


def wind_faces(velocity):
    comps, levels, nx, ny = velocity.shape
    fields = comps * levels
    vmem = pl.BlockSpec(memory_space=pltpu.VMEM)
    return pl.pallas_call(
        faces_kernel,
        in_specs=[pl.BlockSpec(memory_space=pltpu.HBM)],
        out_specs=[vmem] * 4,
        out_shape=[f32(fields, ny)] * 2 + [f32(nx, LANES)] * 2,
        scratch_shapes=[
            pltpu.VMEM((fields, ROWS, ny), jnp.float32),
            pltpu.VMEM((fields, ROWS, ny), jnp.float32),
            pltpu.VMEM((fields, nx, LANES), jnp.float32),
            pltpu.VMEM((fields, nx, LANES), jnp.float32),
            pltpu.SemaphoreType.DMA((2,)),
            pltpu.SemaphoreType.DMA((2, fields)),
        ],
        compiler_params=pltpu.CompilerParams(vmem_limit_bytes=32 << 20),
        cost_estimate=pl.CostEstimate(flops=velocity.size, bytes_accessed=velocity.size * 4, transcendentals=0),
        name="wind_faces",
    )(in_hbm(velocity.reshape(fields, nx, ny)))


def wind_kernel(
    owner_ref, vel_ref, xlo_ref, xhi_ref, ylo_ref, yhi_ref, thr_ref,
    new_ref, send_ref, ring_ref, padded, strip, tiles, load_sem, sems, *, levels
):
    fields, nx, ny = new_ref.shape
    load = pltpu.make_async_copy(vel_ref, padded.at[:, pl.ds(8, nx), :], load_sem)
    load.start()
    load.wait()
    for f in range(fields):
        padded[f, 7:8, :] = xlo_ref[f : f + 1, :]
        padded[f, 8 + nx : 9 + nx, :] = xhi_ref[f : f + 1, :]
    half = 16
    halves = ny // LANES
    tiles_y = ny // TILE
    pattern = ring_pattern(0)
    _, lane8 = iotas()
    group = lane8 // TILE

    def one_strip(ix, carry):
        for sub in range(TILE // half):
            base = pl.multiple_of(ix * TILE + sub * half, 8)
            lane = lax.broadcasted_iota(jnp.int32, (half, ny), 1)
            low = {}
            faces = [ref[pl.ds(base, half), :] for ref in (ylo_ref, yhi_ref)]

            def face(which, f, to):
                moved = pltpu.roll(faces[which], (to - f) % LANES, 1) if f != to else faces[which]
                return jnp.concatenate([moved] * halves, axis=1)

            for z in range(levels):
                u, v, w = (padded[c * levels + z, pl.ds(base + 8, half), :] for c in range(3))
                for c in range(3):
                    f = c * levels + z
                    block = padded[f, pl.ds(base, half + 16), :]
                    centre = (u, v, w)[c]
                    west = pltpu.roll(block, 1, 0)[8 : 8 + half]
                    east = pltpu.roll(block, half + 15, 0)[8 : 8 + half]
                    south = jnp.where(lane == 0, face(0, f, 0), pltpu.roll(centre, 1, 1))
                    north = jnp.where(lane == ny - 1, face(1, f, LANES - 1), pltpu.roll(centre, ny - 1, 1))
                    lower = -centre if z == 0 else padded[f - 1, pl.ds(base + 8, half), :]
                    upper = centre if z == levels - 1 else padded[f + 1, pl.ds(base + 8, half), :]
                    carried = 0.5 * (u * (east - west) + v * (north - south) + w * (upper - lower))
                    spread = east + west + north + south + upper + lower - 6.0 * centre
                    new = centre + time_step * (viscosity * spread - carried)
                    new_ref[f, pl.ds(base, half), :] = new
                    if z < TZ:
                        low[c * TZ + z] = new
            stress = roughness * (low[0] * low[0] + low[TZ] * low[TZ])
            low[PLANES - 1] = emit_rate * stress * jnp.maximum(
                stress - thr_ref[pl.ds(base, half), :], 0.0
            )
            for p in range(PLANES):
                for h in range(halves):
                    strip[p * halves + h, sub * half : (sub + 1) * half, :] = low[p][
                        :, h * LANES : (h + 1) * LANES
                    ]
        for p in range(PLANES):
            for h in range(halves):
                parts = [strip[p * halves + h, pl.ds(k, ROWS, stride=4), :] for k in range(4)]
                for t in range(4):
                    tile = ix * tiles_y + h * 4 + t
                    cells = pltpu.roll(parts[0], (-t * TILE) % LANES, 1) if t else parts[0]
                    for k in range(1, 4):
                        moved = pltpu.roll(parts[k], ((k - t) * TILE) % LANES, 1) if k != t else parts[k]
                        cells = jnp.where(group == k, moved, cells)
                    tiles[tile, p * ROWS : (p + 1) * ROWS, :] = cells
                    ring_ref[tile, p : p + 1, :] = ring_of(cells, pattern)

        def send(t, inner):
            tile = ix * tiles_y + t
            owner = owner_ref[tile]

            @pl.when(owner >= 0)
            def _():
                pltpu.make_async_copy(tiles.at[tile], send_ref.at[owner], sems.at[tile]).start()

            return inner

        lax.fori_loop(0, tiles_y, send, 0)
        return carry

    lax.fori_loop(0, nx // TILE, one_strip, 0)

    def wait(tile, carry):
        owner = owner_ref[tile]

        @pl.when(owner >= 0)
        def _():
            pltpu.make_async_copy(tiles.at[tile], send_ref.at[owner], sems.at[tile]).wait()

        return carry

    lax.fori_loop(0, tiles.shape[0], wait, 0)


def wind_step(owner_of_tile, velocity, xlo, xhi, ylo, yhi, threshold, owners):
    comps, levels, nx, ny = velocity.shape
    fields = comps * levels
    per_home = (nx // TILE) * (ny // TILE)
    smem = pl.BlockSpec(memory_space=pltpu.SMEM)
    hbm = pl.BlockSpec(memory_space=pltpu.HBM)
    vmem = pl.BlockSpec(memory_space=pltpu.VMEM)
    new, send, ring = pl.pallas_call(
        functools.partial(wind_kernel, levels=levels),
        in_specs=[smem, hbm, vmem, vmem, vmem, vmem, vmem],
        out_specs=[vmem, hbm, vmem],
        out_shape=[
            f32(fields, nx, ny),
            pltpu.HBM((owners, PLANES * ROWS, LANES), jnp.float32),
            f32(per_home, 8, LANES),
        ],
        scratch_shapes=[
            pltpu.VMEM((fields, nx + 16, ny), jnp.float32),
            pltpu.VMEM((PLANES * (ny // LANES), TILE, LANES), jnp.float32),
            pltpu.VMEM((per_home, PLANES * ROWS, LANES), jnp.float32),
            pltpu.SemaphoreType.DMA,
            pltpu.SemaphoreType.DMA((per_home,)),
        ],
        compiler_params=pltpu.CompilerParams(vmem_limit_bytes=40 << 20),
        cost_estimate=pl.CostEstimate(
            flops=40 * velocity.size, bytes_accessed=velocity.size * 10, transcendentals=0
        ),
        name="wind_step",
    )(
        owner_of_tile,
        in_hbm(velocity.reshape(fields, nx, ny)),
        xlo,
        xhi,
        ylo,
        yhi,
        threshold,
    )
    return new.reshape(velocity.shape), send, ring


def pack_borders(outs, ring_at, tiles_x, tiles_y):
    rows = outs[0].shape[1]
    lane = lax.broadcasted_iota(jnp.int32, (rows, LANES), 1)
    borders = (
        (EAST, [((tiles_x - 1) * tiles_y + n) for n in range(tiles_y)]),
        (WEST, [n for n in range(tiles_y)]),
        (NORTH, [n * tiles_y + tiles_y - 1 for n in range(tiles_x)]),
        (SOUTH, [n * tiles_y for n in range(tiles_x)]),
    )
    for out, (side, tiles) in zip(outs, borders):
        for g in range(len(tiles) // 4):
            packed = None
            for q in range(4):
                strip = ring_at(tiles[4 * g + q])
                if q != side:
                    strip = pltpu.roll(strip, ((q - side) * TILE) % LANES, 1)
                packed = strip if packed is None else jnp.where(lane // TILE == q, strip, packed)
            out[g] = packed


def fill_halo(ext, borders, tiles_x, tiles_y):
    from_west, from_east, from_south, from_north = borders
    wide = tiles_y + 2
    for ref, side, places in (
        (from_west, EAST, [n + 1 for n in range(tiles_y)]),
        (from_east, WEST, [(tiles_x + 1) * wide + n + 1 for n in range(tiles_y)]),
        (from_south, NORTH, [(n + 1) * wide for n in range(tiles_x)]),
        (from_north, SOUTH, [(n + 1) * wide + tiles_y + 1 for n in range(tiles_x)]),
    ):
        for n, place in enumerate(places):
            strip = ref[n // 4]
            if n % 4 != side:
                strip = pltpu.roll(strip, ((side - n % 4) * TILE) % LANES, 1)
            ext[place] = strip


def seen_by(ext, place, wide):
    west, east = ext[place - wide], ext[place + wide]
    south, north = ext[place - 1], ext[place + 1]
    lane = lax.broadcasted_iota(jnp.int32, west.shape, 1)
    up = pltpu.roll(jnp.where(lane < 2 * TILE, north, west), TILE, 1)
    down = pltpu.roll(jnp.where(lane < 2 * TILE, east, south), LANES - TILE, 1)
    return jnp.where((lane // TILE) % 2 == 0, up, down)


def border_tiles(tiles_x, tiles_y):
    return (
        [(tiles_x - 1) * tiles_y + n for n in range(tiles_y)],
        [n for n in range(tiles_y)],
        [n * tiles_y + tiles_y - 1 for n in range(tiles_x)],
        [n * tiles_y for n in range(tiles_x)],
    )


def pack_borders_kernel(owner_ref, recv_ref, e_ref, w_ref, n_ref, s_ref, strips, sems, *, tiles_x, tiles_y):
    rows = e_ref.shape[1]
    used = sorted(set(sum(border_tiles(tiles_x, tiles_y), [])))

    def copy(t):
        return pltpu.make_async_copy(recv_ref.at[owner_ref[t], pl.ds(0, rows), :], strips.at[t], sems.at[t])

    for t in used:

        @pl.when(owner_ref[t] >= 0)
        def _():
            copy(t).start()

        @pl.when(owner_ref[t] < 0)
        def _():
            strips[t] = jnp.zeros(strips.shape[1:], jnp.float32)

    for t in used:

        @pl.when(owner_ref[t] >= 0)
        def _():
            copy(t).wait()

    pack_borders((e_ref, w_ref, n_ref, s_ref), lambda t: strips[t], tiles_x, tiles_y)


def gather_rings_kernel(owner_ref, recv_ref, rings_ref, *, tiles_x, tiles_y):
    def one(t, carry):
        owner = owner_ref[t]
        rings = recv_ref[jnp.maximum(owner, 0)]
        rings_ref[t] = jnp.where(owner >= 0, rings, 0.0)
        return carry

    lax.fori_loop(0, tiles_x * tiles_y, one, 0)


def fill_tiles(ext, tile, tiles_x, tiles_y):
    def inner(t, carry):
        ext[place_of(t, tiles_y)] = tile(t)
        return carry

    lax.fori_loop(0, tiles_x * tiles_y, inner, 0)


def place_of(t, tiles_y):
    return (t // tiles_y + 1) * (tiles_y + 2) + t % tiles_y + 1


def advance_ring(t, owner_ref, rings_ref, wind_ref, settle_ref, share_ref, seen):
    _, lane = iotas()
    group, within = lane // TILE, lane % TILE
    on_x = (group == WEST) | (group == EAST)
    first, last = within == 0, within == TILE - 1
    high = jnp.where((group == EAST) | (group == NORTH), TILE - 1, 0)
    corner = jnp.where(
        on_x,
        jnp.where(first, SOUTH, NORTH) * TILE + high,
        jnp.where(first, WEST, EAST) * TILE + high,
    )
    rows = rings_ref.shape[1] // 2
    bins = rows // TZ
    uplift = dust_step * spread_rows(wind_ref[t, PLANES - 1 : PLANES, :])
    mix = dust_step * diffusion
    active = owner_ref[t] >= 0
    chunks = []
    for at in range(0, rows, ROWS):
        level, bin_at = at // bins, at % bins
        if bin_at == 0:
            u, v, w = (
                dust_step * spread_rows(wind_ref[t, c * TZ + level : c * TZ + level + 1, :]) for c in range(3)
            )
            from_west = mix + jnp.maximum(u, 0.0)
            from_east = mix + jnp.maximum(-u, 0.0)
            from_south = mix + jnp.maximum(v, 0.0)
            from_north = mix + jnp.maximum(-v, 0.0)
            keep = 1.0 - 6.0 * mix - jnp.abs(u) - jnp.abs(v)
        q = rings_ref[t, at : at + ROWS, :]
        deep = rings_ref[t, rows + at : rows + at + ROWS, :]
        out = seen[at : at + ROWS, :]
        beyond = lane_gather(out, corner)
        before = jnp.where(first, beyond, pltpu.roll(q, 1, 1))
        after = jnp.where(last, beyond, pltpu.roll(q, LANES - 1, 1))
        west = jnp.where(group == WEST, out, jnp.where(group == EAST, deep, before))
        east = jnp.where(group == WEST, deep, jnp.where(group == EAST, out, after))
        south = jnp.where(on_x, before, jnp.where(group == SOUTH, out, deep))
        north = jnp.where(on_x, after, jnp.where(group == SOUTH, deep, out))
        other_at = (1 - level) * bins + bin_at
        other = rings_ref[t, other_at : other_at + ROWS, :]
        rise = w - dust_step * settle_ref[bin_at : bin_at + ROWS, :]
        up = jnp.maximum(rise, 0.0)
        down = up - rise
        new = (
            (keep - up - down) * q
            + from_west * west
            + from_east * east
            + from_south * south
            + from_north * north
            + (mix + (down if level == 0 else up)) * other
        )
        if level == 0:
            new = new + uplift * share_ref[bin_at : bin_at + ROWS, :]
        chunks.append(jnp.where(active, new, 0.0))
    return chunks


def advance_borders_kernel(
    owner_ref, rings_ref, fw_ref, fe_ref, fs_ref, fn_ref, wind_ref, settle_ref, share_ref,
    seen_ref, later_ref, e_ref, w_ref, n_ref, s_ref, ext, *, tiles_x, tiles_y
):
    rows = e_ref.shape[1]
    fill_halo(ext, (fw_ref, fe_ref, fs_ref, fn_ref), tiles_x, tiles_y)
    fill_tiles(ext, lambda t: rings_ref[t, :rows, :], tiles_x, tiles_y)

    def pair(tiles):
        for t in tiles:
            seen = seen_by(ext, place_of(t, tiles_y), tiles_y + 2)
            seen_ref[t] = seen
            chunks = advance_ring(t, owner_ref, rings_ref, wind_ref, settle_ref, share_ref, seen)
            for n, chunk in enumerate(chunks):
                later_ref[t, n * ROWS : (n + 1) * ROWS, :] = chunk

    def along_y(n, carry):
        pair((n, (tiles_x - 1) * tiles_y + n))
        return carry

    def along_x(n, carry):
        pair((n * tiles_y, n * tiles_y + tiles_y - 1))
        return carry

    lax.fori_loop(0, tiles_y, along_y, 0)
    lax.fori_loop(1, tiles_x - 1, along_x, 0)
    pack_borders((e_ref, w_ref, n_ref, s_ref), lambda t: later_ref[t], tiles_x, tiles_y)


def send_seen_kernel(
    owner_ref, rings_ref, wind_ref, settle_ref, share_ref, seen_ref, later_ref,
    fw_ref, fe_ref, fs_ref, fn_ref, send_ref, ext, both, sems, *, tiles_x, tiles_y
):
    rows = later_ref.shape[1]
    wide = tiles_y + 2
    fill_tiles(ext, lambda t: rings_ref[t, :rows, :], tiles_x, tiles_y)

    def place(t):
        return place_of(t, tiles_y)

    def border(t):
        x, y = t // tiles_y, t % tiles_y
        return (x == 0) | (x == tiles_x - 1) | (y == 0) | (y == tiles_y - 1)

    def before(t, carry):
        @pl.when(border(t))
        def _():
            both[t, :rows, :] = seen_ref[t]

        @pl.when(jnp.logical_not(border(t)))
        def _():
            both[t, :rows, :] = seen_by(ext, place(t), wide)

        return carry

    lax.fori_loop(0, tiles_x * tiles_y, before, 0)
    fill_halo(ext, (fw_ref, fe_ref, fs_ref, fn_ref), tiles_x, tiles_y)

    def advance(t, carry):
        @pl.when(border(t))
        def _():
            ext[place(t)] = later_ref[t]

        @pl.when(jnp.logical_not(border(t)))
        def _():
            seen = both[t, :rows, :]
            chunks = advance_ring(t, owner_ref, rings_ref, wind_ref, settle_ref, share_ref, seen)
            for n, chunk in enumerate(chunks):
                ext[place(t), n * ROWS : (n + 1) * ROWS, :] = chunk

        return carry

    lax.fori_loop(0, tiles_x * tiles_y, advance, 0)

    def copy(t):
        return pltpu.make_async_copy(both.at[t], send_ref.at[owner_ref[t]], sems.at[t])

    def after(t, carry):
        both[t, rows:, :] = seen_by(ext, place(t), wide)

        @pl.when(owner_ref[t] >= 0)
        def _():
            copy(t).start()

        return carry

    lax.fori_loop(0, tiles_x * tiles_y, after, 0)

    def wait(t, carry):
        @pl.when(owner_ref[t] >= 0)
        def _():
            copy(t).wait()

        return carry

    lax.fori_loop(0, tiles_x * tiles_y, wait, 0)


def shifted(value, axis, steps):
    count = lax.axis_size(axis)
    return lax.ppermute(value, axis, [(source, (source + steps) % count) for source in range(count)])


def relay_rows(rows):
    return lax.all_to_all(rows, AXES, split_axis=0, concat_axis=0, tiled=True)


def exchange_borders(borders):
    east, west, north, south = borders
    return shifted(east, "gx", 1), shifted(west, "gx", -1), shifted(north, "gy", 1), shifted(south, "gy", -1)


def ring_call(kernel, tiles_x, tiles_y, rows, outs, scratch, name, hbm_in=False, hbm_out=False):
    smem = pl.BlockSpec(memory_space=pltpu.SMEM)
    vmem = pl.BlockSpec(memory_space=pltpu.VMEM)
    hbm = pl.BlockSpec(memory_space=pltpu.HBM)
    size = tiles_x * tiles_y * rows * LANES

    def call(owner_of_tile, *inputs):
        return pl.pallas_call(
            functools.partial(kernel, tiles_x=tiles_x, tiles_y=tiles_y),
            in_specs=[smem] + [hbm if hbm_in else vmem] * len(inputs),
            out_specs=hbm if hbm_out else [vmem] * len(outs),
            out_shape=outs[0] if hbm_out else outs,
            scratch_shapes=scratch,
            compiler_params=pltpu.CompilerParams(vmem_limit_bytes=32 << 20),
            cost_estimate=pl.CostEstimate(flops=16 * size, bytes_accessed=16 * size, transcendentals=0),
            name=name,
        )(owner_of_tile, *inputs)

    return call


def border_shapes(tiles_x, tiles_y, rows):
    return [f32(tiles_y // 4, rows, LANES)] * 2 + [f32(tiles_x // 4, rows, LANES)] * 2


def relay_strips(owner_of_tile, received, wind_send, wind_ring, settle_speed, bin_share, tiles_x, tiles_y):
    owners, both_rows, _ = received.shape
    rows = both_rows // 2
    per_home = tiles_x * tiles_y
    packs = border_shapes(tiles_x, tiles_y, rows)
    ext = pltpu.VMEM(((tiles_x + 2) * (tiles_y + 2), rows, LANES), jnp.float32)
    each_sem = pltpu.SemaphoreType.DMA((per_home,))
    settle_rows = jnp.broadcast_to(settle_speed[:, None], settle_speed.shape + (LANES,))
    share_rows = jnp.broadcast_to(bin_share[:, None], bin_share.shape + (LANES,))

    def call(kernel, outs, scratch, name, *inputs, **places):
        return ring_call(kernel, tiles_x, tiles_y, rows, outs, scratch, name, **places)(owner_of_tile, *inputs)

    strips = pltpu.VMEM((per_home, rows, LANES), jnp.float32)
    borders = call(
        pack_borders_kernel, packs, [strips, each_sem], "pack_borders", in_hbm(received), hbm_in=True
    )
    borders = exchange_borders(borders)
    (rings,) = call(gather_rings_kernel, [f32(per_home, both_rows, LANES)], [], "gather_rings", received)
    seen, later, *borders = call(
        advance_borders_kernel, [f32(per_home, rows, LANES)] * 2 + packs, [ext], "advance_borders",
        rings, *borders, wind_ring, settle_rows, share_rows,
    )
    borders = exchange_borders(borders)
    wind_send, *borders = lax.optimization_barrier((wind_send, *borders))
    wind_recv = relay_rows(wind_send)
    seen_send = call(
        send_seen_kernel,
        [pltpu.HBM((owners, both_rows, LANES), jnp.float32)],
        [ext, pltpu.VMEM((per_home, both_rows, LANES), jnp.float32), each_sem],
        "send_seen",
        rings, wind_ring, settle_rows, share_rows, seen, later, *borders,
        hbm_out=True,
    )
    return wind_recv, relay_rows(seen_send)


def dust_kernel(home_ref, share_ref, settle_ref, dust_ref, shift_ref, wind_ref, *refs, block, bins, outer):
    if outer:
        side_ref, seen_ref, out_ref, coef, sides, edges, *work = refs
    else:
        out_ref, kept_ref, coef, *work = refs
    lanes = len(work) // 2
    step = pl.program_id(0)
    each = TZ * bins
    if outer:
        for j in range(block):
            edges[j] = seen_ref[home_ref[step * block + j]]
        spread = jnp.dot(
            jnp.concatenate(halves_of(edges[...].reshape(block * 2 * each, LANES)), axis=1),
            side_ref[...],
            preferred_element_type=jnp.float32,
        )
        for r in range(ROWS):
            sides[r] = spread[:, r * LANES : (r + 1) * LANES]

    _, lane = iotas()
    within = lane % TILE
    first_y, last_y = within == 0, within == TILE - 1
    low_lanes, high_lanes = lane < TILE, lane >= LANES - TILE
    mix = dust_step * diffusion
    chunks = bins // ROWS
    settle = [dust_step * settle_ref[h * ROWS : (h + 1) * ROWS, :] for h in range(chunks)]
    share = [share_ref[h * ROWS : (h + 1) * ROWS, :] for h in range(chunks)]

    def prepare(k, j):
        held = work[2 * k]
        home = home_ref[step * block + j]
        if not outer:
            kept_ref[j] = wind_ref[home]
        wind_at = j if outer else home
        plane = [wind_ref[wind_at, p * ROWS : (p + 1) * ROWS, :] * dust_step for p in range(PLANES)]
        for level in range(TZ):
            u, v = plane[level], plane[TZ + level]
            south_by = mix + jnp.maximum(v, 0.0)
            north_by = mix + jnp.maximum(-v, 0.0)
            coef[k, 0, level] = mix + jnp.maximum(u, 0.0)
            coef[k, 1, level] = mix + jnp.maximum(-u, 0.0)
            coef[k, 4, level] = 1.0 - 6.0 * mix - jnp.abs(u) - jnp.abs(v)
            coef[k, 5, level] = plane[2 * TZ + level]
            if outer:
                coef[k, 2, level] = south_by
                coef[k, 3, level] = north_by
                coef[k, 7, level] = jnp.where(first_y, south_by, jnp.where(last_y, north_by, 0.0))
            else:
                coef[k, 2, level] = jnp.where(first_y, 0.0, south_by)
                coef[k, 3, level] = jnp.where(last_y, 0.0, north_by)
        coef[k, 6, 0] = plane[PLANES - 1]
        for r in range(ROWS):
            for level in range(TZ):
                at = (r * TZ + level) * bins
                cells = dust_ref[j, pl.ds(r * TZ + level, bins, stride=ROWS * TZ), :]
                if not outer:
                    held[at : at + bins, :] = cells
                    continue
                for h in range(chunks):
                    edge_at = level * bins + h * ROWS
                    q = cells[h * ROWS : (h + 1) * ROWS]
                    q = q + spread_rows(coef[k, 7, level, r : r + 1, :]) * sides[r, pl.ds(j * 2 * each + edge_at, ROWS), :]
                    if r == 0 or r == ROWS - 1:
                        edge = edges[j, edge_at : edge_at + ROWS, :]
                        here = low_lanes if r == 0 else high_lanes
                        by = spread_rows(coef[k, 0 if r == 0 else 1, level, r : r + 1, :])
                        q = q + jnp.where(here, by * edge, 0.0)
                    held[at + h * ROWS : at + (h + 1) * ROWS, :] = q

    def shift(k):
        held, shifts = work[2 * k], work[2 * k + 1]
        shifts[...] = jnp.dot(
            jnp.concatenate(halves_of(held[...]), axis=1), shift_ref[...], preferred_element_type=jnp.float32
        )

    def update(k, j):
        held, shifts = work[2 * k], work[2 * k + 1]
        nothing = jnp.zeros((ROWS, LANES), jnp.float32)
        for r in range(ROWS):
            for h in range(chunks):
                cells = [held[(r * TZ + level) * bins + h * ROWS :][:ROWS] for level in range(TZ)]
                for level in range(TZ):
                    at = (r * TZ + level) * bins + h * ROWS
                    edge_at = each + level * bins + h * ROWS

                    def moved(which, rows_up=0):
                        first = at + rows_up * TZ * bins
                        return shifts[first : first + ROWS, which * LANES : (which + 1) * LANES]

                    def by(which):
                        return spread_rows(coef[k, which, level, r : r + 1, :])

                    edge = edges[j, edge_at : edge_at + ROWS, :] if outer else nothing
                    before = edge if r == 0 else moved(2, -1)
                    after = edge if r == ROWS - 1 else moved(3, 1)
                    south, north = moved(0), moved(1)
                    if outer:
                        side = sides[r, pl.ds(j * 2 * each + edge_at, ROWS), :]
                        south = jnp.where(first_y, side, south)
                        north = jnp.where(last_y, side, north)
                    west = jnp.where(low_lanes, before, moved(2))
                    east = jnp.where(high_lanes, after, moved(3))
                    rise = by(5) - settle[h]
                    up = jnp.maximum(rise, 0.0)
                    mixed = mix + (up - rise if level == 0 else up)
                    value = (
                        (by(4) - jnp.abs(rise)) * cells[level]
                        + by(0) * west
                        + by(1) * east
                        + by(2) * south
                        + by(3) * north
                        + mixed * cells[1 - level]
                    )
                    if level == 0:
                        value = value + spread_rows(coef[k, 6, 0, r : r + 1, :]) * share[h]
                    first = h * ROWS * ROWS * TZ + r * TZ + level
                    out_ref[j, pl.ds(first, ROWS, stride=ROWS * TZ), :] = value

    def some(i, carry):
        for k in range(lanes):
            prepare(k, i * lanes + k)
        for k in range(lanes):
            shift(k)
        for k in range(lanes):
            update(k, i * lanes + k)
        return carry

    lax.fori_loop(0, block // lanes, some, 0)


def dust_substep(home_of_slot, dust, wind, settle_speed, bin_share, seen_recv=None):
    slots, cells = dust.shape[:2]
    bins = settle_speed.shape[0]
    block = 8 if slots % 8 == 0 else 4
    lanes = 2
    outer = seen_recv is not None
    smem = pl.BlockSpec(memory_space=pltpu.SMEM)
    vmem = pl.BlockSpec(memory_space=pltpu.VMEM)
    tile = pl.BlockSpec((block, cells, LANES), lambda i: (i, 0, 0))
    settle = jnp.broadcast_to(settle_speed[:, None], (bins, LANES))
    share = jnp.broadcast_to(bin_share[:, None], (bins, LANES))
    wind_rows = pl.BlockSpec((block,) + wind.shape[1:], lambda i: (i, 0, 0))
    inputs = [home_of_slot, share, settle, in_hbm(dust), jnp.asarray(shift_matrix()), in_hbm(wind) if outer else wind]
    scratch = [pltpu.VMEM((lanes, PLANES + 1, TZ, ROWS, LANES), jnp.float32)]
    if outer:
        inputs += [jnp.asarray(side_matrix()), seen_recv]
        scratch += [
            pltpu.VMEM((ROWS, block * seen_recv.shape[1], LANES), jnp.float32),
            pltpu.VMEM((block,) + seen_recv.shape[1:], jnp.float32),
        ]
    out_shape = f32(*dust.shape)
    if not outer:
        out_shape = [pltpu.HBM(dust.shape, jnp.float32), pltpu.HBM((slots,) + wind.shape[1:], jnp.float32)]
    scratch += [pltpu.VMEM((cells, LANES), jnp.float32), pltpu.VMEM((cells, 4 * LANES), jnp.float32)] * lanes
    return pl.pallas_call(
        functools.partial(dust_kernel, block=block, bins=bins, outer=outer),
        grid=(slots // block,),
        in_specs=[smem, vmem, vmem, tile, vmem, wind_rows if outer else vmem] + [vmem] * (len(inputs) - 6),
        out_specs=tile if outer else [tile, wind_rows],
        out_shape=out_shape,
        scratch_shapes=scratch,
        compiler_params=pltpu.CompilerParams(vmem_limit_bytes=32 << 20),
        cost_estimate=pl.CostEstimate(flops=60 * dust.size, bytes_accessed=dust.size * 12, transcendentals=0),
        name="dust_outer" if outer else "dust_inner",
    )(*inputs)


def per_device(velocity, threshold, dust_mass, settle_speed, bin_share, active_tiles, tile_owner):
    owners = lax.axis_size(AXES)
    grid_cols = lax.axis_size("gy")
    self_index = lax.axis_index(AXES)
    slots, bins = dust_mass.shape[:2]
    tiles_x = velocity.shape[2] // TILE
    tiles_y = velocity.shape[3] // TILE
    per_home = tiles_x * tiles_y
    tiles_across = tiles_y * grid_cols

    tile_x = active_tiles // tiles_across
    tile_y = active_tiles % tiles_across
    home_dev = tile_x // tiles_x * grid_cols + tile_y // tiles_y
    local_tile = tile_x % tiles_x * tiles_y + tile_y % tiles_y
    own_slot = tile_owner - self_index * slots
    mine = jnp.where(home_dev == self_index, local_tile, -1)
    slot_ids = jnp.arange(slots, dtype=jnp.int32)
    home_of_slot = jnp.sum(jnp.where(own_slot[None, :] == slot_ids[:, None], home_dev[None, :], 0), axis=1)
    tile_ids = jnp.arange(per_home, dtype=jnp.int32)
    owner_of_tile = jnp.max(
        jnp.where(mine[None, :] == tile_ids[:, None], (tile_owner // slots)[None, :], -1), axis=1
    )

    dust = dust_mass.reshape(slots, bins, TZ, ROWS, LANES).transpose(0, 1, 3, 2, 4)
    dust = dust.reshape(slots, bins * ROWS * TZ, LANES)

    xlo, xhi, ylo, yhi = exchange_borders(wind_faces(velocity))

    strips_send = dust_strips(home_of_slot, dust, bins, owners)
    strips_send, xlo, xhi, ylo, yhi = lax.optimization_barrier((strips_send, xlo, xhi, ylo, yhi))
    strips = relay_rows(strips_send)
    new_velocity, wind_send, wind_ring = wind_step(
        owner_of_tile, velocity, xlo, xhi, ylo, yhi, threshold, owners
    )
    strips, wind_send, wind_ring = lax.optimization_barrier((strips, wind_send, wind_ring))
    wind_recv, seen_recv = relay_strips(
        owner_of_tile, strips, wind_send, wind_ring, settle_speed, bin_share, tiles_x, tiles_y
    )
    inner, wind_held = dust_substep(home_of_slot, dust, wind_recv, settle_speed, bin_share)
    out = dust_substep(home_of_slot, inner, wind_held, settle_speed, bin_share, seen_recv)
    out = out.reshape(slots, bins, ROWS, TZ, LANES).transpose(0, 1, 3, 2, 4).reshape(dust_mass.shape)
    return new_velocity, out


def solution(mesh):
    in_specs = (
        P(None, None, "gx", "gy"),
        P("gx", "gy"),
        P(AXES, None, None, None),
        P(),
        P(),
        P(),
        P(),
    )
    out_specs = (P(None, None, "gx", "gy"), P(AXES, None, None, None))
    return jax.shard_map(
        per_device, mesh=mesh, in_specs=in_specs, out_specs=out_specs, check_vma=False
    )
```

```python
import functools

import jax
import jax.numpy as jnp
import ml_dtypes
import numpy as np
from jax import lax
from jax.experimental import pallas as pl
from jax.experimental.pallas import tpu as pltpu
from jax.sharding import PartitionSpec as P

TZ = 2
TILE = 32
LANES = 128
ROWS = TILE * TILE // LANES
PLANES = 7
AXES = ("gx", "gy")

time_step = 0.1
viscosity = 0.2
dust_step = 0.1
diffusion = 0.1
roughness = 0.5
emit_rate = 0.5

WEST, SOUTH, NORTH, EAST = range(4)


def iotas(shape=(ROWS, LANES)):
    return lax.broadcasted_iota(jnp.int32, shape, 0), lax.broadcasted_iota(jnp.int32, shape, 1)


def lane_gather(x, index):
    return jnp.take_along_axis(x, index, axis=1)


def ring_pattern(depth):
    row, lane = iotas()
    group, within = lane // TILE, lane % TILE
    side = jnp.where(group == SOUTH, depth, TILE - 1 - depth)
    index = (within % 4) * TILE + side
    index = jnp.where(group == WEST, depth * TILE + within, index)
    index = jnp.where(group == EAST, (3 - depth) * TILE + within, index)
    source = jnp.where(group == WEST, 0, jnp.where(group == EAST, ROWS - 1, within // 4))
    return index, row == source


def ring_of(x, pattern):
    index, taken = pattern
    return jnp.sum(jnp.where(taken, lane_gather(x, index), 0.0), axis=0, keepdims=True)


def spread_rows(row):
    return jnp.broadcast_to(row, (ROWS, LANES))


def f32(*shape):
    return jax.ShapeDtypeStruct(shape, jnp.float32)


def in_hbm(x):
    return pltpu.with_memory_space_constraint(x, pltpu.HBM)


def halves_of(x):
    high = x.astype(jnp.bfloat16)
    return high, (x - high.astype(jnp.float32)).astype(jnp.bfloat16)


def moves(sources):
    lanes = np.arange(LANES)[:, None]
    once = (lanes == np.asarray(sources)[None, :]).astype(ml_dtypes.bfloat16)
    return np.concatenate([once, once], axis=0)


def ring_matrix():
    lane = np.arange(LANES)
    group, within = lane // TILE, lane % TILE
    blocks = []
    for r in range(ROWS):
        columns = []
        for depth in range(2):
            side = np.where(group == SOUTH, depth, TILE - 1 - depth)
            source = np.where(within // 4 == r, (within % 4) * TILE + side, -1)
            source = np.where(group == WEST, depth * TILE + within if r == 0 else -1, source)
            source = np.where(group == EAST, (3 - depth) * TILE + within if r == ROWS - 1 else -1, source)
            columns.append(source)
        blocks.append(moves(np.concatenate(columns)))
    return np.concatenate(blocks, axis=0)


def shift_matrix():
    lane = np.arange(LANES)
    return moves(np.concatenate([(lane + d) % LANES for d in (-1, 1, -TILE, TILE)]))


def side_matrix():
    lane = np.arange(LANES)
    columns = []
    for r in range(ROWS):
        along = 4 * r + lane // TILE
        source = np.where(lane % TILE == 0, SOUTH * TILE + along, -1)
        columns.append(np.where(lane % TILE == TILE - 1, NORTH * TILE + along, source))
    return moves(np.concatenate(columns))


def strips_kernel(home_ref, dust_hbm, matrix_ref, send_ref, dust, rings, load_sems, sems, *, block, bins):
    slots = rings.shape[0]
    each = TZ * bins

    def load(i):
        some = pl.ds(i * block, block)
        return pltpu.make_async_copy(dust_hbm.at[some], dust.at[some], load_sems.at[i])

    def send(s):
        return pltpu.make_async_copy(rings.at[s], send_ref.at[home_ref[s]], sems.at[s])

    for i in range(slots // block):
        load(i).start()

    def one(i, carry):
        load(i).wait()
        parts = []
        for r in range(ROWS):
            x = jnp.concatenate(
                [
                    dust[i * block + j, pl.ds(r * TZ + level, bins, stride=ROWS * TZ), :]
                    for j in range(block)
                    for level in range(TZ)
                ],
                axis=0,
            )
            parts += halves_of(x)
        found = jnp.dot(
            jnp.concatenate(parts, axis=1), matrix_ref[...], preferred_element_type=jnp.float32
        )
        for j in range(block):
            for depth in range(2):
                rings[i * block + j, depth * each : (depth + 1) * each, :] = found[
                    j * each : (j + 1) * each, depth * LANES : (depth + 1) * LANES
                ]
            send(i * block + j).start()
        return carry

    lax.fori_loop(0, slots // block, one, 0)

    def wait(s, carry):
        send(s).wait()
        return carry

    lax.fori_loop(0, slots, wait, 0)


def dust_strips(home_of_slot, dust, bins, owners):
    slots, cells = dust.shape[:2]
    block = 8 if slots % 8 == 0 else 4
    rows = 2 * bins * TZ
    matrix = jnp.asarray(ring_matrix())
    hbm = pl.BlockSpec(memory_space=pltpu.HBM)
    return pl.pallas_call(
        functools.partial(strips_kernel, block=block, bins=bins),
        in_specs=[pl.BlockSpec(memory_space=pltpu.SMEM), hbm, pl.BlockSpec(memory_space=pltpu.VMEM)],
        out_specs=hbm,
        out_shape=pltpu.HBM((owners, rows, LANES), jnp.float32),
        scratch_shapes=[
            pltpu.VMEM(dust.shape, jnp.float32),
            pltpu.VMEM((slots, rows, LANES), jnp.float32),
            pltpu.SemaphoreType.DMA((slots // block,)),
            pltpu.SemaphoreType.DMA((slots,)),
        ],
        compiler_params=pltpu.CompilerParams(vmem_limit_bytes=32 << 20),
        cost_estimate=pl.CostEstimate(
            flops=20 * dust.size, bytes_accessed=dust.size * 4 + slots * rows * LANES * 4, transcendentals=0
        ),
        name="dust_strips",
    )(home_of_slot, in_hbm(dust), matrix)


def faces_kernel(vel_ref, x_last_ref, x_first_ref, y_last_ref, y_first_ref, first, last, low, high, x_sems, y_sems):
    fields, nx, ny = vel_ref.shape
    x_copies = [
        pltpu.make_async_copy(vel_ref.at[:, pl.ds(0, ROWS), :], first, x_sems.at[0]),
        pltpu.make_async_copy(vel_ref.at[:, pl.ds(nx - ROWS, ROWS), :], last, x_sems.at[1]),
    ]
    y_copies = [
        (
            pltpu.make_async_copy(vel_ref.at[f, :, pl.ds(0, LANES)], low.at[f], y_sems.at[0, f]),
            pltpu.make_async_copy(vel_ref.at[f, :, pl.ds(ny - LANES, LANES)], high.at[f], y_sems.at[1, f]),
        )
        for f in range(fields)
    ]
    for pair in y_copies:
        for copy in pair:
            copy.start()
    for copy in x_copies:
        copy.start()
    lane = lax.broadcasted_iota(jnp.int32, (nx, LANES), 1)
    for f, (low_copy, high_copy) in enumerate(y_copies):
        low_copy.wait()
        high_copy.wait()
        from_low = pltpu.roll(low[f], f, 1) if f else low[f]
        from_high = pltpu.roll(high[f], f + 1, 1)
        if f == 0:
            y_first_ref[...], y_last_ref[...] = from_low, from_high
        else:
            y_first_ref[...] = jnp.where(lane == f, from_low, y_first_ref[...])
            y_last_ref[...] = jnp.where(lane == f, from_high, y_last_ref[...])
    for copy in x_copies:
        copy.wait()
    for f in range(fields):
        x_first_ref[f : f + 1, :] = first[f, 0:1, :]
        x_last_ref[f : f + 1, :] = last[f, ROWS - 1 : ROWS, :]


def wind_faces(velocity):
    comps, levels, nx, ny = velocity.shape
    fields = comps * levels
    vmem = pl.BlockSpec(memory_space=pltpu.VMEM)
    return pl.pallas_call(
        faces_kernel,
        in_specs=[pl.BlockSpec(memory_space=pltpu.HBM)],
        out_specs=[vmem] * 4,
        out_shape=[f32(fields, ny)] * 2 + [f32(nx, LANES)] * 2,
        scratch_shapes=[
            pltpu.VMEM((fields, ROWS, ny), jnp.float32),
            pltpu.VMEM((fields, ROWS, ny), jnp.float32),
            pltpu.VMEM((fields, nx, LANES), jnp.float32),
            pltpu.VMEM((fields, nx, LANES), jnp.float32),
            pltpu.SemaphoreType.DMA((2,)),
            pltpu.SemaphoreType.DMA((2, fields)),
        ],
        compiler_params=pltpu.CompilerParams(vmem_limit_bytes=32 << 20),
        cost_estimate=pl.CostEstimate(flops=velocity.size, bytes_accessed=velocity.size * 4, transcendentals=0),
        name="wind_faces",
    )(in_hbm(velocity.reshape(fields, nx, ny)))


def wind_kernel(
    owner_ref, vel_ref, xlo_ref, xhi_ref, ylo_ref, yhi_ref, thr_ref,
    new_ref, send_ref, ring_ref, padded, strip, tiles, load_sem, sems, *, levels
):
    fields, nx, ny = new_ref.shape
    load = pltpu.make_async_copy(vel_ref, padded.at[:, pl.ds(8, nx), :], load_sem)
    load.start()
    load.wait()
    for f in range(fields):
        padded[f, 7:8, :] = xlo_ref[f : f + 1, :]
        padded[f, 8 + nx : 9 + nx, :] = xhi_ref[f : f + 1, :]
    half = 16
    halves = ny // LANES
    tiles_y = ny // TILE
    pattern = ring_pattern(0)
    _, lane8 = iotas()
    group = lane8 // TILE

    def one_strip(ix, carry):
        for sub in range(TILE // half):
            base = pl.multiple_of(ix * TILE + sub * half, 8)
            lane = lax.broadcasted_iota(jnp.int32, (half, ny), 1)
            low = {}
            faces = [ref[pl.ds(base, half), :] for ref in (ylo_ref, yhi_ref)]

            def face(which, f, to):
                moved = pltpu.roll(faces[which], (to - f) % LANES, 1) if f != to else faces[which]
                return jnp.concatenate([moved] * halves, axis=1)

            for z in range(levels):
                u, v, w = (padded[c * levels + z, pl.ds(base + 8, half), :] for c in range(3))
                for c in range(3):
                    f = c * levels + z
                    block = padded[f, pl.ds(base, half + 16), :]
                    centre = (u, v, w)[c]
                    west = pltpu.roll(block, 1, 0)[8 : 8 + half]
                    east = pltpu.roll(block, half + 15, 0)[8 : 8 + half]
                    south = jnp.where(lane == 0, face(0, f, 0), pltpu.roll(centre, 1, 1))
                    north = jnp.where(lane == ny - 1, face(1, f, LANES - 1), pltpu.roll(centre, ny - 1, 1))
                    lower = -centre if z == 0 else padded[f - 1, pl.ds(base + 8, half), :]
                    upper = centre if z == levels - 1 else padded[f + 1, pl.ds(base + 8, half), :]
                    carried = 0.5 * (u * (east - west) + v * (north - south) + w * (upper - lower))
                    spread = east + west + north + south + upper + lower - 6.0 * centre
                    new = centre + time_step * (viscosity * spread - carried)
                    new_ref[f, pl.ds(base, half), :] = new
                    if z < TZ:
                        low[c * TZ + z] = new
            stress = roughness * (low[0] * low[0] + low[TZ] * low[TZ])
            low[PLANES - 1] = emit_rate * stress * jnp.maximum(
                stress - thr_ref[pl.ds(base, half), :], 0.0
            )
            for p in range(PLANES):
                for h in range(halves):
                    strip[p * halves + h, sub * half : (sub + 1) * half, :] = low[p][
                        :, h * LANES : (h + 1) * LANES
                    ]
        for p in range(PLANES):
            for h in range(halves):
                parts = [strip[p * halves + h, pl.ds(k, ROWS, stride=4), :] for k in range(4)]
                for t in range(4):
                    tile = ix * tiles_y + h * 4 + t
                    cells = pltpu.roll(parts[0], (-t * TILE) % LANES, 1) if t else parts[0]
                    for k in range(1, 4):
                        moved = pltpu.roll(parts[k], ((k - t) * TILE) % LANES, 1) if k != t else parts[k]
                        cells = jnp.where(group == k, moved, cells)
                    tiles[tile, p * ROWS : (p + 1) * ROWS, :] = cells
                    ring_ref[tile, p : p + 1, :] = ring_of(cells, pattern)

        def send(t, inner):
            tile = ix * tiles_y + t
            owner = owner_ref[tile]

            @pl.when(owner >= 0)
            def _():
                pltpu.make_async_copy(tiles.at[tile], send_ref.at[owner], sems.at[tile]).start()

            return inner

        lax.fori_loop(0, tiles_y, send, 0)
        return carry

    lax.fori_loop(0, nx // TILE, one_strip, 0)

    def wait(tile, carry):
        owner = owner_ref[tile]

        @pl.when(owner >= 0)
        def _():
            pltpu.make_async_copy(tiles.at[tile], send_ref.at[owner], sems.at[tile]).wait()

        return carry

    lax.fori_loop(0, tiles.shape[0], wait, 0)


def wind_step(owner_of_tile, velocity, xlo, xhi, ylo, yhi, threshold, owners):
    comps, levels, nx, ny = velocity.shape
    fields = comps * levels
    per_home = (nx // TILE) * (ny // TILE)
    smem = pl.BlockSpec(memory_space=pltpu.SMEM)
    hbm = pl.BlockSpec(memory_space=pltpu.HBM)
    vmem = pl.BlockSpec(memory_space=pltpu.VMEM)
    new, send, ring = pl.pallas_call(
        functools.partial(wind_kernel, levels=levels),
        in_specs=[smem, hbm, vmem, vmem, vmem, vmem, vmem],
        out_specs=[vmem, hbm, vmem],
        out_shape=[
            f32(fields, nx, ny),
            pltpu.HBM((owners, PLANES * ROWS, LANES), jnp.float32),
            f32(per_home, 8, LANES),
        ],
        scratch_shapes=[
            pltpu.VMEM((fields, nx + 16, ny), jnp.float32),
            pltpu.VMEM((PLANES * (ny // LANES), TILE, LANES), jnp.float32),
            pltpu.VMEM((per_home, PLANES * ROWS, LANES), jnp.float32),
            pltpu.SemaphoreType.DMA,
            pltpu.SemaphoreType.DMA((per_home,)),
        ],
        compiler_params=pltpu.CompilerParams(vmem_limit_bytes=40 << 20),
        cost_estimate=pl.CostEstimate(
            flops=40 * velocity.size, bytes_accessed=velocity.size * 10, transcendentals=0
        ),
        name="wind_step",
    )(
        owner_of_tile,
        in_hbm(velocity.reshape(fields, nx, ny)),
        xlo,
        xhi,
        ylo,
        yhi,
        threshold,
    )
    return new.reshape(velocity.shape), send, ring


def border_tiles(tiles_x, tiles_y):
    return (
        (EAST, [(tiles_x - 1) * tiles_y + n for n in range(tiles_y)]),
        (WEST, [n for n in range(tiles_y)]),
        (NORTH, [n * tiles_y + tiles_y - 1 for n in range(tiles_x)]),
        (SOUTH, [n * tiles_y for n in range(tiles_x)]),
    )


def fill_halo(ext, strips, tiles_x, tiles_y):
    wide = tiles_y + 2
    for strip_of, side, places in (
        (strips[0], EAST, [n + 1 for n in range(tiles_y)]),
        (strips[1], WEST, [(tiles_x + 1) * wide + n + 1 for n in range(tiles_y)]),
        (strips[2], NORTH, [(n + 1) * wide for n in range(tiles_x)]),
        (strips[3], SOUTH, [(n + 1) * wide + tiles_y + 1 for n in range(tiles_x)]),
    ):
        for n, place in enumerate(places):
            strip = strip_of(n // 4)
            if n % 4 != side:
                strip = pltpu.roll(strip, ((side - n % 4) * TILE) % LANES, 1)
            ext[place] = strip


def seen_by(ext, place, wide):
    west, east = ext[place - wide], ext[place + wide]
    south, north = ext[place - 1], ext[place + 1]
    lane = lax.broadcasted_iota(jnp.int32, west.shape, 1)
    up = pltpu.roll(jnp.where(lane < 2 * TILE, north, west), TILE, 1)
    down = pltpu.roll(jnp.where(lane < 2 * TILE, east, south), LANES - TILE, 1)
    return jnp.where((lane // TILE) % 2 == 0, up, down)


FLAG = 7


def pack_borders_kernel(owner_ref, recv_ref, wind_ref, *refs, tiles_x, tiles_y):
    *outs, rings, sems = refs
    both_rows = rings.shape[1]
    borders = border_tiles(tiles_x, tiles_y)
    used = sorted({t for _, tiles in borders for t in tiles})

    def copy(t):
        return pltpu.make_async_copy(recv_ref.at[owner_ref[t]], rings.at[t], sems.at[t])

    for t in used:

        @pl.when(owner_ref[t] >= 0)
        def _():
            copy(t).start()

        @pl.when(owner_ref[t] < 0)
        def _():
            rings[t] = jnp.zeros(rings.shape[1:], jnp.float32)

    for t in used:

        @pl.when(owner_ref[t] >= 0)
        def _():
            copy(t).wait()

    lane = lax.broadcasted_iota(jnp.int32, (both_rows, LANES), 1) // TILE
    row8, lane8 = iotas()
    group8 = lane8 // TILE
    for out, (side, tiles) in zip(outs, borders):
        for g in range(len(tiles) // 4):
            strips = winds = None
            for q in range(4):
                t = tiles[4 * g + q]
                strip, wind = rings[t], wind_ref[t]
                if q != side:
                    strip = pltpu.roll(strip, ((q - side) * TILE) % LANES, 1)
                    wind = pltpu.roll(wind, ((q - side) * TILE) % LANES, 1)
                wind = jnp.where(row8 == FLAG, jnp.where(owner_ref[t] >= 0, 1.0, 0.0), wind)
                strips = strip if strips is None else jnp.where(lane == q, strip, strips)
                winds = wind if winds is None else jnp.where(group8 == q, wind, winds)
            at = g * (both_rows + ROWS)
            out[at : at + both_rows, :] = strips
            out[at + both_rows : at + both_rows + ROWS, :] = winds


def add_corners_kernel(owner_ref, e_ref, w_ref, fs_ref, fn_ref, e_out, w_out, *, tiles_x, tiles_y):
    size = e_ref.shape[0]
    rows = e_out.shape[0] - size
    last = fs_ref.shape[0] - (2 * rows + ROWS)
    lane = lax.broadcasted_iota(jnp.int32, (rows, LANES), 1)
    e_out[:size, :] = e_ref[...]
    w_out[:size, :] = w_ref[...]
    e_out[size:, :] = jnp.where(
        lane == 0, pltpu.roll(fs_ref[last : last + rows, :], 1, 1), fn_ref[last : last + rows, :]
    )
    w_out[size:, :] = jnp.where(lane == 0, fs_ref[:rows, :], pltpu.roll(fn_ref[:rows, :], LANES - 1, 1))


def gather_rings_kernel(owner_ref, recv_ref, rings_ref, *, tiles_x, tiles_y):
    def one(t, carry):
        owner = owner_ref[t]
        rings = recv_ref[jnp.maximum(owner, 0)]
        rings_ref[t] = jnp.where(owner >= 0, rings, 0.0)
        return carry

    lax.fori_loop(0, tiles_x * tiles_y, one, 0)


def fill_tiles(ext, tile, tiles_x, tiles_y):
    def inner(t, carry):
        ext[place_of(t, tiles_y)] = tile(t)
        return carry

    lax.fori_loop(0, tiles_x * tiles_y, inner, 0)


def place_of(t, tiles_y):
    return (t // tiles_y + 1) * (tiles_y + 2) + t % tiles_y + 1


def advance_ring(t, owner_ref, rings_ref, wind_ref, settle_ref, share_ref, seen):
    _, lane = iotas()
    group, within = lane // TILE, lane % TILE
    on_x = (group == WEST) | (group == EAST)
    first, last = within == 0, within == TILE - 1
    high = jnp.where((group == EAST) | (group == NORTH), TILE - 1, 0)
    corner = jnp.where(
        on_x,
        jnp.where(first, SOUTH, NORTH) * TILE + high,
        jnp.where(first, WEST, EAST) * TILE + high,
    )
    rows = rings_ref.shape[1] // 2
    bins = rows // TZ
    uplift = dust_step * spread_rows(wind_ref[t, PLANES - 1 : PLANES, :])
    mix = dust_step * diffusion
    active = owner_ref[t] >= 0
    chunks = []
    for at in range(0, rows, ROWS):
        level, bin_at = at // bins, at % bins
        if bin_at == 0:
            u, v, w = (
                dust_step * spread_rows(wind_ref[t, c * TZ + level : c * TZ + level + 1, :]) for c in range(3)
            )
            from_west = mix + jnp.maximum(u, 0.0)
            from_east = mix + jnp.maximum(-u, 0.0)
            from_south = mix + jnp.maximum(v, 0.0)
            from_north = mix + jnp.maximum(-v, 0.0)
            keep = 1.0 - 6.0 * mix - jnp.abs(u) - jnp.abs(v)
        q = rings_ref[t, at : at + ROWS, :]
        deep = rings_ref[t, rows + at : rows + at + ROWS, :]
        out = seen[at : at + ROWS, :]
        beyond = lane_gather(out, corner)
        before = jnp.where(first, beyond, pltpu.roll(q, 1, 1))
        after = jnp.where(last, beyond, pltpu.roll(q, LANES - 1, 1))
        west = jnp.where(group == WEST, out, jnp.where(group == EAST, deep, before))
        east = jnp.where(group == WEST, deep, jnp.where(group == EAST, out, after))
        south = jnp.where(on_x, before, jnp.where(group == SOUTH, out, deep))
        north = jnp.where(on_x, after, jnp.where(group == SOUTH, deep, out))
        other_at = (1 - level) * bins + bin_at
        other = rings_ref[t, other_at : other_at + ROWS, :]
        rise = w - dust_step * settle_ref[bin_at : bin_at + ROWS, :]
        up = jnp.maximum(rise, 0.0)
        down = up - rise
        new = (
            (keep - up - down) * q
            + from_west * west
            + from_east * east
            + from_south * south
            + from_north * north
            + (mix + (down if level == 0 else up)) * other
        )
        if level == 0:
            new = new + uplift * share_ref[bin_at : bin_at + ROWS, :]
        chunks.append(jnp.where(active, new, 0.0))
    return chunks


def advance_strip(side, message, ours, low_end, high_end, settle_ref, share_ref, out, rows):
    _, lane = iotas()
    bins = rows // TZ
    each = 2 * rows + ROWS
    groups = out.shape[0]
    mix = dust_step * diffusion
    for g in range(groups):
        wind_at = g * each + 2 * rows

        def wind_row(p):
            return spread_rows(message[wind_at + p : wind_at + p + 1, :])

        for at in range(0, rows, ROWS):
            level, bin_at = at // bins, at % bins
            u, v, w = (dust_step * wind_row(c * TZ + level) for c in range(3))

            def cells(group, first):
                return message[group * each + first : group * each + first + ROWS, :]

            q = cells(g, at)
            deep = cells(g, rows + at)
            near = ours[g * each + at : g * each + at + ROWS, :]
            low = low_end(at) if g == 0 else pltpu.roll(cells(g - 1, at), 1, 1)
            high = high_end(at) if g == groups - 1 else pltpu.roll(cells(g + 1, at), LANES - 1, 1)
            before = jnp.where(lane == 0, low, pltpu.roll(q, 1, 1))
            after = jnp.where(lane == LANES - 1, high, pltpu.roll(q, LANES - 1, 1))
            across = (deep, near) if side in (WEST, SOUTH) else (near, deep)
            (west, east), (south, north) = (
                (across, (before, after)) if side in (WEST, EAST) else ((before, after), across)
            )
            other = cells(g, (1 - level) * bins + bin_at)
            rise = w - dust_step * settle_ref[bin_at : bin_at + ROWS, :]
            up = jnp.maximum(rise, 0.0)
            down = up - rise
            new = (
                (1.0 - 6.0 * mix - jnp.abs(u) - jnp.abs(v) - up - down) * q
                + (mix + jnp.maximum(u, 0.0)) * west
                + (mix + jnp.maximum(-u, 0.0)) * east
                + (mix + jnp.maximum(v, 0.0)) * south
                + (mix + jnp.maximum(-v, 0.0)) * north
                + (mix + (down if level == 0 else up)) * other
            )
            if level == 0:
                new = new + dust_step * wind_row(PLANES - 1) * share_ref[bin_at : bin_at + ROWS, :]
            out[g, at : at + ROWS, :] = jnp.where(wind_row(FLAG) > 0.0, new, 0.0)


def send_seen_kernel(
    owner_ref, rings_ref, wind_ref, settle_ref, share_ref, e_ref, w_ref, n_ref, s_ref, fw_ref, fe_ref, fs_ref, fn_ref,
    send_ref, ext, both, lw_ref, le_ref, ls_ref, ln_ref, sems, *, tiles_x, tiles_y
):
    rows = rings_ref.shape[1] // 2
    wide = tiles_y + 2
    each = 2 * rows + ROWS
    messages = (fw_ref, fe_ref, fs_ref, fn_ref)
    later = (lw_ref, le_ref, ls_ref, ln_ref)

    def place(t):
        return place_of(t, tiles_y)

    fill_halo(
        ext, [lambda g, m=m: m[g * each : g * each + rows, :] for m in messages], tiles_x, tiles_y
    )
    fill_tiles(ext, lambda t: rings_ref[t, :rows, :], tiles_x, tiles_y)

    def before(t, carry):
        both[t, :rows, :] = seen_by(ext, place(t), wide)
        return carry

    lax.fori_loop(0, tiles_x * tiles_y, before, 0)

    def advance(i, carry):
        for t in (2 * i, 2 * i + 1):
            chunks = advance_ring(t, owner_ref, rings_ref, wind_ref, settle_ref, share_ref, both[t, :rows, :])
            for n, chunk in enumerate(chunks):
                ext[place(t), n * ROWS : (n + 1) * ROWS, :] = chunk
        return carry

    lax.fori_loop(0, tiles_x * tiles_y // 2, advance, 0)

    def corner(ref, shift):
        first = ref.shape[0] - rows

        def of(at):
            cells = ref[first + at : first + at + ROWS, :]
            return pltpu.roll(cells, shift, 1) if shift else cells

        return of

    ends = (
        (corner(fw_ref, 0), corner(fw_ref, 0)),
        (corner(fe_ref, 0), corner(fe_ref, 0)),
        (corner(fw_ref, 0), corner(fe_ref, LANES - 1)),
        (corner(fw_ref, 1), corner(fe_ref, 0)),
    )
    for side, message, ours, (low, high), out in zip(
        (WEST, EAST, SOUTH, NORTH), messages, (w_ref, e_ref, s_ref, n_ref), ends, later
    ):
        advance_strip(side, message, ours, low, high, settle_ref, share_ref, out, rows)
    fill_halo(ext, [lambda g, m=m: m[g] for m in later], tiles_x, tiles_y)

    def copy(t):
        return pltpu.make_async_copy(both.at[t], send_ref.at[owner_ref[t]], sems.at[t])

    def after(t, carry):
        both[t, rows:, :] = seen_by(ext, place(t), wide)

        @pl.when(owner_ref[t] >= 0)
        def _():
            copy(t).start()

        return carry

    lax.fori_loop(0, tiles_x * tiles_y, after, 0)

    def wait(t, carry):
        @pl.when(owner_ref[t] >= 0)
        def _():
            copy(t).wait()

        return carry

    lax.fori_loop(0, tiles_x * tiles_y, wait, 0)


def shifted(value, axis, steps):
    count = lax.axis_size(axis)
    return lax.ppermute(value, axis, [(source, (source + steps) % count) for source in range(count)])


def relay_rows(rows):
    return lax.all_to_all(rows, AXES, split_axis=0, concat_axis=0, tiled=True)


def exchange_borders(borders):
    east, west, north, south = borders
    return shifted(east, "gx", 1), shifted(west, "gx", -1), shifted(north, "gy", 1), shifted(south, "gy", -1)


def ring_call(kernel, tiles_x, tiles_y, rows, outs, scratch, name, hbm_in=0, hbm_out=False):
    smem = pl.BlockSpec(memory_space=pltpu.SMEM)
    vmem = pl.BlockSpec(memory_space=pltpu.VMEM)
    hbm = pl.BlockSpec(memory_space=pltpu.HBM)
    size = tiles_x * tiles_y * rows * LANES

    def call(owner_of_tile, *inputs):
        return pl.pallas_call(
            functools.partial(kernel, tiles_x=tiles_x, tiles_y=tiles_y),
            in_specs=[smem] + [hbm] * hbm_in + [vmem] * (len(inputs) - hbm_in),
            out_specs=hbm if hbm_out else [vmem] * len(outs),
            out_shape=outs[0] if hbm_out else outs,
            scratch_shapes=scratch,
            compiler_params=pltpu.CompilerParams(vmem_limit_bytes=32 << 20),
            cost_estimate=pl.CostEstimate(flops=16 * size, bytes_accessed=16 * size, transcendentals=0),
            name=name,
        )(owner_of_tile, *inputs)

    return call


def relay_strips(owner_of_tile, received, wind_send, wind_ring, settle_speed, bin_share, tiles_x, tiles_y):
    owners, both_rows, _ = received.shape
    rows = both_rows // 2
    per_home = tiles_x * tiles_y
    each = both_rows + ROWS
    ext = pltpu.VMEM(((tiles_x + 2) * (tiles_y + 2), rows, LANES), jnp.float32)
    all_rings = pltpu.VMEM((per_home, both_rows, LANES), jnp.float32)
    each_sem = pltpu.SemaphoreType.DMA((per_home,))
    settle_rows = jnp.broadcast_to(settle_speed[:, None], settle_speed.shape + (LANES,))
    share_rows = jnp.broadcast_to(bin_share[:, None], bin_share.shape + (LANES,))

    def call(kernel, outs, scratch, name, *inputs, **places):
        return ring_call(kernel, tiles_x, tiles_y, rows, outs, scratch, name, **places)(owner_of_tile, *inputs)

    along_x, along_y = tiles_y // 4, tiles_x // 4
    east, west, north, south = call(
        pack_borders_kernel,
        [f32(along_x * each, LANES)] * 2 + [f32(along_y * each, LANES)] * 2,
        [all_rings, each_sem],
        "pack_borders",
        in_hbm(received),
        wind_ring,
        hbm_in=1,
    )
    from_south, from_north = shifted(north, "gy", 1), shifted(south, "gy", -1)
    (rings,) = call(gather_rings_kernel, [f32(per_home, both_rows, LANES)], [], "gather_rings", received)
    east_full, west_full = call(
        add_corners_kernel,
        [f32(along_x * each + rows, LANES)] * 2,
        [],
        "add_corners",
        east, west, from_south, from_north,
    )
    from_west, from_east = shifted(east_full, "gx", 1), shifted(west_full, "gx", -1)
    wind_send, from_west, from_east = lax.optimization_barrier((wind_send, from_west, from_east))
    wind_recv = relay_rows(wind_send)
    seen_send = call(
        send_seen_kernel,
        [pltpu.HBM((owners, both_rows, LANES), jnp.float32)],
        [ext, all_rings]
        + [pltpu.VMEM((along_x, rows, LANES), jnp.float32)] * 2
        + [pltpu.VMEM((along_y, rows, LANES), jnp.float32)] * 2
        + [each_sem],
        "send_seen",
        rings, wind_ring, settle_rows, share_rows, east, west, north, south,
        from_west, from_east, from_south, from_north,
        hbm_out=True,
    )
    return wind_recv, relay_rows(seen_send)


def dust_kernel(home_ref, share_ref, settle_ref, dust_ref, shift_ref, wind_ref, *refs, block, bins, outer):
    if outer:
        side_ref, seen_ref, out_ref, coef, sides, edges, *work = refs
    else:
        out_ref, kept_ref, coef, *work = refs
    lanes = len(work) // 2
    step = pl.program_id(0)
    each = TZ * bins
    if outer:
        for j in range(block):
            edges[j] = seen_ref[home_ref[step * block + j]]
        spread = jnp.dot(
            jnp.concatenate(halves_of(edges[...].reshape(block * 2 * each, LANES)), axis=1),
            side_ref[...],
            preferred_element_type=jnp.float32,
        )
        for r in range(ROWS):
            sides[r] = spread[:, r * LANES : (r + 1) * LANES]

    _, lane = iotas()
    within = lane % TILE
    first_y, last_y = within == 0, within == TILE - 1
    low_lanes, high_lanes = lane < TILE, lane >= LANES - TILE
    mix = dust_step * diffusion
    chunks = bins // ROWS
    settle = [dust_step * settle_ref[h * ROWS : (h + 1) * ROWS, :] for h in range(chunks)]
    share = [share_ref[h * ROWS : (h + 1) * ROWS, :] for h in range(chunks)]

    def prepare(k, j):
        held = work[2 * k]
        home = home_ref[step * block + j]
        if not outer:
            kept_ref[j] = wind_ref[home]
        wind_at = j if outer else home
        plane = [wind_ref[wind_at, p * ROWS : (p + 1) * ROWS, :] * dust_step for p in range(PLANES)]
        for level in range(TZ):
            u, v = plane[level], plane[TZ + level]
            south_by = mix + jnp.maximum(v, 0.0)
            north_by = mix + jnp.maximum(-v, 0.0)
            coef[k, 0, level] = mix + jnp.maximum(u, 0.0)
            coef[k, 1, level] = mix + jnp.maximum(-u, 0.0)
            coef[k, 4, level] = 1.0 - 6.0 * mix - jnp.abs(u) - jnp.abs(v)
            coef[k, 5, level] = plane[2 * TZ + level]
            if outer:
                coef[k, 2, level] = south_by
                coef[k, 3, level] = north_by
                coef[k, 7, level] = jnp.where(first_y, south_by, jnp.where(last_y, north_by, 0.0))
            else:
                coef[k, 2, level] = jnp.where(first_y, 0.0, south_by)
                coef[k, 3, level] = jnp.where(last_y, 0.0, north_by)
        coef[k, 6, 0] = plane[PLANES - 1]
        for r in range(ROWS):
            for level in range(TZ):
                at = (r * TZ + level) * bins
                cells = dust_ref[j, pl.ds(r * TZ + level, bins, stride=ROWS * TZ), :]
                if not outer:
                    held[at : at + bins, :] = cells
                    continue
                for h in range(chunks):
                    edge_at = level * bins + h * ROWS
                    q = cells[h * ROWS : (h + 1) * ROWS]
                    q = q + spread_rows(coef[k, 7, level, r : r + 1, :]) * sides[r, pl.ds(j * 2 * each + edge_at, ROWS), :]
                    if r == 0 or r == ROWS - 1:
                        edge = edges[j, edge_at : edge_at + ROWS, :]
                        here = low_lanes if r == 0 else high_lanes
                        by = spread_rows(coef[k, 0 if r == 0 else 1, level, r : r + 1, :])
                        q = q + jnp.where(here, by * edge, 0.0)
                    held[at + h * ROWS : at + (h + 1) * ROWS, :] = q

    def shift(k):
        held, shifts = work[2 * k], work[2 * k + 1]
        shifts[...] = jnp.dot(
            jnp.concatenate(halves_of(held[...]), axis=1), shift_ref[...], preferred_element_type=jnp.float32
        )

    def update(k, j):
        held, shifts = work[2 * k], work[2 * k + 1]
        nothing = jnp.zeros((ROWS, LANES), jnp.float32)
        for r in range(ROWS):
            for h in range(chunks):
                cells = [held[(r * TZ + level) * bins + h * ROWS :][:ROWS] for level in range(TZ)]
                for level in range(TZ):
                    at = (r * TZ + level) * bins + h * ROWS
                    edge_at = each + level * bins + h * ROWS

                    def moved(which, rows_up=0):
                        first = at + rows_up * TZ * bins
                        return shifts[first : first + ROWS, which * LANES : (which + 1) * LANES]

                    def by(which):
                        return spread_rows(coef[k, which, level, r : r + 1, :])

                    edge = edges[j, edge_at : edge_at + ROWS, :] if outer else nothing
                    before = edge if r == 0 else moved(2, -1)
                    after = edge if r == ROWS - 1 else moved(3, 1)
                    south, north = moved(0), moved(1)
                    if outer:
                        side = sides[r, pl.ds(j * 2 * each + edge_at, ROWS), :]
                        south = jnp.where(first_y, side, south)
                        north = jnp.where(last_y, side, north)
                    west = jnp.where(low_lanes, before, moved(2))
                    east = jnp.where(high_lanes, after, moved(3))
                    rise = by(5) - settle[h]
                    up = jnp.maximum(rise, 0.0)
                    mixed = mix + (up - rise if level == 0 else up)
                    value = (
                        (by(4) - jnp.abs(rise)) * cells[level]
                        + by(0) * west
                        + by(1) * east
                        + by(2) * south
                        + by(3) * north
                        + mixed * cells[1 - level]
                    )
                    if level == 0:
                        value = value + spread_rows(coef[k, 6, 0, r : r + 1, :]) * share[h]
                    first = h * ROWS * ROWS * TZ + r * TZ + level
                    out_ref[j, pl.ds(first, ROWS, stride=ROWS * TZ), :] = value

    def some(i, carry):
        for k in range(lanes):
            prepare(k, i * lanes + k)
        for k in range(lanes):
            shift(k)
        for k in range(lanes):
            update(k, i * lanes + k)
        return carry

    lax.fori_loop(0, block // lanes, some, 0)


def dust_substep(home_of_slot, dust, wind, settle_speed, bin_share, seen_recv=None):
    slots, cells = dust.shape[:2]
    bins = settle_speed.shape[0]
    block = 8 if slots % 8 == 0 else 4
    lanes = 2
    outer = seen_recv is not None
    smem = pl.BlockSpec(memory_space=pltpu.SMEM)
    vmem = pl.BlockSpec(memory_space=pltpu.VMEM)
    tile = pl.BlockSpec((block, cells, LANES), lambda i: (i, 0, 0))
    settle = jnp.broadcast_to(settle_speed[:, None], (bins, LANES))
    share = jnp.broadcast_to(bin_share[:, None], (bins, LANES))
    wind_rows = pl.BlockSpec((block,) + wind.shape[1:], lambda i: (i, 0, 0))
    inputs = [home_of_slot, share, settle, in_hbm(dust), jnp.asarray(shift_matrix()), in_hbm(wind) if outer else wind]
    scratch = [pltpu.VMEM((lanes, PLANES + 1, TZ, ROWS, LANES), jnp.float32)]
    if outer:
        inputs += [jnp.asarray(side_matrix()), seen_recv]
        scratch += [
            pltpu.VMEM((ROWS, block * seen_recv.shape[1], LANES), jnp.float32),
            pltpu.VMEM((block,) + seen_recv.shape[1:], jnp.float32),
        ]
    out_shape = f32(*dust.shape)
    if not outer:
        out_shape = [pltpu.HBM(dust.shape, jnp.float32), pltpu.HBM((slots,) + wind.shape[1:], jnp.float32)]
    scratch += [pltpu.VMEM((cells, LANES), jnp.float32), pltpu.VMEM((cells, 4 * LANES), jnp.float32)] * lanes
    return pl.pallas_call(
        functools.partial(dust_kernel, block=block, bins=bins, outer=outer),
        grid=(slots // block,),
        in_specs=[smem, vmem, vmem, tile, vmem, wind_rows if outer else vmem] + [vmem] * (len(inputs) - 6),
        out_specs=tile if outer else [tile, wind_rows],
        out_shape=out_shape,
        scratch_shapes=scratch,
        compiler_params=pltpu.CompilerParams(vmem_limit_bytes=32 << 20),
        cost_estimate=pl.CostEstimate(flops=60 * dust.size, bytes_accessed=dust.size * 12, transcendentals=0),
        name="dust_outer" if outer else "dust_inner",
    )(*inputs)


def per_device(velocity, threshold, dust_mass, settle_speed, bin_share, active_tiles, tile_owner):
    owners = lax.axis_size(AXES)
    grid_cols = lax.axis_size("gy")
    self_index = lax.axis_index(AXES)
    slots, bins = dust_mass.shape[:2]
    tiles_x = velocity.shape[2] // TILE
    tiles_y = velocity.shape[3] // TILE
    per_home = tiles_x * tiles_y
    tiles_across = tiles_y * grid_cols

    tile_x = active_tiles // tiles_across
    tile_y = active_tiles % tiles_across
    home_dev = tile_x // tiles_x * grid_cols + tile_y // tiles_y
    local_tile = tile_x % tiles_x * tiles_y + tile_y % tiles_y
    own_slot = tile_owner - self_index * slots
    mine = jnp.where(home_dev == self_index, local_tile, -1)
    slot_ids = jnp.arange(slots, dtype=jnp.int32)
    home_of_slot = jnp.sum(jnp.where(own_slot[None, :] == slot_ids[:, None], home_dev[None, :], 0), axis=1)
    tile_ids = jnp.arange(per_home, dtype=jnp.int32)
    owner_of_tile = jnp.max(
        jnp.where(mine[None, :] == tile_ids[:, None], (tile_owner // slots)[None, :], -1), axis=1
    )

    dust = dust_mass.reshape(slots, bins, TZ, ROWS, LANES).transpose(0, 1, 3, 2, 4)
    dust = dust.reshape(slots, bins * ROWS * TZ, LANES)

    xlo, xhi, ylo, yhi = exchange_borders(wind_faces(velocity))

    strips_send = dust_strips(home_of_slot, dust, bins, owners)
    strips_send, xlo, xhi, ylo, yhi = lax.optimization_barrier((strips_send, xlo, xhi, ylo, yhi))
    strips = relay_rows(strips_send)
    new_velocity, wind_send, wind_ring = wind_step(
        owner_of_tile, velocity, xlo, xhi, ylo, yhi, threshold, owners
    )
    strips, wind_send, wind_ring = lax.optimization_barrier((strips, wind_send, wind_ring))
    wind_recv, seen_recv = relay_strips(
        owner_of_tile, strips, wind_send, wind_ring, settle_speed, bin_share, tiles_x, tiles_y
    )
    inner, wind_held = dust_substep(home_of_slot, dust, wind_recv, settle_speed, bin_share)
    out = dust_substep(home_of_slot, inner, wind_held, settle_speed, bin_share, seen_recv)
    out = out.reshape(slots, bins, ROWS, TZ, LANES).transpose(0, 1, 3, 2, 4).reshape(dust_mass.shape)
    return new_velocity, out


def solution(mesh):
    in_specs = (
        P(None, None, "gx", "gy"),
        P("gx", "gy"),
        P(AXES, None, None, None),
        P(),
        P(),
        P(),
        P(),
    )
    out_specs = (P(None, None, "gx", "gy"), P(AXES, None, None, None))
    return jax.shard_map(
        per_device, mesh=mesh, in_specs=in_specs, out_specs=out_specs, check_vma=False
    )
```

```python
import functools

import jax
import jax.numpy as jnp
import ml_dtypes
import numpy as np
from jax import lax
from jax.experimental import pallas as pl
from jax.experimental.pallas import tpu as pltpu
from jax.sharding import PartitionSpec as P

TZ = 2
TILE = 32
LANES = 128
ROWS = TILE * TILE // LANES
PLANES = 7
AXES = ("gx", "gy")

time_step = 0.1
viscosity = 0.2
dust_step = 0.1
diffusion = 0.1
roughness = 0.5
emit_rate = 0.5

WEST, SOUTH, NORTH, EAST = range(4)


def iotas(shape=(ROWS, LANES)):
    return lax.broadcasted_iota(jnp.int32, shape, 0), lax.broadcasted_iota(jnp.int32, shape, 1)


def lane_gather(x, index):
    return jnp.take_along_axis(x, index, axis=1)


def ring_pattern(depth):
    row, lane = iotas()
    group, within = lane // TILE, lane % TILE
    side = jnp.where(group == SOUTH, depth, TILE - 1 - depth)
    index = (within % 4) * TILE + side
    index = jnp.where(group == WEST, depth * TILE + within, index)
    index = jnp.where(group == EAST, (3 - depth) * TILE + within, index)
    source = jnp.where(group == WEST, 0, jnp.where(group == EAST, ROWS - 1, within // 4))
    return index, row == source


def ring_of(x, pattern):
    index, taken = pattern
    return jnp.sum(jnp.where(taken, lane_gather(x, index), 0.0), axis=0, keepdims=True)


def spread_rows(row):
    return jnp.broadcast_to(row, (ROWS, LANES))


def f32(*shape):
    return jax.ShapeDtypeStruct(shape, jnp.float32)


def in_hbm(x):
    return pltpu.with_memory_space_constraint(x, pltpu.HBM)


def halves_of(x):
    high = x.astype(jnp.bfloat16)
    return high, (x - high.astype(jnp.float32)).astype(jnp.bfloat16)


def moves(sources, width=LANES):
    lanes = np.arange(width)[:, None]
    once = (lanes == np.asarray(sources)[None, :]).astype(ml_dtypes.bfloat16)
    return np.concatenate([once, once], axis=0)


def ring_matrix():
    lane = np.arange(LANES)
    group, within = lane // TILE, lane % TILE
    blocks = []
    for r in range(ROWS):
        columns = []
        for depth in range(2):
            side = np.where(group == SOUTH, depth, TILE - 1 - depth)
            source = np.where(within // 4 == r, (within % 4) * TILE + side, -1)
            source = np.where(group == WEST, depth * TILE + within if r == 0 else -1, source)
            source = np.where(group == EAST, (3 - depth) * TILE + within if r == ROWS - 1 else -1, source)
            columns.append(source)
        blocks.append(moves(np.concatenate(columns)))
    return np.concatenate(blocks, axis=0)


def shift_matrix():
    lane = np.arange(LANES)
    return moves(np.concatenate([(lane + d) % LANES for d in (-1, 1, -TILE, TILE)]))


def spread_matrix():
    i, j = np.divmod(np.arange(TILE * TILE), TILE)
    source = np.full(TILE * TILE, -1)
    for depth in (1, 0):
        at = depth * LANES
        source = np.where(j == depth, at + SOUTH * TILE + i, source)
        source = np.where(j == TILE - 1 - depth, at + NORTH * TILE + i, source)
        source = np.where(i == depth, at + WEST * TILE + j, source)
        source = np.where(i == TILE - 1 - depth, at + EAST * TILE + j, source)
    return moves(source, 2 * LANES)


def strips_kernel(home_ref, dust_hbm, matrix_ref, send_ref, dust, rings, load_sems, sems, *, block, bins):
    slots = rings.shape[0]
    each = TZ * bins

    def load(i):
        some = pl.ds(i * block, block)
        return pltpu.make_async_copy(dust_hbm.at[some], dust.at[some], load_sems.at[i])

    def send(s):
        return pltpu.make_async_copy(rings.at[s], send_ref.at[home_ref[s]], sems.at[s])

    for i in range(slots // block):
        load(i).start()

    def one(i, carry):
        load(i).wait()
        parts = []
        for r in range(ROWS):
            x = jnp.concatenate(
                [
                    dust[i * block + j, pl.ds(r * TZ + level, bins, stride=ROWS * TZ), :]
                    for j in range(block)
                    for level in range(TZ)
                ],
                axis=0,
            )
            parts += halves_of(x)
        found = jnp.dot(
            jnp.concatenate(parts, axis=1), matrix_ref[...], preferred_element_type=jnp.float32
        )
        for j in range(block):
            for depth in range(2):
                rings[i * block + j, depth * each : (depth + 1) * each, :] = found[
                    j * each : (j + 1) * each, depth * LANES : (depth + 1) * LANES
                ]
            send(i * block + j).start()
        return carry

    lax.fori_loop(0, slots // block, one, 0)

    def wait(s, carry):
        send(s).wait()
        return carry

    lax.fori_loop(0, slots, wait, 0)


def dust_strips(home_of_slot, dust, bins, owners):
    slots, cells = dust.shape[:2]
    block = 8 if slots % 8 == 0 else 4
    rows = 2 * bins * TZ
    matrix = jnp.asarray(ring_matrix())
    hbm = pl.BlockSpec(memory_space=pltpu.HBM)
    return pl.pallas_call(
        functools.partial(strips_kernel, block=block, bins=bins),
        in_specs=[pl.BlockSpec(memory_space=pltpu.SMEM), hbm, pl.BlockSpec(memory_space=pltpu.VMEM)],
        out_specs=hbm,
        out_shape=pltpu.HBM((owners, rows, LANES), jnp.float32),
        scratch_shapes=[
            pltpu.VMEM(dust.shape, jnp.float32),
            pltpu.VMEM((slots, rows, LANES), jnp.float32),
            pltpu.SemaphoreType.DMA((slots // block,)),
            pltpu.SemaphoreType.DMA((slots,)),
        ],
        compiler_params=pltpu.CompilerParams(vmem_limit_bytes=32 << 20),
        cost_estimate=pl.CostEstimate(
            flops=20 * dust.size, bytes_accessed=dust.size * 4 + slots * rows * LANES * 4, transcendentals=0
        ),
        name="dust_strips",
    )(home_of_slot, in_hbm(dust), matrix)


def faces_kernel(vel_ref, x_last_ref, x_first_ref, y_last_ref, y_first_ref, first, last, low, high, x_sems, y_sems):
    fields, nx, ny = vel_ref.shape
    x_copies = [
        pltpu.make_async_copy(vel_ref.at[:, pl.ds(0, ROWS), :], first, x_sems.at[0]),
        pltpu.make_async_copy(vel_ref.at[:, pl.ds(nx - ROWS, ROWS), :], last, x_sems.at[1]),
    ]
    y_copies = [
        (
            pltpu.make_async_copy(vel_ref.at[f, :, pl.ds(0, LANES)], low.at[f], y_sems.at[0, f]),
            pltpu.make_async_copy(vel_ref.at[f, :, pl.ds(ny - LANES, LANES)], high.at[f], y_sems.at[1, f]),
        )
        for f in range(fields)
    ]
    for pair in y_copies:
        for copy in pair:
            copy.start()
    for copy in x_copies:
        copy.start()
    lane = lax.broadcasted_iota(jnp.int32, (nx, LANES), 1)
    for f, (low_copy, high_copy) in enumerate(y_copies):
        low_copy.wait()
        high_copy.wait()
        from_low = pltpu.roll(low[f], f, 1) if f else low[f]
        from_high = pltpu.roll(high[f], f + 1, 1)
        if f == 0:
            y_first_ref[...], y_last_ref[...] = from_low, from_high
        else:
            y_first_ref[...] = jnp.where(lane == f, from_low, y_first_ref[...])
            y_last_ref[...] = jnp.where(lane == f, from_high, y_last_ref[...])
    for copy in x_copies:
        copy.wait()
    for f in range(fields):
        x_first_ref[f : f + 1, :] = first[f, 0:1, :]
        x_last_ref[f : f + 1, :] = last[f, ROWS - 1 : ROWS, :]


def wind_faces(velocity):
    comps, levels, nx, ny = velocity.shape
    fields = comps * levels
    vmem = pl.BlockSpec(memory_space=pltpu.VMEM)
    return pl.pallas_call(
        faces_kernel,
        in_specs=[pl.BlockSpec(memory_space=pltpu.HBM)],
        out_specs=[vmem] * 4,
        out_shape=[f32(fields, ny)] * 2 + [f32(nx, LANES)] * 2,
        scratch_shapes=[
            pltpu.VMEM((fields, ROWS, ny), jnp.float32),
            pltpu.VMEM((fields, ROWS, ny), jnp.float32),
            pltpu.VMEM((fields, nx, LANES), jnp.float32),
            pltpu.VMEM((fields, nx, LANES), jnp.float32),
            pltpu.SemaphoreType.DMA((2,)),
            pltpu.SemaphoreType.DMA((2, fields)),
        ],
        compiler_params=pltpu.CompilerParams(vmem_limit_bytes=32 << 20),
        cost_estimate=pl.CostEstimate(flops=velocity.size, bytes_accessed=velocity.size * 4, transcendentals=0),
        name="wind_faces",
    )(in_hbm(velocity.reshape(fields, nx, ny)))


def wind_kernel(
    owner_ref, vel_ref, xlo_ref, xhi_ref, ylo_ref, yhi_ref, thr_ref,
    new_ref, send_ref, ring_ref, padded, strip, tiles, load_sem, sems, *, levels
):
    fields, nx, ny = new_ref.shape
    load = pltpu.make_async_copy(vel_ref, padded.at[:, pl.ds(8, nx), :], load_sem)
    load.start()
    load.wait()
    for f in range(fields):
        padded[f, 7:8, :] = xlo_ref[f : f + 1, :]
        padded[f, 8 + nx : 9 + nx, :] = xhi_ref[f : f + 1, :]
    half = 16
    halves = ny // LANES
    tiles_y = ny // TILE
    patterns = [ring_pattern(0), ring_pattern(1)]
    _, lane8 = iotas()
    group = lane8 // TILE

    def one_strip(ix, carry):
        for sub in range(TILE // half):
            base = pl.multiple_of(ix * TILE + sub * half, 8)
            lane = lax.broadcasted_iota(jnp.int32, (half, ny), 1)
            low = {}
            faces = [ref[pl.ds(base, half), :] for ref in (ylo_ref, yhi_ref)]

            def face(which, f, to):
                moved = pltpu.roll(faces[which], (to - f) % LANES, 1) if f != to else faces[which]
                return jnp.concatenate([moved] * halves, axis=1)

            for z in range(levels):
                u, v, w = (padded[c * levels + z, pl.ds(base + 8, half), :] for c in range(3))
                for c in range(3):
                    f = c * levels + z
                    block = padded[f, pl.ds(base, half + 16), :]
                    centre = (u, v, w)[c]
                    west = pltpu.roll(block, 1, 0)[8 : 8 + half]
                    east = pltpu.roll(block, half + 15, 0)[8 : 8 + half]
                    south = jnp.where(lane == 0, face(0, f, 0), pltpu.roll(centre, 1, 1))
                    north = jnp.where(lane == ny - 1, face(1, f, LANES - 1), pltpu.roll(centre, ny - 1, 1))
                    lower = -centre if z == 0 else padded[f - 1, pl.ds(base + 8, half), :]
                    upper = centre if z == levels - 1 else padded[f + 1, pl.ds(base + 8, half), :]
                    carried = 0.5 * (u * (east - west) + v * (north - south) + w * (upper - lower))
                    spread = east + west + north + south + upper + lower - 6.0 * centre
                    new = centre + time_step * (viscosity * spread - carried)
                    new_ref[f, pl.ds(base, half), :] = new
                    if z < TZ:
                        low[c * TZ + z] = new
            stress = roughness * (low[0] * low[0] + low[TZ] * low[TZ])
            low[PLANES - 1] = emit_rate * stress * jnp.maximum(
                stress - thr_ref[pl.ds(base, half), :], 0.0
            )
            for p in range(PLANES):
                for h in range(halves):
                    strip[p * halves + h, sub * half : (sub + 1) * half, :] = low[p][
                        :, h * LANES : (h + 1) * LANES
                    ]
        for p in range(PLANES):
            for h in range(halves):
                parts = [strip[p * halves + h, pl.ds(k, ROWS, stride=4), :] for k in range(4)]
                for t in range(4):
                    tile = ix * tiles_y + h * 4 + t
                    cells = pltpu.roll(parts[0], (-t * TILE) % LANES, 1) if t else parts[0]
                    for k in range(1, 4):
                        moved = pltpu.roll(parts[k], ((k - t) * TILE) % LANES, 1) if k != t else parts[k]
                        cells = jnp.where(group == k, moved, cells)
                    tiles[tile, p * ROWS : (p + 1) * ROWS, :] = cells
                    for depth in range(2):
                        ring_ref[tile, depth * 8 + p : depth * 8 + p + 1, :] = ring_of(cells, patterns[depth])

        def send(t, inner):
            tile = ix * tiles_y + t
            owner = owner_ref[tile]

            @pl.when(owner >= 0)
            def _():
                pltpu.make_async_copy(tiles.at[tile], send_ref.at[owner], sems.at[tile]).start()

            return inner

        lax.fori_loop(0, tiles_y, send, 0)
        return carry

    lax.fori_loop(0, nx // TILE, one_strip, 0)

    def wait(tile, carry):
        owner = owner_ref[tile]

        @pl.when(owner >= 0)
        def _():
            pltpu.make_async_copy(tiles.at[tile], send_ref.at[owner], sems.at[tile]).wait()

        return carry

    lax.fori_loop(0, tiles.shape[0], wait, 0)


def wind_step(owner_of_tile, velocity, xlo, xhi, ylo, yhi, threshold, owners):
    comps, levels, nx, ny = velocity.shape
    fields = comps * levels
    per_home = (nx // TILE) * (ny // TILE)
    smem = pl.BlockSpec(memory_space=pltpu.SMEM)
    hbm = pl.BlockSpec(memory_space=pltpu.HBM)
    vmem = pl.BlockSpec(memory_space=pltpu.VMEM)
    new, send, ring = pl.pallas_call(
        functools.partial(wind_kernel, levels=levels),
        in_specs=[smem, hbm, vmem, vmem, vmem, vmem, vmem],
        out_specs=[vmem, hbm, vmem],
        out_shape=[
            f32(fields, nx, ny),
            pltpu.HBM((owners, PLANES * ROWS, LANES), jnp.float32),
            f32(per_home, 16, LANES),
        ],
        scratch_shapes=[
            pltpu.VMEM((fields, nx + 16, ny), jnp.float32),
            pltpu.VMEM((PLANES * (ny // LANES), TILE, LANES), jnp.float32),
            pltpu.VMEM((per_home, PLANES * ROWS, LANES), jnp.float32),
            pltpu.SemaphoreType.DMA,
            pltpu.SemaphoreType.DMA((per_home,)),
        ],
        compiler_params=pltpu.CompilerParams(vmem_limit_bytes=40 << 20),
        cost_estimate=pl.CostEstimate(
            flops=40 * velocity.size, bytes_accessed=velocity.size * 10, transcendentals=0
        ),
        name="wind_step",
    )(
        owner_of_tile,
        in_hbm(velocity.reshape(fields, nx, ny)),
        xlo,
        xhi,
        ylo,
        yhi,
        threshold,
    )
    return new.reshape(velocity.shape), send, ring


def border_tiles(tiles_x, tiles_y):
    return (
        (EAST, [(tiles_x - 1) * tiles_y + n for n in range(tiles_y)]),
        (WEST, [n for n in range(tiles_y)]),
        (NORTH, [n * tiles_y + tiles_y - 1 for n in range(tiles_x)]),
        (SOUTH, [n * tiles_y for n in range(tiles_x)]),
    )


def fill_halo(ext, strips, tiles_x, tiles_y):
    wide = tiles_y + 2
    for strip_of, side, places in (
        (strips[0], EAST, [n + 1 for n in range(tiles_y)]),
        (strips[1], WEST, [(tiles_x + 1) * wide + n + 1 for n in range(tiles_y)]),
        (strips[2], NORTH, [(n + 1) * wide for n in range(tiles_x)]),
        (strips[3], SOUTH, [(n + 1) * wide + tiles_y + 1 for n in range(tiles_x)]),
    ):
        for n, place in enumerate(places):
            strip = strip_of(n // 4)
            if n % 4 != side:
                strip = pltpu.roll(strip, ((side - n % 4) * TILE) % LANES, 1)
            ext[place] = strip


def seen_by(ext, place, wide):
    west, east = ext[place - wide], ext[place + wide]
    south, north = ext[place - 1], ext[place + 1]
    lane = lax.broadcasted_iota(jnp.int32, west.shape, 1)
    up = pltpu.roll(jnp.where(lane < 2 * TILE, north, west), TILE, 1)
    down = pltpu.roll(jnp.where(lane < 2 * TILE, east, south), LANES - TILE, 1)
    return jnp.where((lane // TILE) % 2 == 0, up, down)


FLAG = 7


def pack_borders_kernel(owner_ref, recv_ref, wind_ref, *refs, tiles_x, tiles_y):
    *outs, rings, sems = refs
    both_rows = rings.shape[1]
    borders = border_tiles(tiles_x, tiles_y)
    used = sorted({t for _, tiles in borders for t in tiles})

    def copy(t):
        return pltpu.make_async_copy(recv_ref.at[owner_ref[t]], rings.at[t], sems.at[t])

    for t in used:

        @pl.when(owner_ref[t] >= 0)
        def _():
            copy(t).start()

        @pl.when(owner_ref[t] < 0)
        def _():
            rings[t] = jnp.zeros(rings.shape[1:], jnp.float32)

    for t in used:

        @pl.when(owner_ref[t] >= 0)
        def _():
            copy(t).wait()

    lane = lax.broadcasted_iota(jnp.int32, (both_rows, LANES), 1) // TILE
    row8, lane8 = iotas()
    group8 = lane8 // TILE
    for out, (side, tiles) in zip(outs, borders):
        for g in range(len(tiles) // 4):
            strips = winds = None
            for q in range(4):
                t = tiles[4 * g + q]
                strip, wind = rings[t], wind_ref[t, :ROWS, :]
                if q != side:
                    strip = pltpu.roll(strip, ((q - side) * TILE) % LANES, 1)
                    wind = pltpu.roll(wind, ((q - side) * TILE) % LANES, 1)
                wind = jnp.where(row8 == FLAG, jnp.where(owner_ref[t] >= 0, 1.0, 0.0), wind)
                strips = strip if strips is None else jnp.where(lane == q, strip, strips)
                winds = wind if winds is None else jnp.where(group8 == q, wind, winds)
            at = g * (both_rows + ROWS)
            out[at : at + both_rows, :] = strips
            out[at + both_rows : at + both_rows + ROWS, :] = winds


def add_corners_kernel(owner_ref, e_ref, w_ref, fs_ref, fn_ref, e_out, w_out, *, tiles_x, tiles_y):
    size = e_ref.shape[0]
    rows = e_out.shape[0] - size
    last = fs_ref.shape[0] - (2 * rows + ROWS)
    lane = lax.broadcasted_iota(jnp.int32, (rows, LANES), 1)
    e_out[:size, :] = e_ref[...]
    w_out[:size, :] = w_ref[...]
    e_out[size:, :] = jnp.where(
        lane == 0, pltpu.roll(fs_ref[last : last + rows, :], 1, 1), fn_ref[last : last + rows, :]
    )
    w_out[size:, :] = jnp.where(lane == 0, fs_ref[:rows, :], pltpu.roll(fn_ref[:rows, :], LANES - 1, 1))


def gather_rings_kernel(owner_ref, recv_ref, rings_ref, *, tiles_x, tiles_y):
    def one(t, carry):
        owner = owner_ref[t]
        rings = recv_ref[jnp.maximum(owner, 0)]
        rings_ref[t] = jnp.where(owner >= 0, rings, 0.0)
        return carry

    lax.fori_loop(0, tiles_x * tiles_y, one, 0)


def fill_tiles(ext, tile, tiles_x, tiles_y):
    def inner(t, carry):
        ext[place_of(t, tiles_y)] = tile(t)
        return carry

    lax.fori_loop(0, tiles_x * tiles_y, inner, 0)


def place_of(t, tiles_y):
    return (t // tiles_y + 1) * (tiles_y + 2) + t % tiles_y + 1


def corner_index(inset):
    _, lane = iotas()
    group, within = lane // TILE, lane % TILE
    on_x = (group == WEST) | (group == EAST)
    low = within < TILE // 2
    along = jnp.where((group == EAST) | (group == NORTH), TILE - 1 - inset, inset)
    return jnp.where(on_x, jnp.where(low, SOUTH, NORTH), jnp.where(low, WEST, EAST)) * TILE + along


def ring_effect(t, wind_ref, settle_ref, seen, seen_later):
    row, lane = iotas()
    group, within = lane // TILE, lane % TILE
    on_x = (group == WEST) | (group == EAST)
    low_side = (group == WEST) | (group == SOUTH)
    first, last = within == 0, within == TILE - 1
    second, last_but_one = within == 1, within == TILE - 2
    corner, inner = corner_index(0), corner_index(1)
    rows = seen.shape[0]
    bins = rows // TZ
    mix = dust_step * diffusion

    def wind(depth, p):
        return dust_step * spread_rows(wind_ref[t, depth * 8 + p : depth * 8 + p + 1, :])

    inflow, later_in = [], []
    coefs = []
    for level in range(TZ):
        u, v, w = (wind(0, c * TZ + level) for c in range(3))
        across, along = jnp.where(on_x, u, v), jnp.where(on_x, v, u)
        outward = jnp.where(low_side, across, -across)
        from_out = mix + jnp.maximum(outward, 0.0)
        from_in = jnp.where(first | last, mix + jnp.maximum(-outward, 0.0), 0.0)
        from_before, from_after = mix + jnp.maximum(along, 0.0), mix + jnp.maximum(-along, 0.0)
        from_corner = jnp.where(first, from_before, jnp.where(last, from_after, 0.0))
        from_before = jnp.where(first, 0.0, from_before)
        from_after = jnp.where(last, 0.0, from_after)
        keep = 1.0 - 6.0 * mix - jnp.abs(u) - jnp.abs(v)
        u2, v2 = (wind(1, c * TZ + level) for c in range(2))
        across2, along2 = jnp.where(on_x, u2, v2), jnp.where(on_x, v2, u2)
        deep_out = mix + jnp.maximum(jnp.where(low_side, across2, -across2), 0.0)
        deep_corner = jnp.where(
            second, mix + jnp.maximum(along2, 0.0), jnp.where(last_but_one, mix + jnp.maximum(-along2, 0.0), 0.0)
        )
        coefs.append((w, keep, from_in, from_before, from_after, deep_out, deep_corner))
        for at in range(level * bins, (level + 1) * bins, ROWS):
            for view, taken in ((seen, inflow), (seen_later, later_in)):
                g = view[at : at + ROWS, :]
                taken.append(from_out * g + from_corner * lane_gather(g, corner))
    outer, deep = [], []
    for n, e in enumerate(inflow):
        level, bin_at = n * ROWS // bins, n * ROWS % bins
        w, keep, from_in, from_before, from_after, deep_out, deep_corner = coefs[level]
        other = inflow[n + len(inflow) // 2 if level == 0 else n - len(inflow) // 2]
        rise = w - dust_step * settle_ref[bin_at : bin_at + ROWS, :]
        up = jnp.maximum(rise, 0.0)
        down = up - rise
        turned = lane_gather(e, inner)
        outer.append(
            (keep - up - down) * e
            + from_before * pltpu.roll(e, 1, 1)
            + from_after * pltpu.roll(e, LANES - 1, 1)
            + from_in * turned
            + (mix + (down if level == 0 else up)) * other
            + later_in[n]
        )
        deep.append(deep_out * e + deep_corner * turned)
    return outer, deep


def advance_ring(t, owner_ref, rings_ref, wind_ref, settle_ref, share_ref, seen):
    _, lane = iotas()
    group, within = lane // TILE, lane % TILE
    on_x = (group == WEST) | (group == EAST)
    first, last = within == 0, within == TILE - 1
    corner = corner_index(0)
    rows = rings_ref.shape[1] // 2
    bins = rows // TZ
    uplift = dust_step * spread_rows(wind_ref[t, PLANES - 1 : PLANES, :])
    mix = dust_step * diffusion
    active = owner_ref[t] >= 0
    chunks = []
    for at in range(0, rows, ROWS):
        level, bin_at = at // bins, at % bins
        if bin_at == 0:
            u, v, w = (
                dust_step * spread_rows(wind_ref[t, c * TZ + level : c * TZ + level + 1, :]) for c in range(3)
            )
            from_west = mix + jnp.maximum(u, 0.0)
            from_east = mix + jnp.maximum(-u, 0.0)
            from_south = mix + jnp.maximum(v, 0.0)
            from_north = mix + jnp.maximum(-v, 0.0)
            keep = 1.0 - 6.0 * mix - jnp.abs(u) - jnp.abs(v)
        q = rings_ref[t, at : at + ROWS, :]
        deep = rings_ref[t, rows + at : rows + at + ROWS, :]
        out = seen[at : at + ROWS, :]
        beyond = lane_gather(out, corner)
        before = jnp.where(first, beyond, pltpu.roll(q, 1, 1))
        after = jnp.where(last, beyond, pltpu.roll(q, LANES - 1, 1))
        west = jnp.where(group == WEST, out, jnp.where(group == EAST, deep, before))
        east = jnp.where(group == WEST, deep, jnp.where(group == EAST, out, after))
        south = jnp.where(on_x, before, jnp.where(group == SOUTH, out, deep))
        north = jnp.where(on_x, after, jnp.where(group == SOUTH, deep, out))
        other_at = (1 - level) * bins + bin_at
        other = rings_ref[t, other_at : other_at + ROWS, :]
        rise = w - dust_step * settle_ref[bin_at : bin_at + ROWS, :]
        up = jnp.maximum(rise, 0.0)
        down = up - rise
        new = (
            (keep - up - down) * q
            + from_west * west
            + from_east * east
            + from_south * south
            + from_north * north
            + (mix + (down if level == 0 else up)) * other
        )
        if level == 0:
            new = new + uplift * share_ref[bin_at : bin_at + ROWS, :]
        chunks.append(jnp.where(active, new, 0.0))
    return chunks


def advance_strip(side, message, ours, low_end, high_end, settle_ref, share_ref, out, rows):
    _, lane = iotas()
    bins = rows // TZ
    each = 2 * rows + ROWS
    groups = out.shape[0]
    mix = dust_step * diffusion
    for g in range(groups):
        wind_at = g * each + 2 * rows

        def wind_row(p):
            return spread_rows(message[wind_at + p : wind_at + p + 1, :])

        for at in range(0, rows, ROWS):
            level, bin_at = at // bins, at % bins
            u, v, w = (dust_step * wind_row(c * TZ + level) for c in range(3))

            def cells(group, first):
                return message[group * each + first : group * each + first + ROWS, :]

            q = cells(g, at)
            deep = cells(g, rows + at)
            near = ours[g * each + at : g * each + at + ROWS, :]
            low = low_end(at) if g == 0 else pltpu.roll(cells(g - 1, at), 1, 1)
            high = high_end(at) if g == groups - 1 else pltpu.roll(cells(g + 1, at), LANES - 1, 1)
            before = jnp.where(lane == 0, low, pltpu.roll(q, 1, 1))
            after = jnp.where(lane == LANES - 1, high, pltpu.roll(q, LANES - 1, 1))
            across = (deep, near) if side in (WEST, SOUTH) else (near, deep)
            (west, east), (south, north) = (
                (across, (before, after)) if side in (WEST, EAST) else ((before, after), across)
            )
            other = cells(g, (1 - level) * bins + bin_at)
            rise = w - dust_step * settle_ref[bin_at : bin_at + ROWS, :]
            up = jnp.maximum(rise, 0.0)
            down = up - rise
            new = (
                (1.0 - 6.0 * mix - jnp.abs(u) - jnp.abs(v) - up - down) * q
                + (mix + jnp.maximum(u, 0.0)) * west
                + (mix + jnp.maximum(-u, 0.0)) * east
                + (mix + jnp.maximum(v, 0.0)) * south
                + (mix + jnp.maximum(-v, 0.0)) * north
                + (mix + (down if level == 0 else up)) * other
            )
            if level == 0:
                new = new + dust_step * wind_row(PLANES - 1) * share_ref[bin_at : bin_at + ROWS, :]
            out[g, at : at + ROWS, :] = jnp.where(wind_row(FLAG) > 0.0, new, 0.0)


def send_seen_kernel(
    owner_ref, rings_ref, wind_ref, settle_ref, share_ref, e_ref, w_ref, n_ref, s_ref, fw_ref, fe_ref, fs_ref, fn_ref,
    send_ref, ext, both, lw_ref, le_ref, ls_ref, ln_ref, sems, *, tiles_x, tiles_y
):
    rows = rings_ref.shape[1] // 2
    wide = tiles_y + 2
    each = 2 * rows + ROWS
    messages = (fw_ref, fe_ref, fs_ref, fn_ref)
    later = (lw_ref, le_ref, ls_ref, ln_ref)

    def place(t):
        return place_of(t, tiles_y)

    fill_halo(
        ext, [lambda g, m=m: m[g * each : g * each + rows, :] for m in messages], tiles_x, tiles_y
    )
    fill_tiles(ext, lambda t: rings_ref[t, :rows, :], tiles_x, tiles_y)

    def before(t, carry):
        both[t, :rows, :] = seen_by(ext, place(t), wide)
        return carry

    lax.fori_loop(0, tiles_x * tiles_y, before, 0)

    def advance(i, carry):
        for t in (2 * i, 2 * i + 1):
            chunks = advance_ring(t, owner_ref, rings_ref, wind_ref, settle_ref, share_ref, both[t, :rows, :])
            for n, chunk in enumerate(chunks):
                ext[place(t), n * ROWS : (n + 1) * ROWS, :] = chunk
        return carry

    lax.fori_loop(0, tiles_x * tiles_y // 2, advance, 0)

    def corner(ref, shift):
        first = ref.shape[0] - rows

        def of(at):
            cells = ref[first + at : first + at + ROWS, :]
            return pltpu.roll(cells, shift, 1) if shift else cells

        return of

    ends = (
        (corner(fw_ref, 0), corner(fw_ref, 0)),
        (corner(fe_ref, 0), corner(fe_ref, 0)),
        (corner(fw_ref, 0), corner(fe_ref, LANES - 1)),
        (corner(fw_ref, 1), corner(fe_ref, 0)),
    )
    for side, message, ours, (low, high), out in zip(
        (WEST, EAST, SOUTH, NORTH), messages, (w_ref, e_ref, s_ref, n_ref), ends, later
    ):
        advance_strip(side, message, ours, low, high, settle_ref, share_ref, out, rows)
    fill_halo(ext, [lambda g, m=m: m[g] for m in later], tiles_x, tiles_y)

    def copy(t):
        return pltpu.make_async_copy(both.at[t], send_ref.at[owner_ref[t]], sems.at[t])

    def after(t, carry):
        effect = ring_effect(t, wind_ref, settle_ref, both[t, :rows, :], seen_by(ext, place(t), wide))
        for depth, chunks in enumerate(effect):
            for n, chunk in enumerate(chunks):
                both[t, depth * rows + n * ROWS : depth * rows + (n + 1) * ROWS, :] = chunk

        @pl.when(owner_ref[t] >= 0)
        def _():
            copy(t).start()

        return carry

    lax.fori_loop(0, tiles_x * tiles_y, after, 0)

    def wait(t, carry):
        @pl.when(owner_ref[t] >= 0)
        def _():
            copy(t).wait()

        return carry

    lax.fori_loop(0, tiles_x * tiles_y, wait, 0)


def shifted(value, axis, steps):
    count = lax.axis_size(axis)
    return lax.ppermute(value, axis, [(source, (source + steps) % count) for source in range(count)])


def relay_rows(rows):
    return lax.all_to_all(rows, AXES, split_axis=0, concat_axis=0, tiled=True)


def exchange_borders(borders):
    east, west, north, south = borders
    return shifted(east, "gx", 1), shifted(west, "gx", -1), shifted(north, "gy", 1), shifted(south, "gy", -1)


def ring_call(kernel, tiles_x, tiles_y, rows, outs, scratch, name, hbm_in=0, hbm_out=False):
    smem = pl.BlockSpec(memory_space=pltpu.SMEM)
    vmem = pl.BlockSpec(memory_space=pltpu.VMEM)
    hbm = pl.BlockSpec(memory_space=pltpu.HBM)
    size = tiles_x * tiles_y * rows * LANES

    def call(owner_of_tile, *inputs):
        return pl.pallas_call(
            functools.partial(kernel, tiles_x=tiles_x, tiles_y=tiles_y),
            in_specs=[smem] + [hbm] * hbm_in + [vmem] * (len(inputs) - hbm_in),
            out_specs=hbm if hbm_out else [vmem] * len(outs),
            out_shape=outs[0] if hbm_out else outs,
            scratch_shapes=scratch,
            compiler_params=pltpu.CompilerParams(vmem_limit_bytes=32 << 20),
            cost_estimate=pl.CostEstimate(flops=16 * size, bytes_accessed=16 * size, transcendentals=0),
            name=name,
        )(owner_of_tile, *inputs)

    return call


def relay_strips(owner_of_tile, received, wind_send, wind_ring, settle_speed, bin_share, tiles_x, tiles_y):
    owners, both_rows, _ = received.shape
    rows = both_rows // 2
    per_home = tiles_x * tiles_y
    each = both_rows + ROWS
    ext = pltpu.VMEM(((tiles_x + 2) * (tiles_y + 2), rows, LANES), jnp.float32)
    all_rings = pltpu.VMEM((per_home, both_rows, LANES), jnp.float32)
    each_sem = pltpu.SemaphoreType.DMA((per_home,))
    settle_rows = jnp.broadcast_to(settle_speed[:, None], settle_speed.shape + (LANES,))
    share_rows = jnp.broadcast_to(bin_share[:, None], bin_share.shape + (LANES,))

    def call(kernel, outs, scratch, name, *inputs, **places):
        return ring_call(kernel, tiles_x, tiles_y, rows, outs, scratch, name, **places)(owner_of_tile, *inputs)

    along_x, along_y = tiles_y // 4, tiles_x // 4
    east, west, north, south = call(
        pack_borders_kernel,
        [f32(along_x * each, LANES)] * 2 + [f32(along_y * each, LANES)] * 2,
        [all_rings, each_sem],
        "pack_borders",
        in_hbm(received),
        wind_ring,
        hbm_in=1,
    )
    from_south, from_north = shifted(north, "gy", 1), shifted(south, "gy", -1)
    (rings,) = call(gather_rings_kernel, [f32(per_home, both_rows, LANES)], [], "gather_rings", received)
    east_full, west_full = call(
        add_corners_kernel,
        [f32(along_x * each + rows, LANES)] * 2,
        [],
        "add_corners",
        east, west, from_south, from_north,
    )
    from_west, from_east = shifted(east_full, "gx", 1), shifted(west_full, "gx", -1)
    wind_send, from_west, from_east = lax.optimization_barrier((wind_send, from_west, from_east))
    wind_recv = relay_rows(wind_send)
    seen_send = call(
        send_seen_kernel,
        [pltpu.HBM((owners, both_rows, LANES), jnp.float32)],
        [ext, all_rings]
        + [pltpu.VMEM((along_x, rows, LANES), jnp.float32)] * 2
        + [pltpu.VMEM((along_y, rows, LANES), jnp.float32)] * 2
        + [each_sem],
        "send_seen",
        rings, wind_ring, settle_rows, share_rows, east, west, north, south,
        from_west, from_east, from_south, from_north,
        hbm_out=True,
    )
    return wind_recv, relay_rows(seen_send)


def dust_kernel(home_ref, share_ref, settle_ref, dust_ref, shift_ref, wind_ref, out_ref, coef, *work, block, bins):
    lanes = len(work) // 2
    step = pl.program_id(0)
    _, lane = iotas()
    within = lane % TILE
    low_lanes, high_lanes = lane < TILE, lane >= LANES - TILE
    mix = dust_step * diffusion
    chunks = bins // ROWS
    settle = [dust_step * settle_ref[h * ROWS : (h + 1) * ROWS, :] for h in range(chunks)]
    share = [share_ref[h * ROWS : (h + 1) * ROWS, :] for h in range(chunks)]
    nothing = jnp.zeros((ROWS, LANES), jnp.float32)

    def prepare(k, j):
        held = work[2 * k]
        home = home_ref[step * block + j]
        plane = [wind_ref[home, p * ROWS : (p + 1) * ROWS, :] * dust_step for p in range(PLANES)]
        for level in range(TZ):
            u, v = plane[level], plane[TZ + level]
            coef[k, 0, level] = mix + jnp.maximum(u, 0.0)
            coef[k, 1, level] = mix + jnp.maximum(-u, 0.0)
            coef[k, 2, level] = jnp.where(within == 0, 0.0, mix + jnp.maximum(v, 0.0))
            coef[k, 3, level] = jnp.where(within == TILE - 1, 0.0, mix + jnp.maximum(-v, 0.0))
            coef[k, 4, level] = 1.0 - 6.0 * mix - jnp.abs(u) - jnp.abs(v)
            coef[k, 5, level] = plane[2 * TZ + level]
        coef[k, 6, 0] = plane[PLANES - 1]
        for r in range(ROWS):
            for level in range(TZ):
                at = (r * TZ + level) * bins
                held[at : at + bins, :] = dust_ref[j, pl.ds(r * TZ + level, bins, stride=ROWS * TZ), :]

    def shift(k):
        held, shifts = work[2 * k], work[2 * k + 1]
        shifts[...] = jnp.dot(
            jnp.concatenate(halves_of(held[...]), axis=1), shift_ref[...], preferred_element_type=jnp.float32
        )

    def update(k, j, substep):
        held, shifts = work[2 * k], work[2 * k + 1]
        for r in range(ROWS):
            for h in range(chunks):
                cells = [held[(r * TZ + level) * bins + h * ROWS :][:ROWS] for level in range(TZ)]
                for level in range(TZ):
                    at = (r * TZ + level) * bins + h * ROWS

                    def moved(which, rows_up=0):
                        first = at + rows_up * TZ * bins
                        return shifts[first : first + ROWS, which * LANES : (which + 1) * LANES]

                    def by(which):
                        return spread_rows(coef[k, which, level, r : r + 1, :])

                    before = nothing if r == 0 else moved(2, -1)
                    after = nothing if r == ROWS - 1 else moved(3, 1)
                    west = jnp.where(low_lanes, before, moved(2))
                    east = jnp.where(high_lanes, after, moved(3))
                    rise = by(5) - settle[h]
                    up = jnp.maximum(rise, 0.0)
                    mixed = mix + (up - rise if level == 0 else up)
                    value = (
                        (by(4) - jnp.abs(rise)) * cells[level]
                        + by(0) * west
                        + by(1) * east
                        + by(2) * moved(0)
                        + by(3) * moved(1)
                        + mixed * cells[1 - level]
                    )
                    if level == 0:
                        value = value + spread_rows(coef[k, 6, 0, r : r + 1, :]) * share[h]
                    if substep == 0:
                        held[at : at + ROWS, :] = value
                    else:
                        first = h * ROWS * ROWS * TZ + r * TZ + level
                        out_ref[j, pl.ds(first, ROWS, stride=ROWS * TZ), :] = value

    def some(i, carry):
        for k in range(lanes):
            prepare(k, i * lanes + k)
        for substep in range(2):
            for k in range(lanes):
                shift(k)
            for k in range(lanes):
                update(k, i * lanes + k, substep)
        return carry

    lax.fori_loop(0, block // lanes, some, 0)


def dust_inner(home_of_slot, dust, wind_recv, settle_speed, bin_share):
    slots, cells = dust.shape[:2]
    bins = settle_speed.shape[0]
    block = 8 if slots % 8 == 0 else 4
    lanes = 2
    smem = pl.BlockSpec(memory_space=pltpu.SMEM)
    vmem = pl.BlockSpec(memory_space=pltpu.VMEM)
    tile = pl.BlockSpec((block, cells, LANES), lambda i: (i, 0, 0))
    settle = jnp.broadcast_to(settle_speed[:, None], (bins, LANES))
    share = jnp.broadcast_to(bin_share[:, None], (bins, LANES))
    return pl.pallas_call(
        functools.partial(dust_kernel, block=block, bins=bins),
        grid=(slots // block,),
        in_specs=[smem, vmem, vmem, tile, vmem, vmem],
        out_specs=tile,
        out_shape=pltpu.HBM(dust.shape, jnp.float32),
        scratch_shapes=[pltpu.VMEM((lanes, PLANES, TZ, ROWS, LANES), jnp.float32)]
        + [pltpu.VMEM((cells, LANES), jnp.float32), pltpu.VMEM((cells, 4 * LANES), jnp.float32)] * lanes,
        compiler_params=pltpu.CompilerParams(vmem_limit_bytes=24 << 20),
        cost_estimate=pl.CostEstimate(flops=120 * dust.size, bytes_accessed=dust.size * 12, transcendentals=0),
        name="dust_inner",
    )(home_of_slot, share, settle, in_hbm(dust), jnp.asarray(shift_matrix()), wind_recv)


def dust_outer_kernel(
    home_ref, inner_hbm, matrix_ref, effect_hbm, out_hbm, effect, dust, effect_sems, load_sems, sems, *, block, bins
):
    slots = dust.shape[0]
    rows = TZ * bins

    def arrive(s):
        return pltpu.make_async_copy(effect_hbm.at[home_ref[s]], effect.at[s], effect_sems.at[s])

    def load(i):
        some = pl.ds(i * block, block)
        return pltpu.make_async_copy(inner_hbm.at[some], dust.at[some], load_sems.at[i])

    def store(i):
        some = pl.ds(i * block, block)
        return pltpu.make_async_copy(dust.at[some], out_hbm.at[some], sems.at[i])

    def start(i, carry):
        for j in range(block):
            arrive(i * block + j).start()
        load(i).start()
        return carry

    lax.fori_loop(0, slots // block, start, 0)

    def one(i, carry):
        for j in range(block):
            arrive(i * block + j).wait()
        rings = jnp.concatenate(
            [
                jnp.concatenate([effect[i * block + j, depth * rows : (depth + 1) * rows, :] for depth in range(2)], axis=1)
                for j in range(block)
            ],
            axis=0,
        )
        added = jnp.dot(
            jnp.concatenate(halves_of(rings), axis=1), matrix_ref[...], preferred_element_type=jnp.float32
        )
        load(i).wait()
        for j in range(block):
            for r in range(ROWS):
                for level in range(TZ):
                    at = pl.ds(r * TZ + level, bins, stride=ROWS * TZ)
                    first = j * rows + level * bins
                    dust[i * block + j, at, :] += added[first : first + bins, r * LANES : (r + 1) * LANES]
        store(i).start()
        return carry

    lax.fori_loop(0, slots // block, one, 0)
    for i in range(slots // block):
        store(i).wait()


def dust_outer(home_of_slot, inner, effect, bins):
    slots = inner.shape[0]
    block = 8 if slots % 8 == 0 else 4
    hbm = pl.BlockSpec(memory_space=pltpu.HBM)
    vmem = pl.BlockSpec(memory_space=pltpu.VMEM)
    return pl.pallas_call(
        functools.partial(dust_outer_kernel, block=block, bins=bins),
        in_specs=[pl.BlockSpec(memory_space=pltpu.SMEM), hbm, vmem, hbm],
        out_specs=hbm,
        out_shape=pltpu.HBM(inner.shape, jnp.float32),
        scratch_shapes=[
            pltpu.VMEM((slots,) + effect.shape[1:], jnp.float32),
            pltpu.VMEM(inner.shape, jnp.float32),
            pltpu.SemaphoreType.DMA((slots,)),
            pltpu.SemaphoreType.DMA((slots // block,)),
            pltpu.SemaphoreType.DMA((slots // block,)),
        ],
        compiler_params=pltpu.CompilerParams(vmem_limit_bytes=24 << 20),
        cost_estimate=pl.CostEstimate(flops=2 * inner.size, bytes_accessed=inner.size * 8, transcendentals=0),
        name="dust_outer",
    )(home_of_slot, in_hbm(inner), jnp.asarray(spread_matrix()), in_hbm(effect))


def per_device(velocity, threshold, dust_mass, settle_speed, bin_share, active_tiles, tile_owner):
    owners = lax.axis_size(AXES)
    grid_cols = lax.axis_size("gy")
    self_index = lax.axis_index(AXES)
    slots, bins = dust_mass.shape[:2]
    tiles_x = velocity.shape[2] // TILE
    tiles_y = velocity.shape[3] // TILE
    per_home = tiles_x * tiles_y
    tiles_across = tiles_y * grid_cols

    tile_x = active_tiles // tiles_across
    tile_y = active_tiles % tiles_across
    home_dev = tile_x // tiles_x * grid_cols + tile_y // tiles_y
    local_tile = tile_x % tiles_x * tiles_y + tile_y % tiles_y
    own_slot = tile_owner - self_index * slots
    mine = jnp.where(home_dev == self_index, local_tile, -1)
    slot_ids = jnp.arange(slots, dtype=jnp.int32)
    home_of_slot = jnp.sum(jnp.where(own_slot[None, :] == slot_ids[:, None], home_dev[None, :], 0), axis=1)
    tile_ids = jnp.arange(per_home, dtype=jnp.int32)
    owner_of_tile = jnp.max(
        jnp.where(mine[None, :] == tile_ids[:, None], (tile_owner // slots)[None, :], -1), axis=1
    )

    dust = dust_mass.reshape(slots, bins, TZ, ROWS, LANES).transpose(0, 1, 3, 2, 4)
    dust = dust.reshape(slots, bins * ROWS * TZ, LANES)

    xlo, xhi, ylo, yhi = exchange_borders(wind_faces(velocity))

    strips_send = dust_strips(home_of_slot, dust, bins, owners)
    strips_send, xlo, xhi, ylo, yhi = lax.optimization_barrier((strips_send, xlo, xhi, ylo, yhi))
    strips = relay_rows(strips_send)
    new_velocity, wind_send, wind_ring = wind_step(
        owner_of_tile, velocity, xlo, xhi, ylo, yhi, threshold, owners
    )
    strips, wind_send, wind_ring = lax.optimization_barrier((strips, wind_send, wind_ring))
    wind_recv, effect = relay_strips(
        owner_of_tile, strips, wind_send, wind_ring, settle_speed, bin_share, tiles_x, tiles_y
    )
    inner = dust_inner(home_of_slot, dust, wind_recv, settle_speed, bin_share)
    out = dust_outer(home_of_slot, inner, effect, bins)
    out = out.reshape(slots, bins, ROWS, TZ, LANES).transpose(0, 1, 3, 2, 4).reshape(dust_mass.shape)
    return new_velocity, out


def solution(mesh):
    in_specs = (
        P(None, None, "gx", "gy"),
        P("gx", "gy"),
        P(AXES, None, None, None),
        P(),
        P(),
        P(),
        P(),
    )
    out_specs = (P(None, None, "gx", "gy"), P(AXES, None, None, None))
    return jax.shard_map(
        per_device, mesh=mesh, in_specs=in_specs, out_specs=out_specs, check_vma=False
    )
```

```python
import functools

import jax
import jax.numpy as jnp
import ml_dtypes
import numpy as np
from jax import lax
from jax.experimental import pallas as pl
from jax.experimental.pallas import tpu as pltpu
from jax.sharding import PartitionSpec as P

TZ = 2
TILE = 32
LANES = 128
ROWS = TILE * TILE // LANES
PLANES = 7
AXES = ("gx", "gy")

time_step = 0.1
viscosity = 0.2
dust_step = 0.1
diffusion = 0.1
roughness = 0.5
emit_rate = 0.5

WEST, SOUTH, NORTH, EAST = range(4)


def iotas(shape=(ROWS, LANES)):
    return lax.broadcasted_iota(jnp.int32, shape, 0), lax.broadcasted_iota(jnp.int32, shape, 1)


def lane_gather(x, index):
    return jnp.take_along_axis(x, index, axis=1)


def ring_pattern(depth):
    row, lane = iotas()
    group, within = lane // TILE, lane % TILE
    side = jnp.where(group == SOUTH, depth, TILE - 1 - depth)
    index = (within % 4) * TILE + side
    index = jnp.where(group == WEST, depth * TILE + within, index)
    index = jnp.where(group == EAST, (3 - depth) * TILE + within, index)
    source = jnp.where(group == WEST, 0, jnp.where(group == EAST, ROWS - 1, within // 4))
    return index, row == source


def ring_of(x, pattern):
    index, taken = pattern
    return jnp.sum(jnp.where(taken, lane_gather(x, index), 0.0), axis=0, keepdims=True)


def spread_rows(row):
    return jnp.broadcast_to(row, (ROWS, LANES))


def f32(*shape):
    return jax.ShapeDtypeStruct(shape, jnp.float32)


def in_hbm(x):
    return pltpu.with_memory_space_constraint(x, pltpu.HBM)


def halves_of(x):
    high = x.astype(jnp.bfloat16)
    return high, (x - high.astype(jnp.float32)).astype(jnp.bfloat16)


def moves(sources, width=LANES):
    lanes = np.arange(width)[:, None]
    once = (lanes == np.asarray(sources)[None, :]).astype(ml_dtypes.bfloat16)
    return np.concatenate([once, once], axis=0)


def ring_matrix():
    lane = np.arange(LANES)
    group, within = lane // TILE, lane % TILE
    blocks = []
    for r in range(ROWS):
        columns = []
        for depth in range(2):
            side = np.where(group == SOUTH, depth, TILE - 1 - depth)
            source = np.where(within // 4 == r, (within % 4) * TILE + side, -1)
            source = np.where(group == WEST, depth * TILE + within if r == 0 else -1, source)
            source = np.where(group == EAST, (3 - depth) * TILE + within if r == ROWS - 1 else -1, source)
            columns.append(source)
        blocks.append(moves(np.concatenate(columns)))
    return np.concatenate(blocks, axis=0)


def shift_matrix():
    lane = np.arange(LANES)
    return moves(np.concatenate([(lane + d) % LANES for d in (-1, 1, -TILE, TILE)]))


def spread_matrix():
    i, j = np.divmod(np.arange(TILE * TILE), TILE)
    source = np.full(TILE * TILE, -1)
    for depth in (1, 0):
        at = depth * LANES
        source = np.where(j == depth, at + SOUTH * TILE + i, source)
        source = np.where(j == TILE - 1 - depth, at + NORTH * TILE + i, source)
        source = np.where(i == depth, at + WEST * TILE + j, source)
        source = np.where(i == TILE - 1 - depth, at + EAST * TILE + j, source)
    return moves(source, 2 * LANES)


def strips_kernel(home_ref, dust_hbm, matrix_ref, send_ref, dust, rings, load_sems, sems, *, block, bins):
    slots = rings.shape[0]
    each = TZ * bins

    def load(i):
        some = pl.ds(i * block, block)
        return pltpu.make_async_copy(dust_hbm.at[some], dust.at[some], load_sems.at[i])

    def send(s):
        return pltpu.make_async_copy(rings.at[s], send_ref.at[home_ref[s]], sems.at[s])

    for i in range(slots // block):
        load(i).start()

    def one(i, carry):
        load(i).wait()
        parts = []
        for r in range(ROWS):
            x = jnp.concatenate(
                [
                    dust[i * block + j, pl.ds(r * TZ + level, bins, stride=ROWS * TZ), :]
                    for j in range(block)
                    for level in range(TZ)
                ],
                axis=0,
            )
            parts += halves_of(x)
        found = jnp.dot(
            jnp.concatenate(parts, axis=1), matrix_ref[...], preferred_element_type=jnp.float32
        )
        for j in range(block):
            for depth in range(2):
                rings[i * block + j, depth * each : (depth + 1) * each, :] = found[
                    j * each : (j + 1) * each, depth * LANES : (depth + 1) * LANES
                ]
            send(i * block + j).start()
        return carry

    lax.fori_loop(0, slots // block, one, 0)

    def wait(s, carry):
        send(s).wait()
        return carry

    lax.fori_loop(0, slots, wait, 0)


def dust_strips(home_of_slot, dust, bins, owners):
    slots = dust.shape[0]
    block = 14 if slots % 14 == 0 else 4
    rows = 2 * bins * TZ
    matrix = jnp.asarray(ring_matrix())
    hbm = pl.BlockSpec(memory_space=pltpu.HBM)
    return pl.pallas_call(
        functools.partial(strips_kernel, block=block, bins=bins),
        in_specs=[pl.BlockSpec(memory_space=pltpu.SMEM), hbm, pl.BlockSpec(memory_space=pltpu.VMEM)],
        out_specs=hbm,
        out_shape=pltpu.HBM((owners, rows, LANES), jnp.float32),
        scratch_shapes=[
            pltpu.VMEM(dust.shape, jnp.float32),
            pltpu.VMEM((slots, rows, LANES), jnp.float32),
            pltpu.SemaphoreType.DMA((slots // block,)),
            pltpu.SemaphoreType.DMA((slots,)),
        ],
        compiler_params=pltpu.CompilerParams(vmem_limit_bytes=32 << 20),
        cost_estimate=pl.CostEstimate(
            flops=20 * dust.size, bytes_accessed=dust.size * 4 + slots * rows * LANES * 4, transcendentals=0
        ),
        name="dust_strips",
    )(home_of_slot, in_hbm(dust), matrix)


def faces_kernel(vel_ref, x_last_ref, x_first_ref, y_last_ref, y_first_ref, first, last, low, high, x_sems, y_sems):
    fields, nx, ny = vel_ref.shape
    x_copies = [
        pltpu.make_async_copy(vel_ref.at[:, pl.ds(0, ROWS), :], first, x_sems.at[0]),
        pltpu.make_async_copy(vel_ref.at[:, pl.ds(nx - ROWS, ROWS), :], last, x_sems.at[1]),
    ]
    y_copies = [
        (
            pltpu.make_async_copy(vel_ref.at[f, :, pl.ds(0, LANES)], low.at[f], y_sems.at[0, f]),
            pltpu.make_async_copy(vel_ref.at[f, :, pl.ds(ny - LANES, LANES)], high.at[f], y_sems.at[1, f]),
        )
        for f in range(fields)
    ]
    for pair in y_copies:
        for copy in pair:
            copy.start()
    for copy in x_copies:
        copy.start()
    lane = lax.broadcasted_iota(jnp.int32, (nx, LANES), 1)
    for f, (low_copy, high_copy) in enumerate(y_copies):
        low_copy.wait()
        high_copy.wait()
        from_low = pltpu.roll(low[f], f, 1) if f else low[f]
        from_high = pltpu.roll(high[f], f + 1, 1)
        if f == 0:
            y_first_ref[...], y_last_ref[...] = from_low, from_high
        else:
            y_first_ref[...] = jnp.where(lane == f, from_low, y_first_ref[...])
            y_last_ref[...] = jnp.where(lane == f, from_high, y_last_ref[...])
    for copy in x_copies:
        copy.wait()
    for f in range(fields):
        x_first_ref[f : f + 1, :] = first[f, 0:1, :]
        x_last_ref[f : f + 1, :] = last[f, ROWS - 1 : ROWS, :]


def wind_faces(velocity):
    comps, levels, nx, ny = velocity.shape
    fields = comps * levels
    vmem = pl.BlockSpec(memory_space=pltpu.VMEM)
    return pl.pallas_call(
        faces_kernel,
        in_specs=[pl.BlockSpec(memory_space=pltpu.HBM)],
        out_specs=[vmem] * 4,
        out_shape=[f32(fields, ny)] * 2 + [f32(nx, LANES)] * 2,
        scratch_shapes=[
            pltpu.VMEM((fields, ROWS, ny), jnp.float32),
            pltpu.VMEM((fields, ROWS, ny), jnp.float32),
            pltpu.VMEM((fields, nx, LANES), jnp.float32),
            pltpu.VMEM((fields, nx, LANES), jnp.float32),
            pltpu.SemaphoreType.DMA((2,)),
            pltpu.SemaphoreType.DMA((2, fields)),
        ],
        compiler_params=pltpu.CompilerParams(vmem_limit_bytes=32 << 20),
        cost_estimate=pl.CostEstimate(flops=velocity.size, bytes_accessed=velocity.size * 4, transcendentals=0),
        name="wind_faces",
    )(in_hbm(velocity.reshape(fields, nx, ny)))


def wind_kernel(
    owner_ref, vel_ref, xlo_ref, xhi_ref, ylo_ref, yhi_ref, thr_ref,
    new_ref, send_ref, ring_ref, padded, strip, tiles, load_sem, sems, *, levels
):
    fields, nx, ny = new_ref.shape
    load = pltpu.make_async_copy(vel_ref, padded.at[:, pl.ds(8, nx), :], load_sem)
    load.start()
    load.wait()
    for f in range(fields):
        padded[f, 7:8, :] = xlo_ref[f : f + 1, :]
        padded[f, 8 + nx : 9 + nx, :] = xhi_ref[f : f + 1, :]
    half = 16
    halves = ny // LANES
    tiles_y = ny // TILE
    patterns = [ring_pattern(0), ring_pattern(1)]
    _, lane8 = iotas()
    group = lane8 // TILE

    def one_strip(ix, carry):
        for sub in range(TILE // half):
            base = pl.multiple_of(ix * TILE + sub * half, 8)
            lane = lax.broadcasted_iota(jnp.int32, (half, ny), 1)
            low = {}
            faces = [ref[pl.ds(base, half), :] for ref in (ylo_ref, yhi_ref)]

            def face(which, f, to):
                moved = pltpu.roll(faces[which], (to - f) % LANES, 1) if f != to else faces[which]
                return jnp.concatenate([moved] * halves, axis=1)

            for z in range(levels):
                u, v, w = (padded[c * levels + z, pl.ds(base + 8, half), :] for c in range(3))
                for c in range(3):
                    f = c * levels + z
                    block = padded[f, pl.ds(base, half + 16), :]
                    centre = (u, v, w)[c]
                    west = pltpu.roll(block, 1, 0)[8 : 8 + half]
                    east = pltpu.roll(block, half + 15, 0)[8 : 8 + half]
                    south = jnp.where(lane == 0, face(0, f, 0), pltpu.roll(centre, 1, 1))
                    north = jnp.where(lane == ny - 1, face(1, f, LANES - 1), pltpu.roll(centre, ny - 1, 1))
                    lower = -centre if z == 0 else padded[f - 1, pl.ds(base + 8, half), :]
                    upper = centre if z == levels - 1 else padded[f + 1, pl.ds(base + 8, half), :]
                    carried = 0.5 * (u * (east - west) + v * (north - south) + w * (upper - lower))
                    spread = east + west + north + south + upper + lower - 6.0 * centre
                    new = centre + time_step * (viscosity * spread - carried)
                    new_ref[f, pl.ds(base, half), :] = new
                    if z < TZ:
                        low[c * TZ + z] = new
            stress = roughness * (low[0] * low[0] + low[TZ] * low[TZ])
            low[PLANES - 1] = emit_rate * stress * jnp.maximum(
                stress - thr_ref[pl.ds(base, half), :], 0.0
            )
            for p in range(PLANES):
                for h in range(halves):
                    strip[p * halves + h, sub * half : (sub + 1) * half, :] = low[p][
                        :, h * LANES : (h + 1) * LANES
                    ]
        for p in range(PLANES):
            for h in range(halves):
                parts = [strip[p * halves + h, pl.ds(k, ROWS, stride=4), :] for k in range(4)]
                for t in range(4):
                    tile = ix * tiles_y + h * 4 + t
                    cells = pltpu.roll(parts[0], (-t * TILE) % LANES, 1) if t else parts[0]
                    for k in range(1, 4):
                        moved = pltpu.roll(parts[k], ((k - t) * TILE) % LANES, 1) if k != t else parts[k]
                        cells = jnp.where(group == k, moved, cells)
                    tiles[tile, p * ROWS : (p + 1) * ROWS, :] = cells
                    for depth in range(2):
                        ring_ref[tile, depth * 8 + p : depth * 8 + p + 1, :] = ring_of(cells, patterns[depth])

        def send(t, inner):
            tile = ix * tiles_y + t
            owner = owner_ref[tile]

            @pl.when(owner >= 0)
            def _():
                pltpu.make_async_copy(tiles.at[tile], send_ref.at[owner], sems.at[tile]).start()

            return inner

        lax.fori_loop(0, tiles_y, send, 0)
        return carry

    lax.fori_loop(0, nx // TILE, one_strip, 0)

    def wait(tile, carry):
        owner = owner_ref[tile]

        @pl.when(owner >= 0)
        def _():
            pltpu.make_async_copy(tiles.at[tile], send_ref.at[owner], sems.at[tile]).wait()

        return carry

    lax.fori_loop(0, tiles.shape[0], wait, 0)


def wind_step(owner_of_tile, velocity, xlo, xhi, ylo, yhi, threshold, owners):
    comps, levels, nx, ny = velocity.shape
    fields = comps * levels
    per_home = (nx // TILE) * (ny // TILE)
    smem = pl.BlockSpec(memory_space=pltpu.SMEM)
    hbm = pl.BlockSpec(memory_space=pltpu.HBM)
    vmem = pl.BlockSpec(memory_space=pltpu.VMEM)
    new, send, ring = pl.pallas_call(
        functools.partial(wind_kernel, levels=levels),
        in_specs=[smem, hbm, vmem, vmem, vmem, vmem, vmem],
        out_specs=[vmem, hbm, vmem],
        out_shape=[
            f32(fields, nx, ny),
            pltpu.HBM((owners, PLANES * ROWS, LANES), jnp.float32),
            f32(per_home, 16, LANES),
        ],
        scratch_shapes=[
            pltpu.VMEM((fields, nx + 16, ny), jnp.float32),
            pltpu.VMEM((PLANES * (ny // LANES), TILE, LANES), jnp.float32),
            pltpu.VMEM((per_home, PLANES * ROWS, LANES), jnp.float32),
            pltpu.SemaphoreType.DMA,
            pltpu.SemaphoreType.DMA((per_home,)),
        ],
        compiler_params=pltpu.CompilerParams(vmem_limit_bytes=40 << 20),
        cost_estimate=pl.CostEstimate(
            flops=40 * velocity.size, bytes_accessed=velocity.size * 10, transcendentals=0
        ),
        name="wind_step",
    )(
        owner_of_tile,
        in_hbm(velocity.reshape(fields, nx, ny)),
        xlo,
        xhi,
        ylo,
        yhi,
        threshold,
    )
    return new.reshape(velocity.shape), send, ring


def border_tiles(tiles_x, tiles_y):
    return (
        (EAST, [(tiles_x - 1) * tiles_y + n for n in range(tiles_y)]),
        (WEST, [n for n in range(tiles_y)]),
        (NORTH, [n * tiles_y + tiles_y - 1 for n in range(tiles_x)]),
        (SOUTH, [n * tiles_y for n in range(tiles_x)]),
    )


def fill_halo(ext, strips, tiles_x, tiles_y):
    wide = tiles_y + 2
    for strip_of, side, places in (
        (strips[0], EAST, [n + 1 for n in range(tiles_y)]),
        (strips[1], WEST, [(tiles_x + 1) * wide + n + 1 for n in range(tiles_y)]),
        (strips[2], NORTH, [(n + 1) * wide for n in range(tiles_x)]),
        (strips[3], SOUTH, [(n + 1) * wide + tiles_y + 1 for n in range(tiles_x)]),
    ):
        for n, place in enumerate(places):
            strip = strip_of(n // 4)
            if n % 4 != side:
                strip = pltpu.roll(strip, ((side - n % 4) * TILE) % LANES, 1)
            ext[place] = strip


def seen_by(ext, place, wide):
    west, east = ext[place - wide], ext[place + wide]
    south, north = ext[place - 1], ext[place + 1]
    lane = lax.broadcasted_iota(jnp.int32, west.shape, 1)
    up = pltpu.roll(jnp.where(lane < 2 * TILE, north, west), TILE, 1)
    down = pltpu.roll(jnp.where(lane < 2 * TILE, east, south), LANES - TILE, 1)
    return jnp.where((lane // TILE) % 2 == 0, up, down)


FLAG = 7


def pack_borders_kernel(owner_ref, recv_ref, wind_ref, *refs, tiles_x, tiles_y):
    *outs, rings, sems = refs
    both_rows = rings.shape[1]
    borders = border_tiles(tiles_x, tiles_y)
    used = sorted({t for _, tiles in borders for t in tiles})

    def copy(t):
        return pltpu.make_async_copy(recv_ref.at[owner_ref[t]], rings.at[t], sems.at[t])

    for t in used:

        @pl.when(owner_ref[t] >= 0)
        def _():
            copy(t).start()

        @pl.when(owner_ref[t] < 0)
        def _():
            rings[t] = jnp.zeros(rings.shape[1:], jnp.float32)

    for t in used:

        @pl.when(owner_ref[t] >= 0)
        def _():
            copy(t).wait()

    lane = lax.broadcasted_iota(jnp.int32, (both_rows, LANES), 1) // TILE
    row8, lane8 = iotas()
    group8 = lane8 // TILE
    for out, (side, tiles) in zip(outs, borders):
        for g in range(len(tiles) // 4):
            strips = winds = None
            for q in range(4):
                t = tiles[4 * g + q]
                strip, wind = rings[t], wind_ref[t, :ROWS, :]
                if q != side:
                    strip = pltpu.roll(strip, ((q - side) * TILE) % LANES, 1)
                    wind = pltpu.roll(wind, ((q - side) * TILE) % LANES, 1)
                wind = jnp.where(row8 == FLAG, jnp.where(owner_ref[t] >= 0, 1.0, 0.0), wind)
                strips = strip if strips is None else jnp.where(lane == q, strip, strips)
                winds = wind if winds is None else jnp.where(group8 == q, wind, winds)
            at = g * (both_rows + ROWS)
            out[at : at + both_rows, :] = strips
            out[at + both_rows : at + both_rows + ROWS, :] = winds


def gather_rings_kernel(owner_ref, recv_ref, rings_ref, *, tiles_x, tiles_y):
    def one(t, carry):
        owner = owner_ref[t]
        rings = recv_ref[jnp.maximum(owner, 0)]
        rings_ref[t] = jnp.where(owner >= 0, rings, 0.0)
        return carry

    lax.fori_loop(0, tiles_x * tiles_y, one, 0)


def fill_tiles(ext, tile, tiles_x, tiles_y):
    def inner(t, carry):
        ext[place_of(t, tiles_y)] = tile(t)
        return carry

    lax.fori_loop(0, tiles_x * tiles_y, inner, 0)


def place_of(t, tiles_y):
    return (t // tiles_y + 1) * (tiles_y + 2) + t % tiles_y + 1


def corner_index(inset):
    _, lane = iotas()
    group, within = lane // TILE, lane % TILE
    on_x = (group == WEST) | (group == EAST)
    low = within < TILE // 2
    along = jnp.where((group == EAST) | (group == NORTH), TILE - 1 - inset, inset)
    return jnp.where(on_x, jnp.where(low, SOUTH, NORTH), jnp.where(low, WEST, EAST)) * TILE + along


def ring_effect(t, wind_ref, settle_ref, seen, seen_later):
    row, lane = iotas()
    group, within = lane // TILE, lane % TILE
    on_x = (group == WEST) | (group == EAST)
    low_side = (group == WEST) | (group == SOUTH)
    first, last = within == 0, within == TILE - 1
    second, last_but_one = within == 1, within == TILE - 2
    corner, inner = corner_index(0), corner_index(1)
    rows = seen.shape[0]
    bins = rows // TZ
    mix = dust_step * diffusion

    def wind(depth, p):
        return dust_step * spread_rows(wind_ref[t, depth * 8 + p : depth * 8 + p + 1, :])

    inflow, later_in = [], []
    coefs = []
    for level in range(TZ):
        u, v, w = (wind(0, c * TZ + level) for c in range(3))
        across, along = jnp.where(on_x, u, v), jnp.where(on_x, v, u)
        outward = jnp.where(low_side, across, -across)
        from_out = mix + jnp.maximum(outward, 0.0)
        from_in = jnp.where(first | last, mix + jnp.maximum(-outward, 0.0), 0.0)
        from_before, from_after = mix + jnp.maximum(along, 0.0), mix + jnp.maximum(-along, 0.0)
        from_corner = jnp.where(first, from_before, jnp.where(last, from_after, 0.0))
        from_before = jnp.where(first, 0.0, from_before)
        from_after = jnp.where(last, 0.0, from_after)
        keep = 1.0 - 6.0 * mix - jnp.abs(u) - jnp.abs(v)
        u2, v2 = (wind(1, c * TZ + level) for c in range(2))
        across2, along2 = jnp.where(on_x, u2, v2), jnp.where(on_x, v2, u2)
        deep_out = mix + jnp.maximum(jnp.where(low_side, across2, -across2), 0.0)
        deep_corner = jnp.where(
            second, mix + jnp.maximum(along2, 0.0), jnp.where(last_but_one, mix + jnp.maximum(-along2, 0.0), 0.0)
        )
        coefs.append((w, keep, from_in, from_before, from_after, deep_out, deep_corner))
        for at in range(level * bins, (level + 1) * bins, ROWS):
            for view, taken in ((seen, inflow), (seen_later, later_in)):
                g = view[at : at + ROWS, :]
                taken.append(from_out * g + from_corner * lane_gather(g, corner))
    outer, deep = [], []
    for n, e in enumerate(inflow):
        level, bin_at = n * ROWS // bins, n * ROWS % bins
        w, keep, from_in, from_before, from_after, deep_out, deep_corner = coefs[level]
        other = inflow[n + len(inflow) // 2 if level == 0 else n - len(inflow) // 2]
        rise = w - dust_step * settle_ref[bin_at : bin_at + ROWS, :]
        up = jnp.maximum(rise, 0.0)
        down = up - rise
        turned = lane_gather(e, inner)
        outer.append(
            (keep - up - down) * e
            + from_before * pltpu.roll(e, 1, 1)
            + from_after * pltpu.roll(e, LANES - 1, 1)
            + from_in * turned
            + (mix + (down if level == 0 else up)) * other
            + later_in[n]
        )
        deep.append(deep_out * e + deep_corner * turned)
    return outer, deep


def advance_ring(t, owner_ref, rings_ref, wind_ref, settle_ref, share_ref, seen):
    _, lane = iotas()
    group, within = lane // TILE, lane % TILE
    on_x = (group == WEST) | (group == EAST)
    first, last = within == 0, within == TILE - 1
    corner = corner_index(0)
    rows = rings_ref.shape[1] // 2
    bins = rows // TZ
    uplift = dust_step * spread_rows(wind_ref[t, PLANES - 1 : PLANES, :])
    mix = dust_step * diffusion
    active = owner_ref[t] >= 0
    chunks = []
    for at in range(0, rows, ROWS):
        level, bin_at = at // bins, at % bins
        if bin_at == 0:
            u, v, w = (
                dust_step * spread_rows(wind_ref[t, c * TZ + level : c * TZ + level + 1, :]) for c in range(3)
            )
            from_west = mix + jnp.maximum(u, 0.0)
            from_east = mix + jnp.maximum(-u, 0.0)
            from_south = mix + jnp.maximum(v, 0.0)
            from_north = mix + jnp.maximum(-v, 0.0)
            keep = 1.0 - 6.0 * mix - jnp.abs(u) - jnp.abs(v)
        q = rings_ref[t, at : at + ROWS, :]
        deep = rings_ref[t, rows + at : rows + at + ROWS, :]
        out = seen[at : at + ROWS, :]
        beyond = lane_gather(out, corner)
        before = jnp.where(first, beyond, pltpu.roll(q, 1, 1))
        after = jnp.where(last, beyond, pltpu.roll(q, LANES - 1, 1))
        west = jnp.where(group == WEST, out, jnp.where(group == EAST, deep, before))
        east = jnp.where(group == WEST, deep, jnp.where(group == EAST, out, after))
        south = jnp.where(on_x, before, jnp.where(group == SOUTH, out, deep))
        north = jnp.where(on_x, after, jnp.where(group == SOUTH, deep, out))
        other_at = (1 - level) * bins + bin_at
        other = rings_ref[t, other_at : other_at + ROWS, :]
        rise = w - dust_step * settle_ref[bin_at : bin_at + ROWS, :]
        up = jnp.maximum(rise, 0.0)
        down = up - rise
        new = (
            (keep - up - down) * q
            + from_west * west
            + from_east * east
            + from_south * south
            + from_north * north
            + (mix + (down if level == 0 else up)) * other
        )
        if level == 0:
            new = new + uplift * share_ref[bin_at : bin_at + ROWS, :]
        chunks.append(jnp.where(active, new, 0.0))
    return chunks


def advance_strip(side, message, ours, settle_ref, share_ref, out, rows):
    _, lane = iotas()
    bins = rows // TZ
    each = 2 * rows + ROWS
    groups = out.shape[0]
    mix = dust_step * diffusion
    for g in range(groups):
        wind_at = g * each + 2 * rows

        def wind_row(p):
            return spread_rows(message[wind_at + p : wind_at + p + 1, :])

        for at in range(0, rows, ROWS):
            level, bin_at = at // bins, at % bins
            u, v, w = (dust_step * wind_row(c * TZ + level) for c in range(3))

            def cells(group, first):
                return message[group * each + first : group * each + first + ROWS, :]

            q = cells(g, at)
            deep = cells(g, rows + at)
            near = ours[g * each + at : g * each + at + ROWS, :]
            low = 0.0 if g == 0 else pltpu.roll(cells(g - 1, at), 1, 1)
            high = 0.0 if g == groups - 1 else pltpu.roll(cells(g + 1, at), LANES - 1, 1)
            before = jnp.where(lane == 0, low, pltpu.roll(q, 1, 1))
            after = jnp.where(lane == LANES - 1, high, pltpu.roll(q, LANES - 1, 1))
            across = (deep, near) if side in (WEST, SOUTH) else (near, deep)
            (west, east), (south, north) = (
                (across, (before, after)) if side in (WEST, EAST) else ((before, after), across)
            )
            other = cells(g, (1 - level) * bins + bin_at)
            rise = w - dust_step * settle_ref[bin_at : bin_at + ROWS, :]
            up = jnp.maximum(rise, 0.0)
            down = up - rise
            new = (
                (1.0 - 6.0 * mix - jnp.abs(u) - jnp.abs(v) - up - down) * q
                + (mix + jnp.maximum(u, 0.0)) * west
                + (mix + jnp.maximum(-u, 0.0)) * east
                + (mix + jnp.maximum(v, 0.0)) * south
                + (mix + jnp.maximum(-v, 0.0)) * north
                + (mix + (down if level == 0 else up)) * other
            )
            if level == 0:
                new = new + dust_step * wind_row(PLANES - 1) * share_ref[bin_at : bin_at + ROWS, :]
            out[g, at : at + ROWS, :] = jnp.where(wind_row(FLAG) > 0.0, new, 0.0)


def send_seen_kernel(
    owner_ref, rings_ref, wind_ref, settle_ref, share_ref, e_ref, w_ref, n_ref, s_ref, fw_ref, fe_ref, fs_ref, fn_ref,
    send_ref, corner_ref, ext, both, lw_ref, le_ref, ls_ref, ln_ref, sems, *, tiles_x, tiles_y
):
    rows = rings_ref.shape[1] // 2
    wide = tiles_y + 2
    each = 2 * rows + ROWS
    messages = (fw_ref, fe_ref, fs_ref, fn_ref)
    later = (lw_ref, le_ref, ls_ref, ln_ref)

    def place(t):
        return place_of(t, tiles_y)

    fill_halo(
        ext, [lambda g, m=m: m[g * each : g * each + rows, :] for m in messages], tiles_x, tiles_y
    )
    fill_tiles(ext, lambda t: rings_ref[t, :rows, :], tiles_x, tiles_y)

    def before(t, carry):
        both[t, :rows, :] = seen_by(ext, place(t), wide)
        return carry

    lax.fori_loop(0, tiles_x * tiles_y, before, 0)

    def advance(i, carry):
        for t in (2 * i, 2 * i + 1):
            chunks = advance_ring(t, owner_ref, rings_ref, wind_ref, settle_ref, share_ref, both[t, :rows, :])
            for n, chunk in enumerate(chunks):
                ext[place(t), n * ROWS : (n + 1) * ROWS, :] = chunk
        return carry

    lax.fori_loop(0, tiles_x * tiles_y // 2, advance, 0)

    for side, message, ours, out in zip(
        (WEST, EAST, SOUTH, NORTH), messages, (w_ref, e_ref, s_ref, n_ref), later
    ):
        advance_strip(side, message, ours, settle_ref, share_ref, out, rows)
    fill_halo(ext, [lambda g, m=m: m[g] for m in later], tiles_x, tiles_y)

    def copy(t):
        return pltpu.make_async_copy(both.at[t], send_ref.at[owner_ref[t]], sems.at[t])

    def sent_now(t):
        x, y = t // tiles_y, t % tiles_y
        at_corner = ((x == 0) | (x == tiles_x - 1)) & ((y == 0) | (y == tiles_y - 1))
        return (owner_ref[t] >= 0) & jnp.logical_not(at_corner)

    def after(t, carry):
        effect = ring_effect(t, wind_ref, settle_ref, both[t, :rows, :], seen_by(ext, place(t), wide))
        for depth, chunks in enumerate(effect):
            for n, chunk in enumerate(chunks):
                both[t, depth * rows + n * ROWS : depth * rows + (n + 1) * ROWS, :] = chunk

        @pl.when(sent_now(t))
        def _():
            copy(t).start()

        return carry

    lax.fori_loop(0, tiles_x * tiles_y, after, 0)
    for n, (_, _, t) in enumerate(corner_tiles(tiles_x, tiles_y)):
        corner_ref[n] = both[t]

    def wait(t, carry):
        @pl.when(sent_now(t))
        def _():
            copy(t).wait()

        return carry

    lax.fori_loop(0, tiles_x * tiles_y, wait, 0)


def corner_tiles(tiles_x, tiles_y):
    return [
        (side_x, side_y, x * tiles_y + y)
        for side_x, x in ((WEST, 0), (EAST, tiles_x - 1))
        for side_y, y in ((SOUTH, 0), (NORTH, tiles_y - 1))
    ]


def send_corners_kernel(
    owner_ref, _, effect_ref, wind_ref, fw_ref, fe_ref, fs_ref, fn_ref, cw_ref, ce_ref, send_ref, sums, sems,
    *, tiles_x, tiles_y
):
    rows = cw_ref.shape[0] // 2
    each = 2 * rows + ROWS
    bins = rows // TZ
    mix = dust_step * diffusion
    _, lane = iotas()
    group, within = lane // TILE, lane % TILE
    on_x = (group == WEST) | (group == EAST)
    low_side = (group == WEST) | (group == SOUTH)
    first, last = within == 0, within == TILE - 1
    corner = corner_index(0)
    tiles = corner_tiles(tiles_x, tiles_y)

    def copy(n, t):
        return pltpu.make_async_copy(sums.at[n], send_ref.at[owner_ref[t]], sems.at[n])

    for n, (side_x, side_y, t) in enumerate(tiles):
        strip_x = fw_ref if side_x == WEST else fe_ref
        strip_y = fs_ref if side_y == SOUTH else fn_ref
        cells_ref, cell_lane = (cw_ref, LANES - 1) if side_x == WEST else (ce_ref, 0)
        cells_at = 0 if side_y == SOUTH else rows
        low_x, low_y = side_x == WEST, side_y == SOUTH
        end_x = 0 if low_y else strip_x.shape[0] - each
        end_y = 0 if low_x else strip_y.shape[0] - each
        to_x = side_x * TILE + (0 if low_y else TILE - 1)
        to_y = side_y * TILE + (0 if low_x else TILE - 1)

        def from_end(strip, at, c, level, low):
            def row(p):
                value = strip[at + 2 * rows + p : at + 2 * rows + p + 1, :]
                return lane_gather(spread_rows(value), jnp.full((ROWS, LANES), 0 if low else LANES - 1, jnp.int32))

            along = dust_step * row(c * TZ + level)
            return jnp.where(row(FLAG) > 0.0, mix + jnp.maximum(along if low else -along, 0.0), 0.0)

        for at in range(0, rows, ROWS):
            level = at // bins
            if at % bins == 0:
                u, v = (
                    dust_step * spread_rows(wind_ref[t, c * TZ + level : c * TZ + level + 1, :]) for c in range(2)
                )
                across, along = jnp.where(on_x, u, v), jnp.where(on_x, v, u)
                from_out = mix + jnp.maximum(jnp.where(low_side, across, -across), 0.0)
                from_corner = jnp.where(
                    first, mix + jnp.maximum(along, 0.0), jnp.where(last, mix + jnp.maximum(-along, 0.0), 0.0)
                )
                by_x = from_end(strip_x, end_x, 1, level, low_y)
                by_y = from_end(strip_y, end_y, 0, level, low_x)
            cells = lane_gather(
                cells_ref[cells_at + at : cells_at + at + ROWS, :], jnp.full((ROWS, LANES), cell_lane, jnp.int32)
            )
            more = jnp.where(lane == to_x, by_x * cells, jnp.where(lane == to_y, by_y * cells, 0.0))
            sums[n, at : at + ROWS, :] = (
                effect_ref[n, at : at + ROWS, :] + from_out * more + from_corner * lane_gather(more, corner)
            )
        sums[n, rows:, :] = effect_ref[n, rows:, :]

        @pl.when(owner_ref[t] >= 0)
        def _():
            copy(n, t).start()

    for n, (_, _, t) in enumerate(tiles):

        @pl.when(owner_ref[t] >= 0)
        def _():
            copy(n, t).wait()


def shifted(value, axis, steps):
    count = lax.axis_size(axis)
    return lax.ppermute(value, axis, [(source, (source + steps) % count) for source in range(count)])


def relay_rows(rows):
    return lax.all_to_all(rows, AXES, split_axis=0, concat_axis=0, tiled=True)


def exchange_borders(borders):
    east, west, north, south = borders
    return shifted(east, "gx", 1), shifted(west, "gx", -1), shifted(north, "gy", 1), shifted(south, "gy", -1)


def ring_call(kernel, tiles_x, tiles_y, rows, outs, scratch, name, hbm_in=0, hbm_out=0, aliases={}):
    smem = pl.BlockSpec(memory_space=pltpu.SMEM)
    vmem = pl.BlockSpec(memory_space=pltpu.VMEM)
    hbm = pl.BlockSpec(memory_space=pltpu.HBM)
    size = tiles_x * tiles_y * rows * LANES

    def call(owner_of_tile, *inputs):
        return pl.pallas_call(
            functools.partial(kernel, tiles_x=tiles_x, tiles_y=tiles_y),
            in_specs=[smem] + [hbm] * hbm_in + [vmem] * (len(inputs) - hbm_in),
            out_specs=[hbm] * hbm_out + [vmem] * (len(outs) - hbm_out),
            out_shape=outs,
            scratch_shapes=scratch,
            input_output_aliases=aliases,
            compiler_params=pltpu.CompilerParams(vmem_limit_bytes=32 << 20),
            cost_estimate=pl.CostEstimate(flops=16 * size, bytes_accessed=16 * size, transcendentals=0),
            name=name,
        )(owner_of_tile, *inputs)

    return call


def relay_strips(owner_of_tile, received, wind_send, wind_ring, settle_speed, bin_share, tiles_x, tiles_y):
    owners, both_rows, _ = received.shape
    rows = both_rows // 2
    per_home = tiles_x * tiles_y
    each = both_rows + ROWS
    ext = pltpu.VMEM(((tiles_x + 2) * (tiles_y + 2), rows, LANES), jnp.float32)
    all_rings = pltpu.VMEM((per_home, both_rows, LANES), jnp.float32)
    each_sem = pltpu.SemaphoreType.DMA((per_home,))
    settle_rows = jnp.broadcast_to(settle_speed[:, None], settle_speed.shape + (LANES,))
    share_rows = jnp.broadcast_to(bin_share[:, None], bin_share.shape + (LANES,))

    def call(kernel, outs, scratch, name, *inputs, **places):
        return ring_call(kernel, tiles_x, tiles_y, rows, outs, scratch, name, **places)(owner_of_tile, *inputs)

    along_x, along_y = tiles_y // 4, tiles_x // 4
    east, west, north, south = call(
        pack_borders_kernel,
        [f32(along_x * each, LANES)] * 2 + [f32(along_y * each, LANES)] * 2,
        [all_rings, each_sem],
        "pack_borders",
        in_hbm(received),
        wind_ring,
        hbm_in=1,
    )
    from_west, from_east, from_south, from_north = exchange_borders((east, west, north, south))
    wind_send, from_west, from_east, from_south, from_north = lax.optimization_barrier(
        (wind_send, from_west, from_east, from_south, from_north)
    )
    wind_recv = relay_rows(wind_send)
    top = (along_y - 1) * each
    across_low = jnp.concatenate([from_south[:rows], from_north[:rows]])
    across_high = jnp.concatenate([from_south[top : top + rows], from_north[top : top + rows]])
    corner_west, corner_east = shifted(across_high, "gx", 1), shifted(across_low, "gx", -1)
    (rings,) = call(gather_rings_kernel, [f32(per_home, both_rows, LANES)], [], "gather_rings", received)
    send_buffer = pltpu.HBM((owners, both_rows, LANES), jnp.float32)
    messages = (from_west, from_east, from_south, from_north)
    seen_send, corners = call(
        send_seen_kernel,
        [send_buffer, f32(4, both_rows, LANES)],
        [ext, all_rings]
        + [pltpu.VMEM((along_x, rows, LANES), jnp.float32)] * 2
        + [pltpu.VMEM((along_y, rows, LANES), jnp.float32)] * 2
        + [each_sem],
        "send_seen",
        rings, wind_ring, settle_rows, share_rows, east, west, north, south, *messages,
        hbm_out=1,
    )
    (seen_send,) = call(
        send_corners_kernel,
        [send_buffer],
        [pltpu.VMEM((4, both_rows, LANES), jnp.float32), pltpu.SemaphoreType.DMA((4,))],
        "send_corners",
        seen_send, corners, wind_ring, *messages, corner_west, corner_east,
        hbm_in=1,
        hbm_out=1,
        aliases={1: 0},
    )
    return wind_recv, relay_rows(seen_send)


def dust_kernel(home_ref, share_ref, settle_ref, dust_ref, shift_ref, wind_ref, out_ref, coef, *work, block, bins):
    lanes = len(work) // 2
    step = pl.program_id(0)
    _, lane = iotas()
    within = lane % TILE
    low_lanes, high_lanes = lane < TILE, lane >= LANES - TILE
    mix = dust_step * diffusion
    chunks = bins // ROWS
    settle = [dust_step * settle_ref[h * ROWS : (h + 1) * ROWS, :] for h in range(chunks)]
    share = [share_ref[h * ROWS : (h + 1) * ROWS, :] for h in range(chunks)]
    nothing = jnp.zeros((ROWS, LANES), jnp.float32)

    def prepare(k, j):
        held = work[2 * k]
        home = home_ref[step * block + j]
        plane = [wind_ref[home, p * ROWS : (p + 1) * ROWS, :] * dust_step for p in range(PLANES)]
        for level in range(TZ):
            u, v = plane[level], plane[TZ + level]
            coef[k, 0, level] = mix + jnp.maximum(u, 0.0)
            coef[k, 1, level] = mix + jnp.maximum(-u, 0.0)
            coef[k, 2, level] = jnp.where(within == 0, 0.0, mix + jnp.maximum(v, 0.0))
            coef[k, 3, level] = jnp.where(within == TILE - 1, 0.0, mix + jnp.maximum(-v, 0.0))
            coef[k, 4, level] = 1.0 - 6.0 * mix - jnp.abs(u) - jnp.abs(v)
            coef[k, 5, level] = plane[2 * TZ + level]
        coef[k, 6, 0] = plane[PLANES - 1]
        for r in range(ROWS):
            for level in range(TZ):
                at = (r * TZ + level) * bins
                held[at : at + bins, :] = dust_ref[j, pl.ds(r * TZ + level, bins, stride=ROWS * TZ), :]

    def shift(k):
        held, shifts = work[2 * k], work[2 * k + 1]
        shifts[...] = jnp.dot(
            jnp.concatenate(halves_of(held[...]), axis=1), shift_ref[...], preferred_element_type=jnp.float32
        )

    def update(k, j, substep):
        held, shifts = work[2 * k], work[2 * k + 1]
        for r in range(ROWS):
            for h in range(chunks):
                cells = [held[(r * TZ + level) * bins + h * ROWS :][:ROWS] for level in range(TZ)]
                for level in range(TZ):
                    at = (r * TZ + level) * bins + h * ROWS

                    def moved(which, rows_up=0):
                        first = at + rows_up * TZ * bins
                        return shifts[first : first + ROWS, which * LANES : (which + 1) * LANES]

                    def by(which):
                        return spread_rows(coef[k, which, level, r : r + 1, :])

                    before = nothing if r == 0 else moved(2, -1)
                    after = nothing if r == ROWS - 1 else moved(3, 1)
                    west = jnp.where(low_lanes, before, moved(2))
                    east = jnp.where(high_lanes, after, moved(3))
                    rise = by(5) - settle[h]
                    up = jnp.maximum(rise, 0.0)
                    mixed = mix + (up - rise if level == 0 else up)
                    value = (
                        (by(4) - jnp.abs(rise)) * cells[level]
                        + by(0) * west
                        + by(1) * east
                        + by(2) * moved(0)
                        + by(3) * moved(1)
                        + mixed * cells[1 - level]
                    )
                    if level == 0:
                        value = value + spread_rows(coef[k, 6, 0, r : r + 1, :]) * share[h]
                    if substep == 0:
                        held[at : at + ROWS, :] = value
                    else:
                        first = h * ROWS * ROWS * TZ + r * TZ + level
                        out_ref[j, pl.ds(first, ROWS, stride=ROWS * TZ), :] = value

    def some(i, carry):
        for k in range(lanes):
            prepare(k, i * lanes + k)
        for substep in range(2):
            for k in range(lanes):
                shift(k)
            for k in range(lanes):
                update(k, i * lanes + k, substep)
        return carry

    lax.fori_loop(0, block // lanes, some, 0)


def dust_inner(home_of_slot, dust, wind_recv, settle_speed, bin_share):
    slots, cells = dust.shape[:2]
    bins = settle_speed.shape[0]
    block = 8 if slots % 8 == 0 else 4
    lanes = 2
    smem = pl.BlockSpec(memory_space=pltpu.SMEM)
    vmem = pl.BlockSpec(memory_space=pltpu.VMEM)
    tile = pl.BlockSpec((block, cells, LANES), lambda i: (i, 0, 0))
    settle = jnp.broadcast_to(settle_speed[:, None], (bins, LANES))
    share = jnp.broadcast_to(bin_share[:, None], (bins, LANES))
    return pl.pallas_call(
        functools.partial(dust_kernel, block=block, bins=bins),
        grid=(slots // block,),
        in_specs=[smem, vmem, vmem, tile, vmem, vmem],
        out_specs=tile,
        out_shape=pltpu.HBM(dust.shape, jnp.float32),
        scratch_shapes=[pltpu.VMEM((lanes, PLANES, TZ, ROWS, LANES), jnp.float32)]
        + [pltpu.VMEM((cells, LANES), jnp.float32), pltpu.VMEM((cells, 4 * LANES), jnp.float32)] * lanes,
        compiler_params=pltpu.CompilerParams(vmem_limit_bytes=24 << 20),
        cost_estimate=pl.CostEstimate(flops=120 * dust.size, bytes_accessed=dust.size * 12, transcendentals=0),
        name="dust_inner",
    )(home_of_slot, share, settle, in_hbm(dust), jnp.asarray(shift_matrix()), wind_recv)


def dust_outer_kernel(
    home_ref, inner_hbm, matrix_ref, effect_hbm, out_hbm, effect, dust, effect_sems, load_sems, sems, *, block, bins
):
    slots = dust.shape[0]
    rows = TZ * bins

    def arrive(s):
        return pltpu.make_async_copy(effect_hbm.at[home_ref[s]], effect.at[s], effect_sems.at[s])

    def load(i):
        some = pl.ds(i * block, block)
        return pltpu.make_async_copy(inner_hbm.at[some], dust.at[some], load_sems.at[i])

    def store(i):
        some = pl.ds(i * block, block)
        return pltpu.make_async_copy(dust.at[some], out_hbm.at[some], sems.at[i])

    def start(i, carry):
        for j in range(block):
            arrive(i * block + j).start()
        load(i).start()
        return carry

    lax.fori_loop(0, slots // block, start, 0)

    def one(i, carry):
        for j in range(block):
            arrive(i * block + j).wait()
        rings = jnp.concatenate(
            [
                jnp.concatenate([effect[i * block + j, depth * rows : (depth + 1) * rows, :] for depth in range(2)], axis=1)
                for j in range(block)
            ],
            axis=0,
        )
        added = jnp.dot(
            jnp.concatenate(halves_of(rings), axis=1), matrix_ref[...], preferred_element_type=jnp.float32
        )
        load(i).wait()
        for j in range(block):
            for r in range(ROWS):
                for level in range(TZ):
                    at = pl.ds(r * TZ + level, bins, stride=ROWS * TZ)
                    first = j * rows + level * bins
                    dust[i * block + j, at, :] += added[first : first + bins, r * LANES : (r + 1) * LANES]
        store(i).start()
        return carry

    lax.fori_loop(0, slots // block, one, 0)
    for i in range(slots // block):
        store(i).wait()


def dust_outer(home_of_slot, inner, effect, bins):
    slots = inner.shape[0]
    block = 8 if slots % 8 == 0 else 4
    hbm = pl.BlockSpec(memory_space=pltpu.HBM)
    vmem = pl.BlockSpec(memory_space=pltpu.VMEM)
    return pl.pallas_call(
        functools.partial(dust_outer_kernel, block=block, bins=bins),
        in_specs=[pl.BlockSpec(memory_space=pltpu.SMEM), hbm, vmem, hbm],
        out_specs=hbm,
        out_shape=pltpu.HBM(inner.shape, jnp.float32),
        scratch_shapes=[
            pltpu.VMEM((slots,) + effect.shape[1:], jnp.float32),
            pltpu.VMEM(inner.shape, jnp.float32),
            pltpu.SemaphoreType.DMA((slots,)),
            pltpu.SemaphoreType.DMA((slots // block,)),
            pltpu.SemaphoreType.DMA((slots // block,)),
        ],
        compiler_params=pltpu.CompilerParams(vmem_limit_bytes=24 << 20),
        cost_estimate=pl.CostEstimate(flops=2 * inner.size, bytes_accessed=inner.size * 8, transcendentals=0),
        name="dust_outer",
    )(home_of_slot, in_hbm(inner), jnp.asarray(spread_matrix()), in_hbm(effect))


def per_device(velocity, threshold, dust_mass, settle_speed, bin_share, active_tiles, tile_owner):
    owners = lax.axis_size(AXES)
    grid_cols = lax.axis_size("gy")
    self_index = lax.axis_index(AXES)
    slots, bins = dust_mass.shape[:2]
    tiles_x = velocity.shape[2] // TILE
    tiles_y = velocity.shape[3] // TILE
    per_home = tiles_x * tiles_y
    tiles_across = tiles_y * grid_cols

    tile_x = active_tiles // tiles_across
    tile_y = active_tiles % tiles_across
    home_dev = tile_x // tiles_x * grid_cols + tile_y // tiles_y
    local_tile = tile_x % tiles_x * tiles_y + tile_y % tiles_y
    own_slot = tile_owner - self_index * slots
    mine = jnp.where(home_dev == self_index, local_tile, -1)
    slot_ids = jnp.arange(slots, dtype=jnp.int32)
    home_of_slot = jnp.sum(jnp.where(own_slot[None, :] == slot_ids[:, None], home_dev[None, :], 0), axis=1)
    tile_ids = jnp.arange(per_home, dtype=jnp.int32)
    owner_of_tile = jnp.max(
        jnp.where(mine[None, :] == tile_ids[:, None], (tile_owner // slots)[None, :], -1), axis=1
    )

    dust = dust_mass.reshape(slots, bins, TZ, ROWS, LANES).transpose(0, 1, 3, 2, 4)
    dust = dust.reshape(slots, bins * ROWS * TZ, LANES)

    xlo, xhi, ylo, yhi = exchange_borders(wind_faces(velocity))

    strips_send = dust_strips(home_of_slot, dust, bins, owners)
    strips_send, xlo, xhi, ylo, yhi = lax.optimization_barrier((strips_send, xlo, xhi, ylo, yhi))
    strips = relay_rows(strips_send)
    new_velocity, wind_send, wind_ring = wind_step(
        owner_of_tile, velocity, xlo, xhi, ylo, yhi, threshold, owners
    )
    strips, wind_send, wind_ring = lax.optimization_barrier((strips, wind_send, wind_ring))
    wind_recv, effect = relay_strips(
        owner_of_tile, strips, wind_send, wind_ring, settle_speed, bin_share, tiles_x, tiles_y
    )
    inner = dust_inner(home_of_slot, dust, wind_recv, settle_speed, bin_share)
    out = dust_outer(home_of_slot, inner, effect, bins)
    out = out.reshape(slots, bins, ROWS, TZ, LANES).transpose(0, 1, 3, 2, 4).reshape(dust_mass.shape)
    return new_velocity, out


def solution(mesh):
    in_specs = (
        P(None, None, "gx", "gy"),
        P("gx", "gy"),
        P(AXES, None, None, None),
        P(),
        P(),
        P(),
        P(),
    )
    out_specs = (P(None, None, "gx", "gy"), P(AXES, None, None, None))
    return jax.shard_map(
        per_device, mesh=mesh, in_specs=in_specs, out_specs=out_specs, check_vma=False
    )
```

```python
import functools

import jax
import jax.numpy as jnp
import ml_dtypes
import numpy as np
from jax import lax
from jax.experimental import pallas as pl
from jax.experimental.pallas import tpu as pltpu
from jax.sharding import PartitionSpec as P

TZ = 2
TILE = 32
LANES = 128
ROWS = TILE * TILE // LANES
PLANES = 7
AXES = ("gx", "gy")

time_step = 0.1
viscosity = 0.2
dust_step = 0.1
diffusion = 0.1
roughness = 0.5
emit_rate = 0.5

WEST, SOUTH, NORTH, EAST = range(4)


def iotas(shape=(ROWS, LANES)):
    return lax.broadcasted_iota(jnp.int32, shape, 0), lax.broadcasted_iota(jnp.int32, shape, 1)


def lane_gather(x, index):
    return jnp.take_along_axis(x, index, axis=1)


def ring_pattern(depth):
    row, lane = iotas()
    group, within = lane // TILE, lane % TILE
    side = jnp.where(group == SOUTH, depth, TILE - 1 - depth)
    index = (within % 4) * TILE + side
    index = jnp.where(group == WEST, depth * TILE + within, index)
    index = jnp.where(group == EAST, (3 - depth) * TILE + within, index)
    source = jnp.where(group == WEST, 0, jnp.where(group == EAST, ROWS - 1, within // 4))
    return index, row == source


def ring_of(x, pattern):
    index, taken = pattern
    return jnp.sum(jnp.where(taken, lane_gather(x, index), 0.0), axis=0, keepdims=True)


def spread_rows(row):
    return jnp.broadcast_to(row, (ROWS, LANES))


def f32(*shape):
    return jax.ShapeDtypeStruct(shape, jnp.float32)


def in_hbm(x):
    return pltpu.with_memory_space_constraint(x, pltpu.HBM)


def halves_of(x):
    high = x.astype(jnp.bfloat16)
    return high, (x - high.astype(jnp.float32)).astype(jnp.bfloat16)


def moves(sources, width=LANES):
    lanes = np.arange(width)[:, None]
    once = (lanes == np.asarray(sources)[None, :]).astype(ml_dtypes.bfloat16)
    return np.concatenate([once, once], axis=0)


def ring_matrix():
    lane = np.arange(LANES)
    group, within = lane // TILE, lane % TILE
    blocks = []
    for r in range(ROWS):
        columns = []
        for depth in range(2):
            side = np.where(group == SOUTH, depth, TILE - 1 - depth)
            source = np.where(within // 4 == r, (within % 4) * TILE + side, -1)
            source = np.where(group == WEST, depth * TILE + within if r == 0 else -1, source)
            source = np.where(group == EAST, (3 - depth) * TILE + within if r == ROWS - 1 else -1, source)
            columns.append(source)
        blocks.append(moves(np.concatenate(columns)))
    return np.concatenate(blocks, axis=0)


def shift_matrix():
    lane = np.arange(LANES)
    return moves(np.concatenate([(lane + d) % LANES for d in (-1, 1, -TILE, TILE)]))


def spread_matrix():
    i, j = np.divmod(np.arange(TILE * TILE), TILE)
    source = np.full(TILE * TILE, -1)
    for depth in (1, 0):
        at = depth * LANES
        source = np.where(j == depth, at + SOUTH * TILE + i, source)
        source = np.where(j == TILE - 1 - depth, at + NORTH * TILE + i, source)
        source = np.where(i == depth, at + WEST * TILE + j, source)
        source = np.where(i == TILE - 1 - depth, at + EAST * TILE + j, source)
    return moves(source, 2 * LANES)


def strips_kernel(home_ref, dust_hbm, matrix_ref, send_ref, dust, rings, load_sems, sems, *, block, bins):
    slots = rings.shape[0]
    each = TZ * bins

    def load(i):
        some = pl.ds(i * block, block)
        return pltpu.make_async_copy(dust_hbm.at[some], dust.at[some], load_sems.at[i])

    def send(s):
        return pltpu.make_async_copy(rings.at[s], send_ref.at[home_ref[s]], sems.at[s])

    for i in range(slots // block):
        load(i).start()

    def one(i, carry):
        load(i).wait()
        parts = []
        for r in range(ROWS):
            x = jnp.concatenate(
                [
                    dust[i * block + j, pl.ds(r * TZ + level, bins, stride=ROWS * TZ), :]
                    for j in range(block)
                    for level in range(TZ)
                ],
                axis=0,
            )
            parts += halves_of(x)
        found = jnp.dot(
            jnp.concatenate(parts, axis=1), matrix_ref[...], preferred_element_type=jnp.float32
        )
        for j in range(block):
            for depth in range(2):
                rings[i * block + j, depth * each : (depth + 1) * each, :] = found[
                    j * each : (j + 1) * each, depth * LANES : (depth + 1) * LANES
                ]
            send(i * block + j).start()
        return carry

    lax.fori_loop(0, slots // block, one, 0)

    def wait(s, carry):
        send(s).wait()
        return carry

    lax.fori_loop(0, slots, wait, 0)


def dust_strips(home_of_slot, dust, bins, owners):
    slots = dust.shape[0]
    block = 14 if slots % 14 == 0 else 4
    rows = 2 * bins * TZ
    matrix = jnp.asarray(ring_matrix())
    hbm = pl.BlockSpec(memory_space=pltpu.HBM)
    return pl.pallas_call(
        functools.partial(strips_kernel, block=block, bins=bins),
        in_specs=[pl.BlockSpec(memory_space=pltpu.SMEM), hbm, pl.BlockSpec(memory_space=pltpu.VMEM)],
        out_specs=hbm,
        out_shape=pltpu.HBM((owners, rows, LANES), jnp.float32),
        scratch_shapes=[
            pltpu.VMEM(dust.shape, jnp.float32),
            pltpu.VMEM((slots, rows, LANES), jnp.float32),
            pltpu.SemaphoreType.DMA((slots // block,)),
            pltpu.SemaphoreType.DMA((slots,)),
        ],
        compiler_params=pltpu.CompilerParams(vmem_limit_bytes=32 << 20),
        cost_estimate=pl.CostEstimate(
            flops=20 * dust.size, bytes_accessed=dust.size * 4 + slots * rows * LANES * 4, transcendentals=0
        ),
        name="dust_strips",
    )(home_of_slot, in_hbm(dust), matrix)


def faces_kernel(vel_ref, x_last_ref, x_first_ref, y_last_ref, y_first_ref, wind, sems):
    fields, nx, ny = vel_ref.shape
    copies = [pltpu.make_async_copy(vel_ref.at[f], wind.at[f], sems.at[f]) for f in range(fields)]
    for copy in copies:
        copy.start()
    lane = lax.broadcasted_iota(jnp.int32, (nx, LANES), 1)
    for f, copy in enumerate(copies):
        copy.wait()
        x_first_ref[f : f + 1, :] = wind[f, 0:1, :]
        x_last_ref[f : f + 1, :] = wind[f, nx - 1 : nx, :]
        both = pltpu.roll(jnp.where(lane < LANES // 2, wind[f, :, :LANES], wind[f, :, ny - LANES :]), f + 1, 1)
        if f == 0:
            y_first_ref[...], y_last_ref[...] = both, both
        else:
            y_first_ref[...] = jnp.where(lane == f + 1, both, y_first_ref[...])
            y_last_ref[...] = jnp.where(lane == f, both, y_last_ref[...])


def wind_faces(velocity):
    comps, levels, nx, ny = velocity.shape
    fields = comps * levels
    vmem = pl.BlockSpec(memory_space=pltpu.VMEM)
    return pl.pallas_call(
        faces_kernel,
        in_specs=[pl.BlockSpec(memory_space=pltpu.HBM)],
        out_specs=[vmem] * 4,
        out_shape=[f32(fields, ny)] * 2 + [f32(nx, LANES)] * 2,
        scratch_shapes=[pltpu.VMEM((fields, nx, ny), jnp.float32), pltpu.SemaphoreType.DMA((fields,))],
        compiler_params=pltpu.CompilerParams(vmem_limit_bytes=32 << 20),
        cost_estimate=pl.CostEstimate(flops=velocity.size, bytes_accessed=velocity.size * 4, transcendentals=0),
        name="wind_faces",
    )(in_hbm(velocity.reshape(fields, nx, ny)))


def wind_kernel(
    owner_ref, vel_ref, xlo_ref, xhi_ref, ylo_ref, yhi_ref, thr_ref,
    new_ref, send_ref, ring_ref, padded, strip, tiles, load_sem, sems, *, levels
):
    fields, nx, ny = new_ref.shape
    load = pltpu.make_async_copy(vel_ref, padded.at[:, pl.ds(8, nx), :], load_sem)
    load.start()
    load.wait()
    for f in range(fields):
        padded[f, 7:8, :] = xlo_ref[f : f + 1, :]
        padded[f, 8 + nx : 9 + nx, :] = xhi_ref[f : f + 1, :]
    half = 16
    halves = ny // LANES
    tiles_y = ny // TILE
    patterns = [ring_pattern(0), ring_pattern(1)]
    _, lane8 = iotas()
    group = lane8 // TILE

    def one_strip(ix, carry):
        for sub in range(TILE // half):
            base = pl.multiple_of(ix * TILE + sub * half, 8)
            lane = lax.broadcasted_iota(jnp.int32, (half, ny), 1)
            low = {}
            faces = [ref[pl.ds(base, half), :] for ref in (ylo_ref, yhi_ref)]

            def face(which, f, to):
                moved = pltpu.roll(faces[which], (to - f - which) % LANES, 1) if f + which != to else faces[which]
                return jnp.concatenate([moved] * halves, axis=1)

            for z in range(levels):
                u, v, w = (padded[c * levels + z, pl.ds(base + 8, half), :] for c in range(3))
                for c in range(3):
                    f = c * levels + z
                    block = padded[f, pl.ds(base, half + 16), :]
                    centre = (u, v, w)[c]
                    west = pltpu.roll(block, 1, 0)[8 : 8 + half]
                    east = pltpu.roll(block, half + 15, 0)[8 : 8 + half]
                    south = jnp.where(lane == 0, face(0, f, 0), pltpu.roll(centre, 1, 1))
                    north = jnp.where(lane == ny - 1, face(1, f, LANES - 1), pltpu.roll(centre, ny - 1, 1))
                    lower = -centre if z == 0 else padded[f - 1, pl.ds(base + 8, half), :]
                    upper = centre if z == levels - 1 else padded[f + 1, pl.ds(base + 8, half), :]
                    carried = 0.5 * (u * (east - west) + v * (north - south) + w * (upper - lower))
                    spread = east + west + north + south + upper + lower - 6.0 * centre
                    new = centre + time_step * (viscosity * spread - carried)
                    new_ref[f, pl.ds(base, half), :] = new
                    if z < TZ:
                        low[c * TZ + z] = new
            stress = roughness * (low[0] * low[0] + low[TZ] * low[TZ])
            low[PLANES - 1] = emit_rate * stress * jnp.maximum(
                stress - thr_ref[pl.ds(base, half), :], 0.0
            )
            for p in range(PLANES):
                for h in range(halves):
                    strip[p * halves + h, sub * half : (sub + 1) * half, :] = low[p][
                        :, h * LANES : (h + 1) * LANES
                    ]
        for p in range(PLANES):
            for h in range(halves):
                parts = [strip[p * halves + h, pl.ds(k, ROWS, stride=4), :] for k in range(4)]
                for t in range(4):
                    tile = ix * tiles_y + h * 4 + t
                    cells = pltpu.roll(parts[0], (-t * TILE) % LANES, 1) if t else parts[0]
                    for k in range(1, 4):
                        moved = pltpu.roll(parts[k], ((k - t) * TILE) % LANES, 1) if k != t else parts[k]
                        cells = jnp.where(group == k, moved, cells)
                    tiles[tile, p * ROWS : (p + 1) * ROWS, :] = cells
                    for depth in range(2):
                        ring_ref[tile, depth * 8 + p : depth * 8 + p + 1, :] = ring_of(cells, patterns[depth])

        def send(t, inner):
            tile = ix * tiles_y + t
            owner = owner_ref[tile]

            @pl.when(owner >= 0)
            def _():
                pltpu.make_async_copy(tiles.at[tile], send_ref.at[owner], sems.at[tile]).start()

            return inner

        lax.fori_loop(0, tiles_y, send, 0)
        return carry

    lax.fori_loop(0, nx // TILE, one_strip, 0)

    def wait(tile, carry):
        owner = owner_ref[tile]

        @pl.when(owner >= 0)
        def _():
            pltpu.make_async_copy(tiles.at[tile], send_ref.at[owner], sems.at[tile]).wait()

        return carry

    lax.fori_loop(0, tiles.shape[0], wait, 0)


def wind_step(owner_of_tile, velocity, xlo, xhi, ylo, yhi, threshold, owners):
    comps, levels, nx, ny = velocity.shape
    fields = comps * levels
    per_home = (nx // TILE) * (ny // TILE)
    smem = pl.BlockSpec(memory_space=pltpu.SMEM)
    hbm = pl.BlockSpec(memory_space=pltpu.HBM)
    vmem = pl.BlockSpec(memory_space=pltpu.VMEM)
    new, send, ring = pl.pallas_call(
        functools.partial(wind_kernel, levels=levels),
        in_specs=[smem, hbm, vmem, vmem, vmem, vmem, vmem],
        out_specs=[vmem, hbm, vmem],
        out_shape=[
            f32(fields, nx, ny),
            pltpu.HBM((owners, PLANES * ROWS, LANES), jnp.float32),
            f32(per_home, 16, LANES),
        ],
        scratch_shapes=[
            pltpu.VMEM((fields, nx + 16, ny), jnp.float32),
            pltpu.VMEM((PLANES * (ny // LANES), TILE, LANES), jnp.float32),
            pltpu.VMEM((per_home, PLANES * ROWS, LANES), jnp.float32),
            pltpu.SemaphoreType.DMA,
            pltpu.SemaphoreType.DMA((per_home,)),
        ],
        compiler_params=pltpu.CompilerParams(vmem_limit_bytes=40 << 20),
        cost_estimate=pl.CostEstimate(
            flops=40 * velocity.size, bytes_accessed=velocity.size * 10, transcendentals=0
        ),
        name="wind_step",
    )(
        owner_of_tile,
        in_hbm(velocity.reshape(fields, nx, ny)),
        xlo,
        xhi,
        ylo,
        yhi,
        threshold,
    )
    return new.reshape(velocity.shape), send, ring


def border_tiles(tiles_x, tiles_y):
    return (
        (EAST, [(tiles_x - 1) * tiles_y + n for n in range(tiles_y)]),
        (WEST, [n for n in range(tiles_y)]),
        (NORTH, [n * tiles_y + tiles_y - 1 for n in range(tiles_x)]),
        (SOUTH, [n * tiles_y for n in range(tiles_x)]),
    )


def fill_halo(ext, strips, tiles_x, tiles_y):
    wide = tiles_y + 2
    for strip_of, side, places in (
        (strips[0], EAST, [n + 1 for n in range(tiles_y)]),
        (strips[1], WEST, [(tiles_x + 1) * wide + n + 1 for n in range(tiles_y)]),
        (strips[2], NORTH, [(n + 1) * wide for n in range(tiles_x)]),
        (strips[3], SOUTH, [(n + 1) * wide + tiles_y + 1 for n in range(tiles_x)]),
    ):
        for n, place in enumerate(places):
            strip = strip_of(n // 4)
            if n % 4 != side:
                strip = pltpu.roll(strip, ((side - n % 4) * TILE) % LANES, 1)
            ext[place] = strip


def seen_by(ext, place, wide):
    west, east = ext[place - wide], ext[place + wide]
    south, north = ext[place - 1], ext[place + 1]
    lane = lax.broadcasted_iota(jnp.int32, west.shape, 1)
    up = pltpu.roll(jnp.where(lane < 2 * TILE, north, west), TILE, 1)
    down = pltpu.roll(jnp.where(lane < 2 * TILE, east, south), LANES - TILE, 1)
    return jnp.where((lane // TILE) % 2 == 0, up, down)


FLAG = 7


def pack_borders_kernel(owner_ref, recv_ref, wind_ref, *refs, tiles_x, tiles_y):
    *outs, rings, sems = refs
    both_rows = rings.shape[1]
    borders = border_tiles(tiles_x, tiles_y)
    used = list(dict.fromkeys(t for _, tiles in borders for t in tiles))

    def copy(t):
        return pltpu.make_async_copy(recv_ref.at[jnp.maximum(owner_ref[t], 0)], rings.at[t], sems.at[t])

    for t in used:
        copy(t).start()
    for t in used:
        copy(t).wait()

    lane = lax.broadcasted_iota(jnp.int32, (both_rows, LANES), 1) // TILE
    row8, lane8 = iotas()
    group8 = lane8 // TILE
    for out, (side, tiles) in zip(outs, borders):
        for g in range(len(tiles) // 4):
            strips = winds = None
            for q in range(4):
                t = tiles[4 * g + q]
                active = owner_ref[t] >= 0
                strip, wind = jnp.where(active, rings[t], 0.0), wind_ref[t, :ROWS, :]
                if q != side:
                    strip = pltpu.roll(strip, ((q - side) * TILE) % LANES, 1)
                    wind = pltpu.roll(wind, ((q - side) * TILE) % LANES, 1)
                wind = jnp.where(row8 == FLAG, jnp.where(active, 1.0, 0.0), wind)
                strips = strip if strips is None else jnp.where(lane == q, strip, strips)
                winds = wind if winds is None else jnp.where(group8 == q, wind, winds)
            at = g * (both_rows + ROWS)
            out[at : at + both_rows, :] = strips
            out[at + both_rows : at + both_rows + ROWS, :] = winds


def gather_rings_kernel(owner_ref, recv_ref, rings_ref, *, tiles_x, tiles_y):
    def one(t, carry):
        owner = owner_ref[t]
        rings = recv_ref[jnp.maximum(owner, 0)]
        rings_ref[t] = jnp.where(owner >= 0, rings, 0.0)
        return carry

    lax.fori_loop(0, tiles_x * tiles_y, one, 0)


def fill_tiles(ext, tile, tiles_x, tiles_y):
    def inner(t, carry):
        ext[place_of(t, tiles_y)] = tile(t)
        return carry

    lax.fori_loop(0, tiles_x * tiles_y, inner, 0)


def place_of(t, tiles_y):
    return (t // tiles_y + 1) * (tiles_y + 2) + t % tiles_y + 1


def corner_index(inset):
    _, lane = iotas()
    group, within = lane // TILE, lane % TILE
    on_x = (group == WEST) | (group == EAST)
    low = within < TILE // 2
    along = jnp.where((group == EAST) | (group == NORTH), TILE - 1 - inset, inset)
    return jnp.where(on_x, jnp.where(low, SOUTH, NORTH), jnp.where(low, WEST, EAST)) * TILE + along


def ring_effect(t, wind_ref, settle_ref, seen, seen_later):
    row, lane = iotas()
    group, within = lane // TILE, lane % TILE
    on_x = (group == WEST) | (group == EAST)
    low_side = (group == WEST) | (group == SOUTH)
    first, last = within == 0, within == TILE - 1
    second, last_but_one = within == 1, within == TILE - 2
    corner, inner = corner_index(0), corner_index(1)
    rows = seen.shape[0]
    bins = rows // TZ
    mix = dust_step * diffusion

    def wind(depth, p):
        return dust_step * spread_rows(wind_ref[t, depth * 8 + p : depth * 8 + p + 1, :])

    inflow, later_in = [], []
    coefs = []
    for level in range(TZ):
        u, v, w = (wind(0, c * TZ + level) for c in range(3))
        across, along = jnp.where(on_x, u, v), jnp.where(on_x, v, u)
        outward = jnp.where(low_side, across, -across)
        from_out = mix + jnp.maximum(outward, 0.0)
        from_in = jnp.where(first | last, mix + jnp.maximum(-outward, 0.0), 0.0)
        from_before, from_after = mix + jnp.maximum(along, 0.0), mix + jnp.maximum(-along, 0.0)
        from_corner = jnp.where(first, from_before, jnp.where(last, from_after, 0.0))
        from_before = jnp.where(first, 0.0, from_before)
        from_after = jnp.where(last, 0.0, from_after)
        keep = 1.0 - 6.0 * mix - jnp.abs(u) - jnp.abs(v)
        u2, v2 = (wind(1, c * TZ + level) for c in range(2))
        across2, along2 = jnp.where(on_x, u2, v2), jnp.where(on_x, v2, u2)
        deep_out = mix + jnp.maximum(jnp.where(low_side, across2, -across2), 0.0)
        deep_corner = jnp.where(
            second, mix + jnp.maximum(along2, 0.0), jnp.where(last_but_one, mix + jnp.maximum(-along2, 0.0), 0.0)
        )
        coefs.append((w, keep, from_in, from_before, from_after, deep_out, deep_corner))
        for at in range(level * bins, (level + 1) * bins, ROWS):
            for view, taken in ((seen, inflow), (seen_later, later_in)):
                g = view[at : at + ROWS, :]
                taken.append(from_out * g + from_corner * lane_gather(g, corner))
    outer, deep = [], []
    for n, e in enumerate(inflow):
        level, bin_at = n * ROWS // bins, n * ROWS % bins
        w, keep, from_in, from_before, from_after, deep_out, deep_corner = coefs[level]
        other = inflow[n + len(inflow) // 2 if level == 0 else n - len(inflow) // 2]
        rise = w - dust_step * settle_ref[bin_at : bin_at + ROWS, :]
        up = jnp.maximum(rise, 0.0)
        down = up - rise
        turned = lane_gather(e, inner)
        outer.append(
            (keep - up - down) * e
            + from_before * pltpu.roll(e, 1, 1)
            + from_after * pltpu.roll(e, LANES - 1, 1)
            + from_in * turned
            + (mix + (down if level == 0 else up)) * other
            + later_in[n]
        )
        deep.append(deep_out * e + deep_corner * turned)
    return outer, deep


def advance_ring(t, owner_ref, rings_ref, wind_ref, settle_ref, share_ref, seen):
    _, lane = iotas()
    group, within = lane // TILE, lane % TILE
    on_x = (group == WEST) | (group == EAST)
    first, last = within == 0, within == TILE - 1
    corner = corner_index(0)
    rows = rings_ref.shape[1] // 2
    bins = rows // TZ
    uplift = dust_step * spread_rows(wind_ref[t, PLANES - 1 : PLANES, :])
    mix = dust_step * diffusion
    active = owner_ref[t] >= 0
    chunks = []
    for at in range(0, rows, ROWS):
        level, bin_at = at // bins, at % bins
        if bin_at == 0:
            u, v, w = (
                dust_step * spread_rows(wind_ref[t, c * TZ + level : c * TZ + level + 1, :]) for c in range(3)
            )
            from_west = mix + jnp.maximum(u, 0.0)
            from_east = mix + jnp.maximum(-u, 0.0)
            from_south = mix + jnp.maximum(v, 0.0)
            from_north = mix + jnp.maximum(-v, 0.0)
            keep = 1.0 - 6.0 * mix - jnp.abs(u) - jnp.abs(v)
        q = rings_ref[t, at : at + ROWS, :]
        deep = rings_ref[t, rows + at : rows + at + ROWS, :]
        out = seen[at : at + ROWS, :]
        beyond = lane_gather(out, corner)
        before = jnp.where(first, beyond, pltpu.roll(q, 1, 1))
        after = jnp.where(last, beyond, pltpu.roll(q, LANES - 1, 1))
        west = jnp.where(group == WEST, out, jnp.where(group == EAST, deep, before))
        east = jnp.where(group == WEST, deep, jnp.where(group == EAST, out, after))
        south = jnp.where(on_x, before, jnp.where(group == SOUTH, out, deep))
        north = jnp.where(on_x, after, jnp.where(group == SOUTH, deep, out))
        other_at = (1 - level) * bins + bin_at
        other = rings_ref[t, other_at : other_at + ROWS, :]
        rise = w - dust_step * settle_ref[bin_at : bin_at + ROWS, :]
        up = jnp.maximum(rise, 0.0)
        down = up - rise
        new = (
            (keep - up - down) * q
            + from_west * west
            + from_east * east
            + from_south * south
            + from_north * north
            + (mix + (down if level == 0 else up)) * other
        )
        if level == 0:
            new = new + uplift * share_ref[bin_at : bin_at + ROWS, :]
        chunks.append(jnp.where(active, new, 0.0))
    return chunks


def advance_strip(side, message, ours, settle_ref, share_ref, out, rows):
    _, lane = iotas()
    bins = rows // TZ
    each = 2 * rows + ROWS
    groups = out.shape[0]
    mix = dust_step * diffusion
    for g in range(groups):
        wind_at = g * each + 2 * rows

        def wind_row(p):
            return spread_rows(message[wind_at + p : wind_at + p + 1, :])

        for at in range(0, rows, ROWS):
            level, bin_at = at // bins, at % bins
            u, v, w = (dust_step * wind_row(c * TZ + level) for c in range(3))

            def cells(group, first):
                return message[group * each + first : group * each + first + ROWS, :]

            q = cells(g, at)
            deep = cells(g, rows + at)
            near = ours[g * each + at : g * each + at + ROWS, :]
            low = 0.0 if g == 0 else pltpu.roll(cells(g - 1, at), 1, 1)
            high = 0.0 if g == groups - 1 else pltpu.roll(cells(g + 1, at), LANES - 1, 1)
            before = jnp.where(lane == 0, low, pltpu.roll(q, 1, 1))
            after = jnp.where(lane == LANES - 1, high, pltpu.roll(q, LANES - 1, 1))
            across = (deep, near) if side in (WEST, SOUTH) else (near, deep)
            (west, east), (south, north) = (
                (across, (before, after)) if side in (WEST, EAST) else ((before, after), across)
            )
            other = cells(g, (1 - level) * bins + bin_at)
            rise = w - dust_step * settle_ref[bin_at : bin_at + ROWS, :]
            up = jnp.maximum(rise, 0.0)
            down = up - rise
            new = (
                (1.0 - 6.0 * mix - jnp.abs(u) - jnp.abs(v) - up - down) * q
                + (mix + jnp.maximum(u, 0.0)) * west
                + (mix + jnp.maximum(-u, 0.0)) * east
                + (mix + jnp.maximum(v, 0.0)) * south
                + (mix + jnp.maximum(-v, 0.0)) * north
                + (mix + (down if level == 0 else up)) * other
            )
            if level == 0:
                new = new + dust_step * wind_row(PLANES - 1) * share_ref[bin_at : bin_at + ROWS, :]
            out[g, at : at + ROWS, :] = jnp.where(wind_row(FLAG) > 0.0, new, 0.0)


def send_seen_kernel(
    owner_ref, rings_ref, wind_ref, settle_ref, share_ref, e_ref, w_ref, n_ref, s_ref, fw_ref, fe_ref, fs_ref, fn_ref,
    send_ref, corner_ref, ext, both, lw_ref, le_ref, ls_ref, ln_ref, sems, *, tiles_x, tiles_y
):
    rows = rings_ref.shape[1] // 2
    wide = tiles_y + 2
    each = 2 * rows + ROWS
    messages = (fw_ref, fe_ref, fs_ref, fn_ref)
    later = (lw_ref, le_ref, ls_ref, ln_ref)

    def place(t):
        return place_of(t, tiles_y)

    fill_halo(
        ext, [lambda g, m=m: m[g * each : g * each + rows, :] for m in messages], tiles_x, tiles_y
    )
    fill_tiles(ext, lambda t: rings_ref[t, :rows, :], tiles_x, tiles_y)

    def before(t, carry):
        both[t, :rows, :] = seen_by(ext, place(t), wide)
        return carry

    lax.fori_loop(0, tiles_x * tiles_y, before, 0)

    def advance(i, carry):
        for t in (2 * i, 2 * i + 1):
            chunks = advance_ring(t, owner_ref, rings_ref, wind_ref, settle_ref, share_ref, both[t, :rows, :])
            for n, chunk in enumerate(chunks):
                ext[place(t), n * ROWS : (n + 1) * ROWS, :] = chunk
        return carry

    lax.fori_loop(0, tiles_x * tiles_y // 2, advance, 0)

    for side, message, ours, out in zip(
        (WEST, EAST, SOUTH, NORTH), messages, (w_ref, e_ref, s_ref, n_ref), later
    ):
        advance_strip(side, message, ours, settle_ref, share_ref, out, rows)
    fill_halo(ext, [lambda g, m=m: m[g] for m in later], tiles_x, tiles_y)

    def copy(t):
        return pltpu.make_async_copy(both.at[t], send_ref.at[owner_ref[t]], sems.at[t])

    def sent_now(t):
        x, y = t // tiles_y, t % tiles_y
        at_corner = ((x == 0) | (x == tiles_x - 1)) & ((y == 0) | (y == tiles_y - 1))
        return (owner_ref[t] >= 0) & jnp.logical_not(at_corner)

    def after(t, carry):
        effect = ring_effect(t, wind_ref, settle_ref, both[t, :rows, :], seen_by(ext, place(t), wide))
        for depth, chunks in enumerate(effect):
            for n, chunk in enumerate(chunks):
                both[t, depth * rows + n * ROWS : depth * rows + (n + 1) * ROWS, :] = chunk

        @pl.when(sent_now(t))
        def _():
            copy(t).start()

        return carry

    lax.fori_loop(0, tiles_x * tiles_y, after, 0)
    for n, (_, _, t) in enumerate(corner_tiles(tiles_x, tiles_y)):
        corner_ref[n] = both[t]

    def wait(t, carry):
        @pl.when(sent_now(t))
        def _():
            copy(t).wait()

        return carry

    lax.fori_loop(0, tiles_x * tiles_y, wait, 0)


def corner_tiles(tiles_x, tiles_y):
    return [
        (side_x, side_y, x * tiles_y + y)
        for side_x, x in ((WEST, 0), (EAST, tiles_x - 1))
        for side_y, y in ((SOUTH, 0), (NORTH, tiles_y - 1))
    ]


def send_corners_kernel(
    owner_ref, _, effect_ref, wind_ref, fw_ref, fe_ref, fs_ref, fn_ref, cw_ref, ce_ref, send_ref, sums, sems,
    *, tiles_x, tiles_y
):
    rows = cw_ref.shape[0] // 2
    each = 2 * rows + ROWS
    bins = rows // TZ
    mix = dust_step * diffusion
    _, lane = iotas()
    group, within = lane // TILE, lane % TILE
    on_x = (group == WEST) | (group == EAST)
    low_side = (group == WEST) | (group == SOUTH)
    first, last = within == 0, within == TILE - 1
    corner = corner_index(0)
    tiles = corner_tiles(tiles_x, tiles_y)

    def copy(n, t):
        return pltpu.make_async_copy(sums.at[n], send_ref.at[owner_ref[t]], sems.at[n])

    for n, (side_x, side_y, t) in enumerate(tiles):
        strip_x = fw_ref if side_x == WEST else fe_ref
        strip_y = fs_ref if side_y == SOUTH else fn_ref
        cells_ref, cell_lane = (cw_ref, LANES - 1) if side_x == WEST else (ce_ref, 0)
        cells_at = 0 if side_y == SOUTH else rows
        low_x, low_y = side_x == WEST, side_y == SOUTH
        end_x = 0 if low_y else strip_x.shape[0] - each
        end_y = 0 if low_x else strip_y.shape[0] - each
        to_x = side_x * TILE + (0 if low_y else TILE - 1)
        to_y = side_y * TILE + (0 if low_x else TILE - 1)

        def from_end(strip, at, c, level, low):
            def row(p):
                value = strip[at + 2 * rows + p : at + 2 * rows + p + 1, :]
                return lane_gather(spread_rows(value), jnp.full((ROWS, LANES), 0 if low else LANES - 1, jnp.int32))

            along = dust_step * row(c * TZ + level)
            return jnp.where(row(FLAG) > 0.0, mix + jnp.maximum(along if low else -along, 0.0), 0.0)

        for at in range(0, rows, ROWS):
            level = at // bins
            if at % bins == 0:
                u, v = (
                    dust_step * spread_rows(wind_ref[t, c * TZ + level : c * TZ + level + 1, :]) for c in range(2)
                )
                across, along = jnp.where(on_x, u, v), jnp.where(on_x, v, u)
                from_out = mix + jnp.maximum(jnp.where(low_side, across, -across), 0.0)
                from_corner = jnp.where(
                    first, mix + jnp.maximum(along, 0.0), jnp.where(last, mix + jnp.maximum(-along, 0.0), 0.0)
                )
                by_x = from_end(strip_x, end_x, 1, level, low_y)
                by_y = from_end(strip_y, end_y, 0, level, low_x)
            cells = lane_gather(
                cells_ref[cells_at + at : cells_at + at + ROWS, :], jnp.full((ROWS, LANES), cell_lane, jnp.int32)
            )
            more = jnp.where(lane == to_x, by_x * cells, jnp.where(lane == to_y, by_y * cells, 0.0))
            sums[n, at : at + ROWS, :] = (
                effect_ref[n, at : at + ROWS, :] + from_out * more + from_corner * lane_gather(more, corner)
            )
        sums[n, rows:, :] = effect_ref[n, rows:, :]

        @pl.when(owner_ref[t] >= 0)
        def _():
            copy(n, t).start()

    for n, (_, _, t) in enumerate(tiles):

        @pl.when(owner_ref[t] >= 0)
        def _():
            copy(n, t).wait()


def shifted(value, axis, steps):
    count = lax.axis_size(axis)
    return lax.ppermute(value, axis, [(source, (source + steps) % count) for source in range(count)])


def relay_rows(rows):
    return lax.all_to_all(rows, AXES, split_axis=0, concat_axis=0, tiled=True)


def exchange_borders(borders):
    east, west, north, south = borders
    return shifted(east, "gx", 1), shifted(west, "gx", -1), shifted(north, "gy", 1), shifted(south, "gy", -1)


def ring_call(kernel, tiles_x, tiles_y, rows, outs, scratch, name, hbm_in=0, hbm_out=0, aliases={}):
    smem = pl.BlockSpec(memory_space=pltpu.SMEM)
    vmem = pl.BlockSpec(memory_space=pltpu.VMEM)
    hbm = pl.BlockSpec(memory_space=pltpu.HBM)
    size = tiles_x * tiles_y * rows * LANES

    def call(owner_of_tile, *inputs):
        return pl.pallas_call(
            functools.partial(kernel, tiles_x=tiles_x, tiles_y=tiles_y),
            in_specs=[smem] + [hbm] * hbm_in + [vmem] * (len(inputs) - hbm_in),
            out_specs=[hbm] * hbm_out + [vmem] * (len(outs) - hbm_out),
            out_shape=outs,
            scratch_shapes=scratch,
            input_output_aliases=aliases,
            compiler_params=pltpu.CompilerParams(vmem_limit_bytes=32 << 20),
            cost_estimate=pl.CostEstimate(flops=16 * size, bytes_accessed=16 * size, transcendentals=0),
            name=name,
        )(owner_of_tile, *inputs)

    return call


def relay_strips(owner_of_tile, received, wind_send, wind_ring, settle_speed, bin_share, tiles_x, tiles_y):
    owners, both_rows, _ = received.shape
    rows = both_rows // 2
    per_home = tiles_x * tiles_y
    each = both_rows + ROWS
    ext = pltpu.VMEM(((tiles_x + 2) * (tiles_y + 2), rows, LANES), jnp.float32)
    all_rings = pltpu.VMEM((per_home, both_rows, LANES), jnp.float32)
    each_sem = pltpu.SemaphoreType.DMA((per_home,))
    settle_rows = jnp.broadcast_to(settle_speed[:, None], settle_speed.shape + (LANES,))
    share_rows = jnp.broadcast_to(bin_share[:, None], bin_share.shape + (LANES,))

    def call(kernel, outs, scratch, name, *inputs, **places):
        return ring_call(kernel, tiles_x, tiles_y, rows, outs, scratch, name, **places)(owner_of_tile, *inputs)

    along_x, along_y = tiles_y // 4, tiles_x // 4
    east, west, north, south = call(
        pack_borders_kernel,
        [f32(along_x * each, LANES)] * 2 + [f32(along_y * each, LANES)] * 2,
        [all_rings, each_sem],
        "pack_borders",
        in_hbm(received),
        wind_ring,
        hbm_in=1,
    )
    from_west, from_east, from_south, from_north = exchange_borders((east, west, north, south))
    wind_send, from_west, from_east, from_south, from_north = lax.optimization_barrier(
        (wind_send, from_west, from_east, from_south, from_north)
    )
    wind_recv = relay_rows(wind_send)
    top = (along_y - 1) * each
    across_low = jnp.concatenate([from_south[:rows], from_north[:rows]])
    across_high = jnp.concatenate([from_south[top : top + rows], from_north[top : top + rows]])
    corner_west, corner_east = shifted(across_high, "gx", 1), shifted(across_low, "gx", -1)
    (rings,) = call(gather_rings_kernel, [f32(per_home, both_rows, LANES)], [], "gather_rings", received)
    send_buffer = pltpu.HBM((owners, both_rows, LANES), jnp.float32)
    messages = (from_west, from_east, from_south, from_north)
    seen_send, corners = call(
        send_seen_kernel,
        [send_buffer, f32(4, both_rows, LANES)],
        [ext, all_rings]
        + [pltpu.VMEM((along_x, rows, LANES), jnp.float32)] * 2
        + [pltpu.VMEM((along_y, rows, LANES), jnp.float32)] * 2
        + [each_sem],
        "send_seen",
        rings, wind_ring, settle_rows, share_rows, east, west, north, south, *messages,
        hbm_out=1,
    )
    (seen_send,) = call(
        send_corners_kernel,
        [send_buffer],
        [pltpu.VMEM((4, both_rows, LANES), jnp.float32), pltpu.SemaphoreType.DMA((4,))],
        "send_corners",
        seen_send, corners, wind_ring, *messages, corner_west, corner_east,
        hbm_in=1,
        hbm_out=1,
        aliases={1: 0},
    )
    return wind_recv, relay_rows(seen_send)


def dust_kernel(home_ref, share_ref, settle_ref, dust_ref, shift_ref, wind_ref, out_ref, coef, *work, block, bins):
    lanes = len(work) // 2
    step = pl.program_id(0)
    _, lane = iotas()
    within = lane % TILE
    low_lanes, high_lanes = lane < TILE, lane >= LANES - TILE
    mix = dust_step * diffusion
    chunks = bins // ROWS
    settle = [dust_step * settle_ref[h * ROWS : (h + 1) * ROWS, :] for h in range(chunks)]
    share = [share_ref[h * ROWS : (h + 1) * ROWS, :] for h in range(chunks)]
    nothing = jnp.zeros((ROWS, LANES), jnp.float32)

    def prepare(k, j):
        held = work[2 * k]
        home = home_ref[step * block + j]
        plane = [wind_ref[home, p * ROWS : (p + 1) * ROWS, :] * dust_step for p in range(PLANES)]
        for level in range(TZ):
            u, v = plane[level], plane[TZ + level]
            coef[k, 0, level] = mix + jnp.maximum(u, 0.0)
            coef[k, 1, level] = mix + jnp.maximum(-u, 0.0)
            coef[k, 2, level] = jnp.where(within == 0, 0.0, mix + jnp.maximum(v, 0.0))
            coef[k, 3, level] = jnp.where(within == TILE - 1, 0.0, mix + jnp.maximum(-v, 0.0))
            coef[k, 4, level] = 1.0 - 6.0 * mix - jnp.abs(u) - jnp.abs(v)
            coef[k, 5, level] = plane[2 * TZ + level]
        coef[k, 6, 0] = plane[PLANES - 1]
        for r in range(ROWS):
            for level in range(TZ):
                at = (r * TZ + level) * bins
                held[at : at + bins, :] = dust_ref[j, pl.ds(r * TZ + level, bins, stride=ROWS * TZ), :]

    def shift(k):
        held, shifts = work[2 * k], work[2 * k + 1]
        shifts[...] = jnp.dot(
            jnp.concatenate(halves_of(held[...]), axis=1), shift_ref[...], preferred_element_type=jnp.float32
        )

    def update(k, j, substep):
        held, shifts = work[2 * k], work[2 * k + 1]
        for r in range(ROWS):
            for h in range(chunks):
                cells = [held[(r * TZ + level) * bins + h * ROWS :][:ROWS] for level in range(TZ)]
                for level in range(TZ):
                    at = (r * TZ + level) * bins + h * ROWS

                    def moved(which, rows_up=0):
                        first = at + rows_up * TZ * bins
                        return shifts[first : first + ROWS, which * LANES : (which + 1) * LANES]

                    def by(which):
                        return spread_rows(coef[k, which, level, r : r + 1, :])

                    before = nothing if r == 0 else moved(2, -1)
                    after = nothing if r == ROWS - 1 else moved(3, 1)
                    west = jnp.where(low_lanes, before, moved(2))
                    east = jnp.where(high_lanes, after, moved(3))
                    rise = by(5) - settle[h]
                    up = jnp.maximum(rise, 0.0)
                    mixed = mix + (up - rise if level == 0 else up)
                    value = (
                        (by(4) - jnp.abs(rise)) * cells[level]
                        + by(0) * west
                        + by(1) * east
                        + by(2) * moved(0)
                        + by(3) * moved(1)
                        + mixed * cells[1 - level]
                    )
                    if level == 0:
                        value = value + spread_rows(coef[k, 6, 0, r : r + 1, :]) * share[h]
                    if substep == 0:
                        held[at : at + ROWS, :] = value
                    else:
                        first = h * ROWS * ROWS * TZ + r * TZ + level
                        out_ref[j, pl.ds(first, ROWS, stride=ROWS * TZ), :] = value

    def some(i, carry):
        for k in range(lanes):
            prepare(k, i * lanes + k)
        for substep in range(2):
            for k in range(lanes):
                shift(k)
            for k in range(lanes):
                update(k, i * lanes + k, substep)
        return carry

    lax.fori_loop(0, block // lanes, some, 0)


def dust_inner(home_of_slot, dust, wind_recv, settle_speed, bin_share):
    slots, cells = dust.shape[:2]
    bins = settle_speed.shape[0]
    block = 8 if slots % 8 == 0 else 4
    lanes = 2
    smem = pl.BlockSpec(memory_space=pltpu.SMEM)
    vmem = pl.BlockSpec(memory_space=pltpu.VMEM)
    tile = pl.BlockSpec((block, cells, LANES), lambda i: (i, 0, 0))
    settle = jnp.broadcast_to(settle_speed[:, None], (bins, LANES))
    share = jnp.broadcast_to(bin_share[:, None], (bins, LANES))
    return pl.pallas_call(
        functools.partial(dust_kernel, block=block, bins=bins),
        grid=(slots // block,),
        in_specs=[smem, vmem, vmem, tile, vmem, vmem],
        out_specs=tile,
        out_shape=pltpu.HBM(dust.shape, jnp.float32),
        scratch_shapes=[pltpu.VMEM((lanes, PLANES, TZ, ROWS, LANES), jnp.float32)]
        + [pltpu.VMEM((cells, LANES), jnp.float32), pltpu.VMEM((cells, 4 * LANES), jnp.float32)] * lanes,
        compiler_params=pltpu.CompilerParams(vmem_limit_bytes=24 << 20),
        cost_estimate=pl.CostEstimate(flops=120 * dust.size, bytes_accessed=dust.size * 12, transcendentals=0),
        name="dust_inner",
    )(home_of_slot, share, settle, in_hbm(dust), jnp.asarray(shift_matrix()), wind_recv)


def dust_outer_kernel(
    home_ref, inner_hbm, matrix_ref, effect_hbm, out_hbm, effect, dust, added, effect_sems, load_sems, sems, *, block, bins
):
    slots = dust.shape[0]
    rows = TZ * bins

    def arrive(s):
        return pltpu.make_async_copy(effect_hbm.at[home_ref[s]], effect.at[s], effect_sems.at[s])

    def load(i):
        some = pl.ds(i * block, block)
        return pltpu.make_async_copy(inner_hbm.at[some], dust.at[some], load_sems.at[i])

    def store(i):
        some = pl.ds(i * block, block)
        return pltpu.make_async_copy(dust.at[some], out_hbm.at[some], sems.at[i])

    def start(i, carry):
        for j in range(block):
            arrive(i * block + j).start()
        load(i).start()
        return carry

    count = slots // block
    lax.fori_loop(0, count, start, 0)

    def wait_for(i):
        for j in range(block):
            arrive(i * block + j).wait()

    def expand(i):
        rings = jnp.concatenate(
            [
                jnp.concatenate([effect[i * block + j, depth * rows : (depth + 1) * rows, :] for depth in range(2)], axis=1)
                for j in range(block)
            ],
            axis=0,
        )
        return jnp.dot(
            jnp.concatenate(halves_of(rings), axis=1), matrix_ref[...], preferred_element_type=jnp.float32
        )

    wait_for(0)
    added[0] = expand(0)

    def one(i, carry):
        later = jnp.minimum(i + 1, count - 1)

        @pl.when(i + 1 < count)
        def _():
            wait_for(later)

        load(i).wait()
        now = lax.rem(i, 2)
        added[1 - now] = expand(later)
        for j in range(block):
            for r in range(ROWS):
                for level in range(TZ):
                    at = pl.ds(r * TZ + level, bins, stride=ROWS * TZ)
                    first = j * rows + level * bins
                    dust[i * block + j, at, :] += added[now, first : first + bins, r * LANES : (r + 1) * LANES]
        store(i).start()
        return carry

    lax.fori_loop(0, count, one, 0)
    for i in range(count):
        store(i).wait()


def dust_outer(home_of_slot, inner, effect, bins):
    slots = inner.shape[0]
    block = 8 if slots % 8 == 0 else 4
    hbm = pl.BlockSpec(memory_space=pltpu.HBM)
    vmem = pl.BlockSpec(memory_space=pltpu.VMEM)
    return pl.pallas_call(
        functools.partial(dust_outer_kernel, block=block, bins=bins),
        in_specs=[pl.BlockSpec(memory_space=pltpu.SMEM), hbm, vmem, hbm],
        out_specs=hbm,
        out_shape=pltpu.HBM(inner.shape, jnp.float32),
        scratch_shapes=[
            pltpu.VMEM((slots,) + effect.shape[1:], jnp.float32),
            pltpu.VMEM(inner.shape, jnp.float32),
            pltpu.VMEM((2, block * bins * TZ, TILE * TILE), jnp.float32),
            pltpu.SemaphoreType.DMA((slots,)),
            pltpu.SemaphoreType.DMA((slots // block,)),
            pltpu.SemaphoreType.DMA((slots // block,)),
        ],
        compiler_params=pltpu.CompilerParams(vmem_limit_bytes=24 << 20),
        cost_estimate=pl.CostEstimate(flops=2 * inner.size, bytes_accessed=inner.size * 8, transcendentals=0),
        name="dust_outer",
    )(home_of_slot, in_hbm(inner), jnp.asarray(spread_matrix()), in_hbm(effect))


def per_device(velocity, threshold, dust_mass, settle_speed, bin_share, active_tiles, tile_owner):
    owners = lax.axis_size(AXES)
    grid_cols = lax.axis_size("gy")
    self_index = lax.axis_index(AXES)
    slots, bins = dust_mass.shape[:2]
    tiles_x = velocity.shape[2] // TILE
    tiles_y = velocity.shape[3] // TILE
    per_home = tiles_x * tiles_y
    tiles_across = tiles_y * grid_cols

    tile_x = active_tiles // tiles_across
    tile_y = active_tiles % tiles_across
    home_dev = tile_x // tiles_x * grid_cols + tile_y // tiles_y
    local_tile = tile_x % tiles_x * tiles_y + tile_y % tiles_y
    own_slot = tile_owner - self_index * slots
    mine = jnp.where(home_dev == self_index, local_tile, -1)
    slot_ids = jnp.arange(slots, dtype=jnp.int32)
    home_of_slot = jnp.sum(jnp.where(own_slot[None, :] == slot_ids[:, None], home_dev[None, :], 0), axis=1)
    tile_ids = jnp.arange(per_home, dtype=jnp.int32)
    owner_of_tile = jnp.max(
        jnp.where(mine[None, :] == tile_ids[:, None], (tile_owner // slots)[None, :], -1), axis=1
    )

    dust = dust_mass.reshape(slots, bins, TZ, ROWS, LANES).transpose(0, 1, 3, 2, 4)
    dust = dust.reshape(slots, bins * ROWS * TZ, LANES)

    xlo, xhi, ylo, yhi = exchange_borders(wind_faces(velocity))

    strips_send = dust_strips(home_of_slot, dust, bins, owners)
    strips_send, xlo, xhi, ylo, yhi = lax.optimization_barrier((strips_send, xlo, xhi, ylo, yhi))
    strips = relay_rows(strips_send)
    new_velocity, wind_send, wind_ring = wind_step(
        owner_of_tile, velocity, xlo, xhi, ylo, yhi, threshold, owners
    )
    strips, wind_send, wind_ring = lax.optimization_barrier((strips, wind_send, wind_ring))
    wind_recv, effect = relay_strips(
        owner_of_tile, strips, wind_send, wind_ring, settle_speed, bin_share, tiles_x, tiles_y
    )
    inner = dust_inner(home_of_slot, dust, wind_recv, settle_speed, bin_share)
    out = dust_outer(home_of_slot, inner, effect, bins)
    out = out.reshape(slots, bins, ROWS, TZ, LANES).transpose(0, 1, 3, 2, 4).reshape(dust_mass.shape)
    return new_velocity, out


def solution(mesh):
    in_specs = (
        P(None, None, "gx", "gy"),
        P("gx", "gy"),
        P(AXES, None, None, None),
        P(),
        P(),
        P(),
        P(),
    )
    out_specs = (P(None, None, "gx", "gy"), P(AXES, None, None, None))
    return jax.shard_map(
        per_device, mesh=mesh, in_specs=in_specs, out_specs=out_specs, check_vma=False
    )
```

```python
import functools

import jax
import jax.numpy as jnp
import ml_dtypes
import numpy as np
from jax import lax
from jax.experimental import pallas as pl
from jax.experimental.pallas import tpu as pltpu
from jax.sharding import PartitionSpec as P

TZ = 2
TILE = 32
LANES = 128
ROWS = TILE * TILE // LANES
PLANES = 7
AXES = ("gx", "gy")

time_step = 0.1
viscosity = 0.2
dust_step = 0.1
diffusion = 0.1
roughness = 0.5
emit_rate = 0.5

WEST, SOUTH, NORTH, EAST = range(4)


def iotas(shape=(ROWS, LANES)):
    return lax.broadcasted_iota(jnp.int32, shape, 0), lax.broadcasted_iota(jnp.int32, shape, 1)


def lane_gather(x, index):
    return jnp.take_along_axis(x, index, axis=1)


def ring_pattern(depth):
    row, lane = iotas()
    group, within = lane // TILE, lane % TILE
    side = jnp.where(group == SOUTH, depth, TILE - 1 - depth)
    index = (within % 4) * TILE + side
    index = jnp.where(group == WEST, depth * TILE + within, index)
    index = jnp.where(group == EAST, (3 - depth) * TILE + within, index)
    source = jnp.where(group == WEST, 0, jnp.where(group == EAST, ROWS - 1, within // 4))
    return index, row == source


def ring_of(x, pattern):
    index, taken = pattern
    return jnp.sum(jnp.where(taken, lane_gather(x, index), 0.0), axis=0, keepdims=True)


def spread_rows(row):
    return jnp.broadcast_to(row, (ROWS, LANES))


def f32(*shape):
    return jax.ShapeDtypeStruct(shape, jnp.float32)


def in_hbm(x):
    return pltpu.with_memory_space_constraint(x, pltpu.HBM)


def halves_of(x):
    high = x.astype(jnp.bfloat16)
    return high, (x - high.astype(jnp.float32)).astype(jnp.bfloat16)


def moves(sources, width=LANES):
    lanes = np.arange(width)[:, None]
    once = (lanes == np.asarray(sources)[None, :]).astype(ml_dtypes.bfloat16)
    return np.concatenate([once, once], axis=0)


def ring_matrix():
    lane = np.arange(LANES)
    group, within = lane // TILE, lane % TILE
    on_y = (group == SOUTH) | (group == NORTH)
    blocks = []
    for p in range(ROWS // 2):
        columns = []
        for depth in range(2):
            cell = (within % 4) * TILE + np.where(group == SOUTH, depth, TILE - 1 - depth)
            source = np.where(within // 4 == p, cell, -1)
            source = np.where(within // 4 == p + ROWS // 2, (cell + 4) % LANES, source)
            columns.append(np.where(on_y, source, -1))
        blocks.append(moves(np.concatenate(columns)))
    columns = [
        np.where(group == WEST, depth * TILE + within, np.where(group == EAST, (3 - depth) * TILE + within, -1))
        for depth in range(2)
    ]
    blocks.append(moves(np.concatenate(columns)))
    return np.concatenate(blocks, axis=0)


def ring_parts(rows):
    lane = lax.broadcasted_iota(jnp.int32, rows[0].shape, 1)
    within = lane % TILE
    kept = (within < 2) | (within >= TILE - 2)
    half = len(rows) // 2
    parts = [jnp.where(kept, rows[p], pltpu.roll(rows[p + half], 4, 1)) for p in range(half)]
    return parts + [jnp.where(lane < LANES // 2, rows[0], rows[-1])]


def shift_matrix():
    lane = np.arange(LANES)
    return moves(np.concatenate([(lane + d) % LANES for d in (-1, 1, -TILE, TILE)]))


def spread_matrix():
    i, j = np.divmod(np.arange(TILE * TILE), TILE)
    source = np.full(TILE * TILE, -1)
    for depth in (1, 0):
        at = depth * LANES
        source = np.where(j == depth, at + SOUTH * TILE + i, source)
        source = np.where(j == TILE - 1 - depth, at + NORTH * TILE + i, source)
        source = np.where(i == depth, at + WEST * TILE + j, source)
        source = np.where(i == TILE - 1 - depth, at + EAST * TILE + j, source)
    return moves(source, 2 * LANES)


def strips_kernel(home_ref, dust_hbm, matrix_ref, send_ref, dust, rings, load_sems, sems, *, block, bins):
    slots = rings.shape[0]
    each = TZ * bins

    def load(i):
        some = pl.ds(i * block, block)
        return pltpu.make_async_copy(dust_hbm.at[some], dust.at[some], load_sems.at[i])

    def send(s):
        return pltpu.make_async_copy(rings.at[s], send_ref.at[home_ref[s]], sems.at[s])

    for i in range(slots // block):
        load(i).start()

    def one(i, carry):
        load(i).wait()
        cells = [
            jnp.concatenate(
                [
                    dust[i * block + j, pl.ds(r * TZ + level, bins, stride=ROWS * TZ), :]
                    for j in range(block)
                    for level in range(TZ)
                ],
                axis=0,
            )
            for r in range(ROWS)
        ]
        parts = [half for x in ring_parts(cells) for half in halves_of(x)]
        found = jnp.dot(
            jnp.concatenate(parts, axis=1), matrix_ref[...], preferred_element_type=jnp.float32
        )
        for j in range(block):
            for depth in range(2):
                rings[i * block + j, depth * each : (depth + 1) * each, :] = found[
                    j * each : (j + 1) * each, depth * LANES : (depth + 1) * LANES
                ]
            send(i * block + j).start()
        return carry

    lax.fori_loop(0, slots // block, one, 0)

    def wait(s, carry):
        send(s).wait()
        return carry

    lax.fori_loop(0, slots, wait, 0)


def dust_strips(home_of_slot, dust, bins, owners):
    slots = dust.shape[0]
    block = 14 if slots % 14 == 0 else 4
    rows = 2 * bins * TZ
    matrix = jnp.asarray(ring_matrix())
    hbm = pl.BlockSpec(memory_space=pltpu.HBM)
    return pl.pallas_call(
        functools.partial(strips_kernel, block=block, bins=bins),
        in_specs=[pl.BlockSpec(memory_space=pltpu.SMEM), hbm, pl.BlockSpec(memory_space=pltpu.VMEM)],
        out_specs=hbm,
        out_shape=pltpu.HBM((owners, rows, LANES), jnp.float32),
        scratch_shapes=[
            pltpu.VMEM(dust.shape, jnp.float32),
            pltpu.VMEM((slots, rows, LANES), jnp.float32),
            pltpu.SemaphoreType.DMA((slots // block,)),
            pltpu.SemaphoreType.DMA((slots,)),
        ],
        compiler_params=pltpu.CompilerParams(vmem_limit_bytes=32 << 20),
        cost_estimate=pl.CostEstimate(
            flops=20 * dust.size, bytes_accessed=dust.size * 4 + slots * rows * LANES * 4, transcendentals=0
        ),
        name="dust_strips",
    )(home_of_slot, in_hbm(dust), matrix)


def faces_kernel(vel_ref, x_last_ref, x_first_ref, y_last_ref, y_first_ref, wind, sems):
    fields, nx, ny = vel_ref.shape
    copies = [pltpu.make_async_copy(vel_ref.at[f], wind.at[f], sems.at[f]) for f in range(fields)]
    for copy in copies:
        copy.start()
    lane = lax.broadcasted_iota(jnp.int32, (nx, LANES), 1)
    for f, copy in enumerate(copies):
        copy.wait()
        x_first_ref[f : f + 1, :] = wind[f, 0:1, :]
        x_last_ref[f : f + 1, :] = wind[f, nx - 1 : nx, :]
        both = pltpu.roll(jnp.where(lane < LANES // 2, wind[f, :, :LANES], wind[f, :, ny - LANES :]), f + 1, 1)
        if f == 0:
            y_first_ref[...], y_last_ref[...] = both, both
        else:
            y_first_ref[...] = jnp.where(lane == f + 1, both, y_first_ref[...])
            y_last_ref[...] = jnp.where(lane == f, both, y_last_ref[...])


def wind_faces(velocity):
    comps, levels, nx, ny = velocity.shape
    fields = comps * levels
    vmem = pl.BlockSpec(memory_space=pltpu.VMEM)
    return pl.pallas_call(
        faces_kernel,
        in_specs=[pl.BlockSpec(memory_space=pltpu.HBM)],
        out_specs=[vmem] * 4,
        out_shape=[f32(fields, ny)] * 2 + [f32(nx, LANES)] * 2,
        scratch_shapes=[pltpu.VMEM((fields, nx, ny), jnp.float32), pltpu.SemaphoreType.DMA((fields,))],
        compiler_params=pltpu.CompilerParams(vmem_limit_bytes=32 << 20),
        cost_estimate=pl.CostEstimate(flops=velocity.size, bytes_accessed=velocity.size * 4, transcendentals=0),
        name="wind_faces",
    )(in_hbm(velocity.reshape(fields, nx, ny)))


def wind_kernel(
    owner_ref, vel_ref, xlo_ref, xhi_ref, ylo_ref, yhi_ref, thr_ref,
    new_ref, send_ref, ring_ref, padded, strip, tiles, load_sem, sems, *, levels
):
    fields, nx, ny = new_ref.shape
    load = pltpu.make_async_copy(vel_ref, padded.at[:, pl.ds(8, nx), :], load_sem)
    load.start()
    load.wait()
    for f in range(fields):
        padded[f, 7:8, :] = xlo_ref[f : f + 1, :]
        padded[f, 8 + nx : 9 + nx, :] = xhi_ref[f : f + 1, :]
    half = 16
    halves = ny // LANES
    tiles_y = ny // TILE
    patterns = [ring_pattern(0), ring_pattern(1)]
    _, lane8 = iotas()
    group = lane8 // TILE

    def one_strip(ix, carry):
        for sub in range(TILE // half):
            base = pl.multiple_of(ix * TILE + sub * half, 8)
            lane = lax.broadcasted_iota(jnp.int32, (half, ny), 1)
            low = {}
            faces = [ref[pl.ds(base, half), :] for ref in (ylo_ref, yhi_ref)]

            def face(which, f, to):
                moved = pltpu.roll(faces[which], (to - f - which) % LANES, 1) if f + which != to else faces[which]
                return jnp.concatenate([moved] * halves, axis=1)

            for z in range(levels):
                u, v, w = (padded[c * levels + z, pl.ds(base + 8, half), :] for c in range(3))
                for c in range(3):
                    f = c * levels + z
                    block = padded[f, pl.ds(base, half + 16), :]
                    centre = (u, v, w)[c]
                    west = pltpu.roll(block, 1, 0)[8 : 8 + half]
                    east = pltpu.roll(block, half + 15, 0)[8 : 8 + half]
                    south = jnp.where(lane == 0, face(0, f, 0), pltpu.roll(centre, 1, 1))
                    north = jnp.where(lane == ny - 1, face(1, f, LANES - 1), pltpu.roll(centre, ny - 1, 1))
                    lower = -centre if z == 0 else padded[f - 1, pl.ds(base + 8, half), :]
                    upper = centre if z == levels - 1 else padded[f + 1, pl.ds(base + 8, half), :]
                    carried = 0.5 * (u * (east - west) + v * (north - south) + w * (upper - lower))
                    spread = east + west + north + south + upper + lower - 6.0 * centre
                    new = centre + time_step * (viscosity * spread - carried)
                    new_ref[f, pl.ds(base, half), :] = new
                    if z < TZ:
                        low[c * TZ + z] = new
            stress = roughness * (low[0] * low[0] + low[TZ] * low[TZ])
            low[PLANES - 1] = emit_rate * stress * jnp.maximum(
                stress - thr_ref[pl.ds(base, half), :], 0.0
            )
            for p in range(PLANES):
                for h in range(halves):
                    strip[p * halves + h, sub * half : (sub + 1) * half, :] = low[p][
                        :, h * LANES : (h + 1) * LANES
                    ]
        for p in range(PLANES):
            for h in range(halves):
                parts = [strip[p * halves + h, pl.ds(k, ROWS, stride=4), :] for k in range(4)]
                for t in range(4):
                    tile = ix * tiles_y + h * 4 + t
                    cells = pltpu.roll(parts[0], (-t * TILE) % LANES, 1) if t else parts[0]
                    for k in range(1, 4):
                        moved = pltpu.roll(parts[k], ((k - t) * TILE) % LANES, 1) if k != t else parts[k]
                        cells = jnp.where(group == k, moved, cells)
                    tiles[tile, p * ROWS : (p + 1) * ROWS, :] = cells
                    for depth in range(2):
                        ring_ref[tile, depth * 8 + p : depth * 8 + p + 1, :] = ring_of(cells, patterns[depth])

        def send(t, inner):
            tile = ix * tiles_y + t
            owner = owner_ref[tile]

            @pl.when(owner >= 0)
            def _():
                pltpu.make_async_copy(tiles.at[tile], send_ref.at[owner], sems.at[tile]).start()

            return inner

        lax.fori_loop(0, tiles_y, send, 0)
        return carry

    lax.fori_loop(0, nx // TILE, one_strip, 0)

    def wait(tile, carry):
        owner = owner_ref[tile]

        @pl.when(owner >= 0)
        def _():
            pltpu.make_async_copy(tiles.at[tile], send_ref.at[owner], sems.at[tile]).wait()

        return carry

    lax.fori_loop(0, tiles.shape[0], wait, 0)


def wind_step(owner_of_tile, velocity, xlo, xhi, ylo, yhi, threshold, owners):
    comps, levels, nx, ny = velocity.shape
    fields = comps * levels
    per_home = (nx // TILE) * (ny // TILE)
    smem = pl.BlockSpec(memory_space=pltpu.SMEM)
    hbm = pl.BlockSpec(memory_space=pltpu.HBM)
    vmem = pl.BlockSpec(memory_space=pltpu.VMEM)
    new, send, ring = pl.pallas_call(
        functools.partial(wind_kernel, levels=levels),
        in_specs=[smem, hbm, vmem, vmem, vmem, vmem, vmem],
        out_specs=[vmem, hbm, vmem],
        out_shape=[
            f32(fields, nx, ny),
            pltpu.HBM((owners, PLANES * ROWS, LANES), jnp.float32),
            f32(per_home, 16, LANES),
        ],
        scratch_shapes=[
            pltpu.VMEM((fields, nx + 16, ny), jnp.float32),
            pltpu.VMEM((PLANES * (ny // LANES), TILE, LANES), jnp.float32),
            pltpu.VMEM((per_home, PLANES * ROWS, LANES), jnp.float32),
            pltpu.SemaphoreType.DMA,
            pltpu.SemaphoreType.DMA((per_home,)),
        ],
        compiler_params=pltpu.CompilerParams(vmem_limit_bytes=40 << 20),
        cost_estimate=pl.CostEstimate(
            flops=40 * velocity.size, bytes_accessed=velocity.size * 10, transcendentals=0
        ),
        name="wind_step",
    )(
        owner_of_tile,
        in_hbm(velocity.reshape(fields, nx, ny)),
        xlo,
        xhi,
        ylo,
        yhi,
        threshold,
    )
    return new.reshape(velocity.shape), send, ring


def border_tiles(tiles_x, tiles_y):
    return (
        (EAST, [(tiles_x - 1) * tiles_y + n for n in range(tiles_y)]),
        (WEST, [n for n in range(tiles_y)]),
        (NORTH, [n * tiles_y + tiles_y - 1 for n in range(tiles_x)]),
        (SOUTH, [n * tiles_y for n in range(tiles_x)]),
    )


def fill_halo(ext, strips, tiles_x, tiles_y):
    wide = tiles_y + 2
    for strip_of, side, places in (
        (strips[0], EAST, [n + 1 for n in range(tiles_y)]),
        (strips[1], WEST, [(tiles_x + 1) * wide + n + 1 for n in range(tiles_y)]),
        (strips[2], NORTH, [(n + 1) * wide for n in range(tiles_x)]),
        (strips[3], SOUTH, [(n + 1) * wide + tiles_y + 1 for n in range(tiles_x)]),
    ):
        for n, place in enumerate(places):
            strip = strip_of(n // 4)
            if n % 4 != side:
                strip = pltpu.roll(strip, ((side - n % 4) * TILE) % LANES, 1)
            ext[place] = strip


def seen_by(ext, place, wide):
    west, east = ext[place - wide], ext[place + wide]
    south, north = ext[place - 1], ext[place + 1]
    lane = lax.broadcasted_iota(jnp.int32, west.shape, 1)
    up = pltpu.roll(jnp.where(lane < 2 * TILE, north, west), TILE, 1)
    down = pltpu.roll(jnp.where(lane < 2 * TILE, east, south), LANES - TILE, 1)
    return jnp.where((lane // TILE) % 2 == 0, up, down)


FLAG = 7


def pack_borders_kernel(owner_ref, recv_ref, wind_ref, *refs, tiles_x, tiles_y):
    *outs, rings, sems = refs
    both_rows = rings.shape[1]
    borders = border_tiles(tiles_x, tiles_y)
    used = list(dict.fromkeys(t for _, tiles in borders for t in tiles))

    def copy(t):
        return pltpu.make_async_copy(recv_ref.at[jnp.maximum(owner_ref[t], 0)], rings.at[t], sems.at[t])

    for t in used:
        copy(t).start()
    for t in used:
        copy(t).wait()

    lane = lax.broadcasted_iota(jnp.int32, (both_rows, LANES), 1) // TILE
    row8, lane8 = iotas()
    group8 = lane8 // TILE
    for out, (side, tiles) in zip(outs, borders):
        for g in range(len(tiles) // 4):
            strips = winds = None
            for q in range(4):
                t = tiles[4 * g + q]
                active = owner_ref[t] >= 0
                strip, wind = jnp.where(active, rings[t], 0.0), wind_ref[t, :ROWS, :]
                if q != side:
                    strip = pltpu.roll(strip, ((q - side) * TILE) % LANES, 1)
                    wind = pltpu.roll(wind, ((q - side) * TILE) % LANES, 1)
                wind = jnp.where(row8 == FLAG, jnp.where(active, 1.0, 0.0), wind)
                strips = strip if strips is None else jnp.where(lane == q, strip, strips)
                winds = wind if winds is None else jnp.where(group8 == q, wind, winds)
            at = g * (both_rows + ROWS)
            out[at : at + both_rows, :] = strips
            out[at + both_rows : at + both_rows + ROWS, :] = winds


def gather_rings_kernel(owner_ref, recv_ref, rings_ref, *, tiles_x, tiles_y):
    def one(t, carry):
        owner = owner_ref[t]
        rings = recv_ref[jnp.maximum(owner, 0)]
        rings_ref[t] = jnp.where(owner >= 0, rings, 0.0)
        return carry

    lax.fori_loop(0, tiles_x * tiles_y, one, 0)


def fill_tiles(ext, tile, tiles_x, tiles_y):
    def inner(t, carry):
        ext[place_of(t, tiles_y)] = tile(t)
        return carry

    lax.fori_loop(0, tiles_x * tiles_y, inner, 0)


def place_of(t, tiles_y):
    return (t // tiles_y + 1) * (tiles_y + 2) + t % tiles_y + 1


def corner_index(inset):
    _, lane = iotas()
    group, within = lane // TILE, lane % TILE
    on_x = (group == WEST) | (group == EAST)
    low = within < TILE // 2
    along = jnp.where((group == EAST) | (group == NORTH), TILE - 1 - inset, inset)
    return jnp.where(on_x, jnp.where(low, SOUTH, NORTH), jnp.where(low, WEST, EAST)) * TILE + along


def ring_effect(t, wind_ref, settle_ref, seen, seen_later):
    row, lane = iotas()
    group, within = lane // TILE, lane % TILE
    on_x = (group == WEST) | (group == EAST)
    low_side = (group == WEST) | (group == SOUTH)
    first, last = within == 0, within == TILE - 1
    second, last_but_one = within == 1, within == TILE - 2
    corner, inner = corner_index(0), corner_index(1)
    rows = seen.shape[0]
    bins = rows // TZ
    mix = dust_step * diffusion

    def wind(depth, p):
        return dust_step * spread_rows(wind_ref[t, depth * 8 + p : depth * 8 + p + 1, :])

    inflow, later_in = [], []
    coefs = []
    for level in range(TZ):
        u, v, w = (wind(0, c * TZ + level) for c in range(3))
        across, along = jnp.where(on_x, u, v), jnp.where(on_x, v, u)
        outward = jnp.where(low_side, across, -across)
        from_out = mix + jnp.maximum(outward, 0.0)
        from_in = jnp.where(first | last, mix + jnp.maximum(-outward, 0.0), 0.0)
        from_before, from_after = mix + jnp.maximum(along, 0.0), mix + jnp.maximum(-along, 0.0)
        from_corner = jnp.where(first, from_before, jnp.where(last, from_after, 0.0))
        from_before = jnp.where(first, 0.0, from_before)
        from_after = jnp.where(last, 0.0, from_after)
        keep = 1.0 - 6.0 * mix - jnp.abs(u) - jnp.abs(v)
        u2, v2 = (wind(1, c * TZ + level) for c in range(2))
        across2, along2 = jnp.where(on_x, u2, v2), jnp.where(on_x, v2, u2)
        deep_out = mix + jnp.maximum(jnp.where(low_side, across2, -across2), 0.0)
        deep_corner = jnp.where(
            second, mix + jnp.maximum(along2, 0.0), jnp.where(last_but_one, mix + jnp.maximum(-along2, 0.0), 0.0)
        )
        coefs.append((w, keep, from_in, from_before, from_after, deep_out, deep_corner))
        for at in range(level * bins, (level + 1) * bins, ROWS):
            for view, taken in ((seen, inflow), (seen_later, later_in)):
                g = view[at : at + ROWS, :]
                taken.append(from_out * g + from_corner * lane_gather(g, corner))
    outer, deep = [], []
    for n, e in enumerate(inflow):
        level, bin_at = n * ROWS // bins, n * ROWS % bins
        w, keep, from_in, from_before, from_after, deep_out, deep_corner = coefs[level]
        other = inflow[n + len(inflow) // 2 if level == 0 else n - len(inflow) // 2]
        rise = w - dust_step * settle_ref[bin_at : bin_at + ROWS, :]
        up = jnp.maximum(rise, 0.0)
        down = up - rise
        turned = lane_gather(e, inner)
        outer.append(
            (keep - up - down) * e
            + from_before * pltpu.roll(e, 1, 1)
            + from_after * pltpu.roll(e, LANES - 1, 1)
            + from_in * turned
            + (mix + (down if level == 0 else up)) * other
            + later_in[n]
        )
        deep.append(deep_out * e + deep_corner * turned)
    return outer, deep


def advance_ring(t, owner_ref, rings_ref, wind_ref, settle_ref, share_ref, seen):
    _, lane = iotas()
    group, within = lane // TILE, lane % TILE
    on_x = (group == WEST) | (group == EAST)
    first, last = within == 0, within == TILE - 1
    corner = corner_index(0)
    rows = rings_ref.shape[1] // 2
    bins = rows // TZ
    uplift = dust_step * spread_rows(wind_ref[t, PLANES - 1 : PLANES, :])
    mix = dust_step * diffusion
    active = owner_ref[t] >= 0
    chunks = []
    for at in range(0, rows, ROWS):
        level, bin_at = at // bins, at % bins
        if bin_at == 0:
            u, v, w = (
                dust_step * spread_rows(wind_ref[t, c * TZ + level : c * TZ + level + 1, :]) for c in range(3)
            )
            from_west = mix + jnp.maximum(u, 0.0)
            from_east = mix + jnp.maximum(-u, 0.0)
            from_south = mix + jnp.maximum(v, 0.0)
            from_north = mix + jnp.maximum(-v, 0.0)
            keep = 1.0 - 6.0 * mix - jnp.abs(u) - jnp.abs(v)
        q = rings_ref[t, at : at + ROWS, :]
        deep = rings_ref[t, rows + at : rows + at + ROWS, :]
        out = seen[at : at + ROWS, :]
        beyond = lane_gather(out, corner)
        before = jnp.where(first, beyond, pltpu.roll(q, 1, 1))
        after = jnp.where(last, beyond, pltpu.roll(q, LANES - 1, 1))
        west = jnp.where(group == WEST, out, jnp.where(group == EAST, deep, before))
        east = jnp.where(group == WEST, deep, jnp.where(group == EAST, out, after))
        south = jnp.where(on_x, before, jnp.where(group == SOUTH, out, deep))
        north = jnp.where(on_x, after, jnp.where(group == SOUTH, deep, out))
        other_at = (1 - level) * bins + bin_at
        other = rings_ref[t, other_at : other_at + ROWS, :]
        rise = w - dust_step * settle_ref[bin_at : bin_at + ROWS, :]
        up = jnp.maximum(rise, 0.0)
        down = up - rise
        new = (
            (keep - up - down) * q
            + from_west * west
            + from_east * east
            + from_south * south
            + from_north * north
            + (mix + (down if level == 0 else up)) * other
        )
        if level == 0:
            new = new + uplift * share_ref[bin_at : bin_at + ROWS, :]
        chunks.append(jnp.where(active, new, 0.0))
    return chunks


def advance_strip(side, message, ours, settle_ref, share_ref, out, rows):
    _, lane = iotas()
    bins = rows // TZ
    each = 2 * rows + ROWS
    groups = out.shape[0]
    mix = dust_step * diffusion
    for g in range(groups):
        wind_at = g * each + 2 * rows

        def wind_row(p):
            return spread_rows(message[wind_at + p : wind_at + p + 1, :])

        for at in range(0, rows, ROWS):
            level, bin_at = at // bins, at % bins
            u, v, w = (dust_step * wind_row(c * TZ + level) for c in range(3))

            def cells(group, first):
                return message[group * each + first : group * each + first + ROWS, :]

            q = cells(g, at)
            deep = cells(g, rows + at)
            near = ours[g * each + at : g * each + at + ROWS, :]
            low = 0.0 if g == 0 else pltpu.roll(cells(g - 1, at), 1, 1)
            high = 0.0 if g == groups - 1 else pltpu.roll(cells(g + 1, at), LANES - 1, 1)
            before = jnp.where(lane == 0, low, pltpu.roll(q, 1, 1))
            after = jnp.where(lane == LANES - 1, high, pltpu.roll(q, LANES - 1, 1))
            across = (deep, near) if side in (WEST, SOUTH) else (near, deep)
            (west, east), (south, north) = (
                (across, (before, after)) if side in (WEST, EAST) else ((before, after), across)
            )
            other = cells(g, (1 - level) * bins + bin_at)
            rise = w - dust_step * settle_ref[bin_at : bin_at + ROWS, :]
            up = jnp.maximum(rise, 0.0)
            down = up - rise
            new = (
                (1.0 - 6.0 * mix - jnp.abs(u) - jnp.abs(v) - up - down) * q
                + (mix + jnp.maximum(u, 0.0)) * west
                + (mix + jnp.maximum(-u, 0.0)) * east
                + (mix + jnp.maximum(v, 0.0)) * south
                + (mix + jnp.maximum(-v, 0.0)) * north
                + (mix + (down if level == 0 else up)) * other
            )
            if level == 0:
                new = new + dust_step * wind_row(PLANES - 1) * share_ref[bin_at : bin_at + ROWS, :]
            out[g, at : at + ROWS, :] = jnp.where(wind_row(FLAG) > 0.0, new, 0.0)


def send_seen_kernel(
    owner_ref, rings_ref, wind_ref, settle_ref, share_ref, e_ref, w_ref, n_ref, s_ref, fw_ref, fe_ref, fs_ref, fn_ref,
    send_ref, corner_ref, ext, both, lw_ref, le_ref, ls_ref, ln_ref, sems, *, tiles_x, tiles_y
):
    rows = rings_ref.shape[1] // 2
    wide = tiles_y + 2
    each = 2 * rows + ROWS
    messages = (fw_ref, fe_ref, fs_ref, fn_ref)
    later = (lw_ref, le_ref, ls_ref, ln_ref)

    def place(t):
        return place_of(t, tiles_y)

    fill_halo(
        ext, [lambda g, m=m: m[g * each : g * each + rows, :] for m in messages], tiles_x, tiles_y
    )
    fill_tiles(ext, lambda t: rings_ref[t, :rows, :], tiles_x, tiles_y)

    def before(t, carry):
        both[t, :rows, :] = seen_by(ext, place(t), wide)
        return carry

    lax.fori_loop(0, tiles_x * tiles_y, before, 0)

    def advance(i, carry):
        for t in (2 * i, 2 * i + 1):
            chunks = advance_ring(t, owner_ref, rings_ref, wind_ref, settle_ref, share_ref, both[t, :rows, :])
            for n, chunk in enumerate(chunks):
                ext[place(t), n * ROWS : (n + 1) * ROWS, :] = chunk
        return carry

    lax.fori_loop(0, tiles_x * tiles_y // 2, advance, 0)

    for side, message, ours, out in zip(
        (WEST, EAST, SOUTH, NORTH), messages, (w_ref, e_ref, s_ref, n_ref), later
    ):
        advance_strip(side, message, ours, settle_ref, share_ref, out, rows)
    fill_halo(ext, [lambda g, m=m: m[g] for m in later], tiles_x, tiles_y)

    def copy(t):
        return pltpu.make_async_copy(both.at[t], send_ref.at[owner_ref[t]], sems.at[t])

    def sent_now(t):
        x, y = t // tiles_y, t % tiles_y
        at_corner = ((x == 0) | (x == tiles_x - 1)) & ((y == 0) | (y == tiles_y - 1))
        return (owner_ref[t] >= 0) & jnp.logical_not(at_corner)

    def after(t, carry):
        effect = ring_effect(t, wind_ref, settle_ref, both[t, :rows, :], seen_by(ext, place(t), wide))
        for depth, chunks in enumerate(effect):
            for n, chunk in enumerate(chunks):
                both[t, depth * rows + n * ROWS : depth * rows + (n + 1) * ROWS, :] = chunk

        @pl.when(sent_now(t))
        def _():
            copy(t).start()

        return carry

    lax.fori_loop(0, tiles_x * tiles_y, after, 0)
    for n, (_, _, t) in enumerate(corner_tiles(tiles_x, tiles_y)):
        corner_ref[n] = both[t]

    def wait(t, carry):
        @pl.when(sent_now(t))
        def _():
            copy(t).wait()

        return carry

    lax.fori_loop(0, tiles_x * tiles_y, wait, 0)


def corner_tiles(tiles_x, tiles_y):
    return [
        (side_x, side_y, x * tiles_y + y)
        for side_x, x in ((WEST, 0), (EAST, tiles_x - 1))
        for side_y, y in ((SOUTH, 0), (NORTH, tiles_y - 1))
    ]


def send_corners_kernel(
    owner_ref, _, effect_ref, wind_ref, fw_ref, fe_ref, fs_ref, fn_ref, cw_ref, ce_ref, send_ref, sums, sems,
    *, tiles_x, tiles_y
):
    rows = cw_ref.shape[0] // 2
    each = 2 * rows + ROWS
    bins = rows // TZ
    mix = dust_step * diffusion
    _, lane = iotas()
    group, within = lane // TILE, lane % TILE
    on_x = (group == WEST) | (group == EAST)
    low_side = (group == WEST) | (group == SOUTH)
    first, last = within == 0, within == TILE - 1
    corner = corner_index(0)
    tiles = corner_tiles(tiles_x, tiles_y)

    def copy(n, t):
        return pltpu.make_async_copy(sums.at[n], send_ref.at[owner_ref[t]], sems.at[n])

    for n, (side_x, side_y, t) in enumerate(tiles):
        strip_x = fw_ref if side_x == WEST else fe_ref
        strip_y = fs_ref if side_y == SOUTH else fn_ref
        cells_ref, cell_lane = (cw_ref, LANES - 1) if side_x == WEST else (ce_ref, 0)
        cells_at = 0 if side_y == SOUTH else rows
        low_x, low_y = side_x == WEST, side_y == SOUTH
        end_x = 0 if low_y else strip_x.shape[0] - each
        end_y = 0 if low_x else strip_y.shape[0] - each
        to_x = side_x * TILE + (0 if low_y else TILE - 1)
        to_y = side_y * TILE + (0 if low_x else TILE - 1)

        def from_end(strip, at, c, level, low):
            def row(p):
                value = strip[at + 2 * rows + p : at + 2 * rows + p + 1, :]
                return lane_gather(spread_rows(value), jnp.full((ROWS, LANES), 0 if low else LANES - 1, jnp.int32))

            along = dust_step * row(c * TZ + level)
            return jnp.where(row(FLAG) > 0.0, mix + jnp.maximum(along if low else -along, 0.0), 0.0)

        for at in range(0, rows, ROWS):
            level = at // bins
            if at % bins == 0:
                u, v = (
                    dust_step * spread_rows(wind_ref[t, c * TZ + level : c * TZ + level + 1, :]) for c in range(2)
                )
                across, along = jnp.where(on_x, u, v), jnp.where(on_x, v, u)
                from_out = mix + jnp.maximum(jnp.where(low_side, across, -across), 0.0)
                from_corner = jnp.where(
                    first, mix + jnp.maximum(along, 0.0), jnp.where(last, mix + jnp.maximum(-along, 0.0), 0.0)
                )
                by_x = from_end(strip_x, end_x, 1, level, low_y)
                by_y = from_end(strip_y, end_y, 0, level, low_x)
            cells = lane_gather(
                cells_ref[cells_at + at : cells_at + at + ROWS, :], jnp.full((ROWS, LANES), cell_lane, jnp.int32)
            )
            more = jnp.where(lane == to_x, by_x * cells, jnp.where(lane == to_y, by_y * cells, 0.0))
            sums[n, at : at + ROWS, :] = (
                effect_ref[n, at : at + ROWS, :] + from_out * more + from_corner * lane_gather(more, corner)
            )
        sums[n, rows:, :] = effect_ref[n, rows:, :]

        @pl.when(owner_ref[t] >= 0)
        def _():
            copy(n, t).start()

    for n, (_, _, t) in enumerate(tiles):

        @pl.when(owner_ref[t] >= 0)
        def _():
            copy(n, t).wait()


def shifted(value, axis, steps):
    count = lax.axis_size(axis)
    return lax.ppermute(value, axis, [(source, (source + steps) % count) for source in range(count)])


def relay_rows(rows):
    return lax.all_to_all(rows, AXES, split_axis=0, concat_axis=0, tiled=True)


def exchange_borders(borders):
    east, west, north, south = borders
    return shifted(east, "gx", 1), shifted(west, "gx", -1), shifted(north, "gy", 1), shifted(south, "gy", -1)


def ring_call(kernel, tiles_x, tiles_y, rows, outs, scratch, name, hbm_in=0, hbm_out=0, aliases={}):
    smem = pl.BlockSpec(memory_space=pltpu.SMEM)
    vmem = pl.BlockSpec(memory_space=pltpu.VMEM)
    hbm = pl.BlockSpec(memory_space=pltpu.HBM)
    size = tiles_x * tiles_y * rows * LANES

    def call(owner_of_tile, *inputs):
        return pl.pallas_call(
            functools.partial(kernel, tiles_x=tiles_x, tiles_y=tiles_y),
            in_specs=[smem] + [hbm] * hbm_in + [vmem] * (len(inputs) - hbm_in),
            out_specs=[hbm] * hbm_out + [vmem] * (len(outs) - hbm_out),
            out_shape=outs,
            scratch_shapes=scratch,
            input_output_aliases=aliases,
            compiler_params=pltpu.CompilerParams(vmem_limit_bytes=32 << 20),
            cost_estimate=pl.CostEstimate(flops=16 * size, bytes_accessed=16 * size, transcendentals=0),
            name=name,
        )(owner_of_tile, *inputs)

    return call


def relay_strips(owner_of_tile, received, wind_send, wind_ring, settle_speed, bin_share, tiles_x, tiles_y):
    owners, both_rows, _ = received.shape
    rows = both_rows // 2
    per_home = tiles_x * tiles_y
    each = both_rows + ROWS
    ext = pltpu.VMEM(((tiles_x + 2) * (tiles_y + 2), rows, LANES), jnp.float32)
    all_rings = pltpu.VMEM((per_home, both_rows, LANES), jnp.float32)
    each_sem = pltpu.SemaphoreType.DMA((per_home,))
    settle_rows = jnp.broadcast_to(settle_speed[:, None], settle_speed.shape + (LANES,))
    share_rows = jnp.broadcast_to(bin_share[:, None], bin_share.shape + (LANES,))

    def call(kernel, outs, scratch, name, *inputs, **places):
        return ring_call(kernel, tiles_x, tiles_y, rows, outs, scratch, name, **places)(owner_of_tile, *inputs)

    along_x, along_y = tiles_y // 4, tiles_x // 4
    east, west, north, south = call(
        pack_borders_kernel,
        [f32(along_x * each, LANES)] * 2 + [f32(along_y * each, LANES)] * 2,
        [all_rings, each_sem],
        "pack_borders",
        in_hbm(received),
        wind_ring,
        hbm_in=1,
    )
    from_west, from_east, from_south, from_north = exchange_borders((east, west, north, south))
    wind_send, from_west, from_east, from_south, from_north = lax.optimization_barrier(
        (wind_send, from_west, from_east, from_south, from_north)
    )
    wind_recv = relay_rows(wind_send)
    top = (along_y - 1) * each
    across_low = jnp.concatenate([from_south[:rows], from_north[:rows]])
    across_high = jnp.concatenate([from_south[top : top + rows], from_north[top : top + rows]])
    corner_west, corner_east = shifted(across_high, "gx", 1), shifted(across_low, "gx", -1)
    (rings,) = call(gather_rings_kernel, [f32(per_home, both_rows, LANES)], [], "gather_rings", received)
    send_buffer = pltpu.HBM((owners, both_rows, LANES), jnp.float32)
    messages = (from_west, from_east, from_south, from_north)
    seen_send, corners = call(
        send_seen_kernel,
        [send_buffer, f32(4, both_rows, LANES)],
        [ext, all_rings]
        + [pltpu.VMEM((along_x, rows, LANES), jnp.float32)] * 2
        + [pltpu.VMEM((along_y, rows, LANES), jnp.float32)] * 2
        + [each_sem],
        "send_seen",
        rings, wind_ring, settle_rows, share_rows, east, west, north, south, *messages,
        hbm_out=1,
    )
    (seen_send,) = call(
        send_corners_kernel,
        [send_buffer],
        [pltpu.VMEM((4, both_rows, LANES), jnp.float32), pltpu.SemaphoreType.DMA((4,))],
        "send_corners",
        seen_send, corners, wind_ring, *messages, corner_west, corner_east,
        hbm_in=1,
        hbm_out=1,
        aliases={1: 0},
    )
    return wind_recv, relay_rows(seen_send)


def dust_kernel(home_ref, share_ref, settle_ref, dust_ref, shift_ref, wind_ref, out_ref, coef, *work, block, bins):
    lanes = len(work) // 2
    step = pl.program_id(0)
    _, lane = iotas()
    within = lane % TILE
    low_lanes, high_lanes = lane < TILE, lane >= LANES - TILE
    mix = dust_step * diffusion
    chunks = bins // ROWS
    settle = [dust_step * settle_ref[h * ROWS : (h + 1) * ROWS, :] for h in range(chunks)]
    share = [share_ref[h * ROWS : (h + 1) * ROWS, :] for h in range(chunks)]
    nothing = jnp.zeros((ROWS, LANES), jnp.float32)

    def prepare(k, j):
        held = work[2 * k]
        home = home_ref[step * block + j]
        plane = [wind_ref[home, p * ROWS : (p + 1) * ROWS, :] * dust_step for p in range(PLANES)]
        for level in range(TZ):
            u, v = plane[level], plane[TZ + level]
            coef[k, 0, level] = mix + jnp.maximum(u, 0.0)
            coef[k, 1, level] = mix + jnp.maximum(-u, 0.0)
            coef[k, 2, level] = jnp.where(within == 0, 0.0, mix + jnp.maximum(v, 0.0))
            coef[k, 3, level] = jnp.where(within == TILE - 1, 0.0, mix + jnp.maximum(-v, 0.0))
            coef[k, 4, level] = 1.0 - 6.0 * mix - jnp.abs(u) - jnp.abs(v)
            coef[k, 5, level] = plane[2 * TZ + level]
        coef[k, 6, 0] = plane[PLANES - 1]
        for r in range(ROWS):
            for level in range(TZ):
                at = (r * TZ + level) * bins
                held[at : at + bins, :] = dust_ref[j, pl.ds(r * TZ + level, bins, stride=ROWS * TZ), :]

    def shift(k):
        held, shifts = work[2 * k], work[2 * k + 1]
        shifts[...] = jnp.dot(
            jnp.concatenate(halves_of(held[...]), axis=1), shift_ref[...], preferred_element_type=jnp.float32
        )

    def update(k, j, substep):
        held, shifts = work[2 * k], work[2 * k + 1]
        for r in range(ROWS):
            for h in range(chunks):
                cells = [held[(r * TZ + level) * bins + h * ROWS :][:ROWS] for level in range(TZ)]
                for level in range(TZ):
                    at = (r * TZ + level) * bins + h * ROWS

                    def moved(which, rows_up=0):
                        first = at + rows_up * TZ * bins
                        return shifts[first : first + ROWS, which * LANES : (which + 1) * LANES]

                    def by(which):
                        return spread_rows(coef[k, which, level, r : r + 1, :])

                    before = nothing if r == 0 else moved(2, -1)
                    after = nothing if r == ROWS - 1 else moved(3, 1)
                    west = jnp.where(low_lanes, before, moved(2))
                    east = jnp.where(high_lanes, after, moved(3))
                    rise = by(5) - settle[h]
                    up = jnp.maximum(rise, 0.0)
                    mixed = mix + (up - rise if level == 0 else up)
                    value = (
                        (by(4) - jnp.abs(rise)) * cells[level]
                        + by(0) * west
                        + by(1) * east
                        + by(2) * moved(0)
                        + by(3) * moved(1)
                        + mixed * cells[1 - level]
                    )
                    if level == 0:
                        value = value + spread_rows(coef[k, 6, 0, r : r + 1, :]) * share[h]
                    if substep == 0:
                        held[at : at + ROWS, :] = value
                    else:
                        first = h * ROWS * ROWS * TZ + r * TZ + level
                        out_ref[j, pl.ds(first, ROWS, stride=ROWS * TZ), :] = value

    def some(i, carry):
        for k in range(lanes):
            prepare(k, i * lanes + k)
        for substep in range(2):
            for k in range(lanes):
                shift(k)
            for k in range(lanes):
                update(k, i * lanes + k, substep)
        return carry

    lax.fori_loop(0, block // lanes, some, 0)


def dust_inner(home_of_slot, dust, wind_recv, settle_speed, bin_share):
    slots, cells = dust.shape[:2]
    bins = settle_speed.shape[0]
    block = 8 if slots % 8 == 0 else 4
    lanes = 2
    smem = pl.BlockSpec(memory_space=pltpu.SMEM)
    vmem = pl.BlockSpec(memory_space=pltpu.VMEM)
    tile = pl.BlockSpec((block, cells, LANES), lambda i: (i, 0, 0))
    settle = jnp.broadcast_to(settle_speed[:, None], (bins, LANES))
    share = jnp.broadcast_to(bin_share[:, None], (bins, LANES))
    return pl.pallas_call(
        functools.partial(dust_kernel, block=block, bins=bins),
        grid=(slots // block,),
        in_specs=[smem, vmem, vmem, tile, vmem, vmem],
        out_specs=tile,
        out_shape=pltpu.HBM(dust.shape, jnp.float32),
        scratch_shapes=[pltpu.VMEM((lanes, PLANES, TZ, ROWS, LANES), jnp.float32)]
        + [pltpu.VMEM((cells, LANES), jnp.float32), pltpu.VMEM((cells, 4 * LANES), jnp.float32)] * lanes,
        compiler_params=pltpu.CompilerParams(vmem_limit_bytes=24 << 20),
        cost_estimate=pl.CostEstimate(flops=120 * dust.size, bytes_accessed=dust.size * 12, transcendentals=0),
        name="dust_inner",
    )(home_of_slot, share, settle, in_hbm(dust), jnp.asarray(shift_matrix()), wind_recv)


def dust_outer_kernel(
    home_ref, inner_hbm, matrix_ref, effect_hbm, out_hbm, effect, dust, added, effect_sems, load_sems, sems, *, block, bins
):
    slots = dust.shape[0]
    rows = TZ * bins

    def arrive(s):
        return pltpu.make_async_copy(effect_hbm.at[home_ref[s]], effect.at[s], effect_sems.at[s])

    def load(i):
        some = pl.ds(i * block, block)
        return pltpu.make_async_copy(inner_hbm.at[some], dust.at[some], load_sems.at[i])

    def store(i):
        some = pl.ds(i * block, block)
        return pltpu.make_async_copy(dust.at[some], out_hbm.at[some], sems.at[i])

    def start(i, carry):
        for j in range(block):
            arrive(i * block + j).start()
        load(i).start()
        return carry

    count = slots // block
    lax.fori_loop(0, count, start, 0)

    def wait_for(i):
        for j in range(block):
            arrive(i * block + j).wait()

    def expand(i):
        rings = jnp.concatenate(
            [
                jnp.concatenate([effect[i * block + j, depth * rows : (depth + 1) * rows, :] for depth in range(2)], axis=1)
                for j in range(block)
            ],
            axis=0,
        )
        return jnp.dot(
            jnp.concatenate(halves_of(rings), axis=1), matrix_ref[...], preferred_element_type=jnp.float32
        )

    wait_for(0)
    added[0] = expand(0)

    def one(i, carry):
        later = jnp.minimum(i + 1, count - 1)

        @pl.when(i + 1 < count)
        def _():
            wait_for(later)

        load(i).wait()
        now = lax.rem(i, 2)
        added[1 - now] = expand(later)
        for j in range(block):
            for r in range(ROWS):
                for level in range(TZ):
                    at = pl.ds(r * TZ + level, bins, stride=ROWS * TZ)
                    first = j * rows + level * bins
                    dust[i * block + j, at, :] += added[now, first : first + bins, r * LANES : (r + 1) * LANES]
        store(i).start()
        return carry

    lax.fori_loop(0, count, one, 0)
    for i in range(count):
        store(i).wait()


def dust_outer(home_of_slot, inner, effect, bins):
    slots = inner.shape[0]
    block = 8 if slots % 8 == 0 else 4
    hbm = pl.BlockSpec(memory_space=pltpu.HBM)
    vmem = pl.BlockSpec(memory_space=pltpu.VMEM)
    return pl.pallas_call(
        functools.partial(dust_outer_kernel, block=block, bins=bins),
        in_specs=[pl.BlockSpec(memory_space=pltpu.SMEM), hbm, vmem, hbm],
        out_specs=hbm,
        out_shape=pltpu.HBM(inner.shape, jnp.float32),
        scratch_shapes=[
            pltpu.VMEM((slots,) + effect.shape[1:], jnp.float32),
            pltpu.VMEM(inner.shape, jnp.float32),
            pltpu.VMEM((2, block * bins * TZ, TILE * TILE), jnp.float32),
            pltpu.SemaphoreType.DMA((slots,)),
            pltpu.SemaphoreType.DMA((slots // block,)),
            pltpu.SemaphoreType.DMA((slots // block,)),
        ],
        compiler_params=pltpu.CompilerParams(vmem_limit_bytes=24 << 20),
        cost_estimate=pl.CostEstimate(flops=2 * inner.size, bytes_accessed=inner.size * 8, transcendentals=0),
        name="dust_outer",
    )(home_of_slot, in_hbm(inner), jnp.asarray(spread_matrix()), in_hbm(effect))


def per_device(velocity, threshold, dust_mass, settle_speed, bin_share, active_tiles, tile_owner):
    owners = lax.axis_size(AXES)
    grid_cols = lax.axis_size("gy")
    self_index = lax.axis_index(AXES)
    slots, bins = dust_mass.shape[:2]
    tiles_x = velocity.shape[2] // TILE
    tiles_y = velocity.shape[3] // TILE
    per_home = tiles_x * tiles_y
    tiles_across = tiles_y * grid_cols

    tile_x = active_tiles // tiles_across
    tile_y = active_tiles % tiles_across
    home_dev = tile_x // tiles_x * grid_cols + tile_y // tiles_y
    local_tile = tile_x % tiles_x * tiles_y + tile_y % tiles_y
    own_slot = tile_owner - self_index * slots
    mine = jnp.where(home_dev == self_index, local_tile, -1)
    slot_ids = jnp.arange(slots, dtype=jnp.int32)
    home_of_slot = jnp.sum(jnp.where(own_slot[None, :] == slot_ids[:, None], home_dev[None, :], 0), axis=1)
    tile_ids = jnp.arange(per_home, dtype=jnp.int32)
    owner_of_tile = jnp.max(
        jnp.where(mine[None, :] == tile_ids[:, None], (tile_owner // slots)[None, :], -1), axis=1
    )

    dust = dust_mass.reshape(slots, bins, TZ, ROWS, LANES).transpose(0, 1, 3, 2, 4)
    dust = dust.reshape(slots, bins * ROWS * TZ, LANES)

    xlo, xhi, ylo, yhi = exchange_borders(wind_faces(velocity))

    strips_send = dust_strips(home_of_slot, dust, bins, owners)
    strips_send, xlo, xhi, ylo, yhi = lax.optimization_barrier((strips_send, xlo, xhi, ylo, yhi))
    strips = relay_rows(strips_send)
    new_velocity, wind_send, wind_ring = wind_step(
        owner_of_tile, velocity, xlo, xhi, ylo, yhi, threshold, owners
    )
    strips, wind_send, wind_ring = lax.optimization_barrier((strips, wind_send, wind_ring))
    wind_recv, effect = relay_strips(
        owner_of_tile, strips, wind_send, wind_ring, settle_speed, bin_share, tiles_x, tiles_y
    )
    inner = dust_inner(home_of_slot, dust, wind_recv, settle_speed, bin_share)
    out = dust_outer(home_of_slot, inner, effect, bins)
    out = out.reshape(slots, bins, ROWS, TZ, LANES).transpose(0, 1, 3, 2, 4).reshape(dust_mass.shape)
    return new_velocity, out


def solution(mesh):
    in_specs = (
        P(None, None, "gx", "gy"),
        P("gx", "gy"),
        P(AXES, None, None, None),
        P(),
        P(),
        P(),
        P(),
    )
    out_specs = (P(None, None, "gx", "gy"), P(AXES, None, None, None))
    return jax.shard_map(
        per_device, mesh=mesh, in_specs=in_specs, out_specs=out_specs, check_vma=False
    )
```
